128 devices in a mesh: gx: 4 (over x_lo, core), gz: 32 (over y, z, x_hi).
Axes of the slice: x: 4 (x_hi: 2, x_lo: 2; x = x_hi * 2 + x_lo), y: 4, z: 4, core: 2. Of those that a mesh axis runs over, the one named last changes fastest.
Arguments:
- fields: float32 [5, 64, 512, 256], P(None, 'gx', 'gz'), may hold values from -8 to 8
- courant: float32 [256], replicated, may hold values from 0.1 to 0.6
- shear_rate: float32 [256], replicated, may hold values from -1 to 1
- gradient: float32 [256], replicated, may hold values from -1 to 1
- earlier: float32 [14, 16, 8192], P(None, 'gx', 'gz'), may hold values from -8 to 8
- basis_modes: float32 [16, 128, 64, 256], P('gx', None, 'gz'), may hold values from -4 to 4
- core_matrix: float32 [256, 256], replicated, may hold values from -1 to 60, as said below
Outputs:
- new_fields: float32 [5, 64, 512, 256], P(None, 'gx', 'gz')
- new_basis: float32 [16, 128, 64, 256], P('gx', None, 'gz')
- new_core: float32 [256, 256], replicated
The draws below stay inside these ranges and needn't reach their ends.
Inputs may be any that keep to these rules, and one draw needn't show every extreme that they name: `core_matrix`: symmetric, every eigenvalue 2 or more.
All inputs are finite; a program needn't handle non-finite values.
Results may differ from the reference program's by a relative error of at most 0.0001.
Values sent between devices are 32-bit elements; how exact they have to be, the bound alone decides.
A program may use at most 192 MiB of HBM per device.

```python
import jax
import jax.numpy as jnp
from jax import lax

NY = 256
K = 256
M = 16
SIGN_STEPS = 10
POLAR_STEPS = 3
NX = 64
NZ = 512
DX = 16
DZ = 128
DY = 64
ROWS = 131072


def shared_parts(key):
    basis_key, coef_key, column_key = jax.random.split(key, 3)
    column_scale = jax.random.uniform(column_key, (K,), jnp.float32, 0.7, 1.3)
    raw_basis = jax.random.normal(basis_key, (DX, DZ, DY, K), jnp.float32) * column_scale
    basis_whole = jnp.clip(raw_basis, -4.0, 4.0)
    coefs = jax.random.normal(coef_key, (K, M - 1), jnp.float32) / jnp.sqrt(jnp.float32(K))
    return (basis_whole, coefs)


def ramp_along(count, low, high):
    place = jnp.arange(count, dtype=jnp.float32) / jnp.float32(max(count - 1, 1))
    return low + (high - low) * place


def draw_basis_modes(key, part):
    basis_whole, coefs = shared_parts(key)
    return basis_whole


def draw_earlier(key, part):
    basis_whole, coefs = shared_parts(key)
    key = jax.random.fold_in(key, 11)
    noise_key = jax.random.fold_in(key, 0)
    captured = jnp.einsum('xzyk,km->mxzy', basis_whole, coefs[:, :M - 2], precision=lax.Precision.HIGHEST)
    noise = jax.random.normal(noise_key, (M - 2, DX, DZ, DY), jnp.float32)
    rising = ramp_along(DX, 0.5, 1.6)
    noise = noise * rising[None, :, None, None]
    values = jnp.clip(captured + 0.3 * noise, -8.0, 8.0)
    return values.reshape(M - 2, DX, DZ * DY)


def draw_fields(key, part):
    basis_whole, coefs = shared_parts(key)
    key = jax.random.fold_in(key, 13)
    coarse_part = jnp.einsum('xzyk,k->xzy', basis_whole, coefs[:, M - 2], precision=lax.Precision.HIGHEST)
    fine_part = jnp.repeat(jnp.repeat(jnp.repeat(coarse_part, 4, axis=0), 4, axis=1), 4, axis=2)
    noise = jax.random.normal(key, (5, NX, NZ, NY), jnp.float32)
    rising = ramp_along(NX, 0.5, 1.6)
    values = noise.at[0].set(fine_part + 0.7 * noise[0] * rising[:, None, None])
    return jnp.clip(values, -8.0, 8.0)


def draw_core_matrix(key, part):
    key = jax.random.fold_in(key, 17)
    diag_key, factor_key, place_key, strong_key = jax.random.split(key, 4)
    diagonal = jnp.exp(jax.random.uniform(diag_key, (K,), jnp.float32, jnp.log(2.0), jnp.log(8.0)))
    places = jax.random.permutation(place_key, K)[:2]
    strong = jax.random.uniform(strong_key, (2,), jnp.float32, 52.0, 56.0)
    diagonal = diagonal.at[places].set(strong)
    factor = jnp.clip(jax.random.normal(factor_key, (K, K), jnp.float32), -3.0, 3.0) / jnp.sqrt(jnp.float32(K))
    return jnp.diag(diagonal) + jnp.dot(factor, factor.T, precision=lax.Precision.HIGHEST)


def setup_inputs(seed: int = 0) -> dict:
    seeds = jax.random.split(jax.random.key(seed), 8)
    fields = draw_fields(jax.random.fold_in(seeds[7], 71), 0)
    courant = jnp.clip(jax.random.uniform(seeds[1], (NY,), jnp.float32, 0.1, 0.6), 0.1, 0.6)
    shear_rate = jnp.clip(jax.random.uniform(seeds[2], (NY,), jnp.float32, -1.0, 1.0), -1.0, 1.0)
    gradient = jnp.clip(jax.random.uniform(seeds[3], (NY,), jnp.float32, -1.0, 1.0), -1.0, 1.0)
    earlier = draw_earlier(jax.random.fold_in(seeds[7], 71), 0)
    basis_modes = draw_basis_modes(jax.random.fold_in(seeds[7], 71), 0)
    core_matrix = draw_core_matrix(jax.random.fold_in(seeds[7], 71), 0)
    return {"fields": fields, "courant": courant, "shear_rate": shear_rate, "gradient": gradient, "earlier": earlier, "basis_modes": basis_modes, "core_matrix": core_matrix}


press_coef = 0.25
compress_coef = 0.25
visc_coef = 0.05
heat_coef = 0.03
gram_eps = 1e-06

def advance(padded, courant, shear_rate, gradient):
    centre = padded[:, 1:-1, 1:-1, :]
    x_lower = padded[:, :-2, 1:-1, :]
    x_upper = padded[:, 2:, 1:-1, :]
    z_lower = padded[:, 1:-1, :-2, :]
    z_upper = padded[:, 1:-1, 2:, :]
    y_lower = jnp.pad(centre[..., :-1], ((0, 0), (0, 0), (0, 0), (1, 0)))
    y_upper = jnp.pad(centre[..., 1:], ((0, 0), (0, 0), (0, 0), (0, 1)))
    laplace = x_lower + x_upper + z_lower + z_upper + y_lower + y_upper - 6.0 * centre
    upwind = courant * (centre - x_lower)
    along_x = centre[0] - upwind[0] - shear_rate * centre[1] - press_coef * 0.5 * (x_upper[3] - x_lower[3]) + visc_coef * laplace[0]
    along_y = centre[1] - upwind[1] - press_coef * 0.5 * (y_upper[3] - y_lower[3]) + visc_coef * laplace[1]
    along_z = centre[2] - upwind[2] - press_coef * 0.5 * (z_upper[3] - z_lower[3]) + visc_coef * laplace[2]
    divergence = x_upper[0] - x_lower[0] + (y_upper[1] - y_lower[1]) + (z_upper[2] - z_lower[2])
    pressure = centre[3] - compress_coef * 0.5 * divergence + visc_coef * laplace[3]
    heat = centre[4] - upwind[4] - gradient * centre[1] + heat_coef * laplace[4]
    return jnp.stack([along_x, along_y, along_z, pressure, heat])

def coarsen(values):
    return values.reshape(values.shape[0] // 4, 4, values.shape[1] // 4, 4, values.shape[2] // 4, 4).mean(axis=(1, 3, 5))

def rotate(core_matrix, coeffs, factor):
    mode_count = core_matrix.shape[0]
    extra = coeffs.shape[0]
    extension = jnp.concatenate([coeffs.T, factor.T], axis=0)
    correlation = jnp.pad(core_matrix, ((0, extra), (0, extra))) + jnp.dot(extension, extension.T, precision=lax.Precision.HIGHEST)
    identity = jnp.eye(mode_count + extra, dtype=jnp.float32)
    shifted = correlation - identity
    start = shifted / jnp.sqrt(jnp.sum(shifted * shifted))

    def sign_step(iteration, matrix):
        cubed = jnp.dot(matrix, jnp.dot(matrix, matrix, precision=lax.Precision.HIGHEST), precision=lax.Precision.HIGHEST)
        return 1.5 * matrix - 0.5 * cubed
    sign_matrix = lax.fori_loop(0, SIGN_STEPS, sign_step, start)
    rotation = (0.5 * (identity + sign_matrix))[:, :mode_count]
    for _ in range(POLAR_STEPS):
        inner = jnp.dot(rotation.T, rotation, precision=lax.Precision.HIGHEST)
        rotation = 1.5 * rotation - 0.5 * jnp.dot(rotation, inner, precision=lax.Precision.HIGHEST)
    moved = jnp.dot(correlation, rotation, precision=lax.Precision.HIGHEST)
    new_core = jnp.dot(rotation.T, moved, precision=lax.Precision.HIGHEST)
    return (rotation, new_core)

def reference(fields, courant, shear_rate, gradient, earlier, basis_modes, core_matrix):
    halfway = advance(jnp.pad(fields, ((0, 0), (1, 1), (1, 1), (0, 0)), mode='wrap'), courant, shear_rate, gradient)
    finished = advance(jnp.pad(halfway, ((0, 0), (1, 1), (1, 1), (0, 0)), mode='wrap'), courant, shear_rate, gradient)
    buffered = earlier.reshape(M - 2, DX, DZ, DY)
    stacked = jnp.concatenate([buffered, coarsen(halfway[0])[None], coarsen(finished[0])[None]], axis=0)
    snapshots = stacked.reshape(M, ROWS)
    basis_rows = basis_modes.reshape(ROWS, K)
    c_one = jnp.dot(snapshots, basis_rows, precision=lax.Precision.HIGHEST) / ROWS
    p_one = snapshots - jnp.dot(c_one, basis_rows.T, precision=lax.Precision.HIGHEST)
    c_two = jnp.dot(p_one, basis_rows, precision=lax.Precision.HIGHEST) / ROWS
    residual = p_one - jnp.dot(c_two, basis_rows.T, precision=lax.Precision.HIGHEST)
    coeffs = c_one + c_two
    identity_m = jnp.eye(M, dtype=jnp.float32)
    gram_matrix = jnp.dot(residual, residual.T, precision=lax.Precision.HIGHEST) / ROWS + gram_eps * identity_m
    factor = jnp.linalg.cholesky(gram_matrix)
    inverse_factor = jax.scipy.linalg.solve_triangular(factor, identity_m, lower=True)
    q_rows = jnp.dot(inverse_factor, residual, precision=lax.Precision.HIGHEST)
    rotation, new_core = rotate(core_matrix, coeffs, factor)
    new_rows = jnp.dot(basis_rows, rotation[:K], precision=lax.Precision.HIGHEST)
    new_rows = new_rows + jnp.einsum('mr,mk->rk', q_rows, rotation[K:], precision=lax.Precision.HIGHEST)
    return (finished, new_rows.reshape(DX, DZ, DY, K), new_core)
```

```python
import jax
import jax.numpy as jnp
from jax import lax
from jax.experimental import pallas as pl
from jax.experimental.pallas import tpu as pltpu
from jax.sharding import PartitionSpec as P

F32, BF16 = jnp.float32, jnp.bfloat16
HIGH = lax.Precision.HIGHEST
SIGN_STEPS = 10
POLAR_STEPS = 3


press_coef = 0.25
compress_coef = 0.25
visc_coef = 0.05
heat_coef = 0.03
gram_eps = 1e-06


def extended(cells, sides, width):
    for axis, dim in sides:
        count = lax.axis_size(axis)
        head = lax.slice_in_dim(cells, 0, width, axis=dim)
        tail = lax.slice_in_dim(cells, cells.shape[dim] - width, cells.shape[dim], axis=dim)
        cells = jnp.concatenate(
            [
                lax.ppermute(tail, axis, [(i, (i + 1) % count) for i in range(count)]),
                cells,
                lax.ppermute(head, axis, [((i + 1) % count, i) for i in range(count)]),
            ],
            axis=dim,
        )
    return cells


def advance(padded, courant, shear_rate, gradient):
    centre = padded[:, 1:-1, 1:-1, :]
    x_lower = padded[:, :-2, 1:-1, :]
    x_upper = padded[:, 2:, 1:-1, :]
    z_lower = padded[:, 1:-1, :-2, :]
    z_upper = padded[:, 1:-1, 2:, :]
    y_lower = jnp.pad(centre[..., :-1], ((0, 0), (0, 0), (0, 0), (1, 0)))
    y_upper = jnp.pad(centre[..., 1:], ((0, 0), (0, 0), (0, 0), (0, 1)))
    laplace = x_lower + x_upper + z_lower + z_upper + y_lower + y_upper - 6.0 * centre
    upwind = courant * (centre - x_lower)
    along_x = (
        centre[0]
        - upwind[0]
        - shear_rate * centre[1]
        - press_coef * 0.5 * (x_upper[3] - x_lower[3])
        + visc_coef * laplace[0]
    )
    along_y = (
        centre[1]
        - upwind[1]
        - press_coef * 0.5 * (y_upper[3] - y_lower[3])
        + visc_coef * laplace[1]
    )
    along_z = (
        centre[2]
        - upwind[2]
        - press_coef * 0.5 * (z_upper[3] - z_lower[3])
        + visc_coef * laplace[2]
    )
    divergence = x_upper[0] - x_lower[0] + (y_upper[1] - y_lower[1]) + (z_upper[2] - z_lower[2])
    pressure = centre[3] - compress_coef * 0.5 * divergence + visc_coef * laplace[3]
    heat = centre[4] - upwind[4] - gradient * centre[1] + heat_coef * laplace[4]
    return jnp.stack([along_x, along_y, along_z, pressure, heat])


def advance_with_rim(fields, courant, shear_rate, gradient):
    padded = extended(fields, (("gx", 1), ("gz", 2)), 1)
    return advance(padded, courant, shear_rate, gradient)


def coarsen(values):
    return values.reshape(
        values.shape[0] // 4, 4, values.shape[1] // 4, 4, values.shape[2] // 4, 4
    ).mean(axis=(1, 3, 5))


def halves(values):
    head = values.astype(BF16)
    return head, (values - head.astype(F32)).astype(BF16)


def dot(left, right, over=((1,), (0,))):
    return lax.dot_general(left, right, (over, ((), ())), preferred_element_type=F32)


def dot_three(left, right, over=((1,), (0,))):
    (lh, ll), (rh, rl) = left, right
    return dot(lh, rh, over) + (dot(lh, rl, over) + dot(ll, rh, over))


def dot_high(left, right, over=((1,), (0,))):
    return lax.dot_general(
        left, right, (over, ((), ())), precision=HIGH, preferred_element_type=F32
    )


TN = ((0,), (0,))
NT = ((1,), (1,))


def tripled_left(pair):
    return jnp.concatenate([pair[0], pair[0], pair[1]], axis=0)


def tripled_right(pair):
    return jnp.concatenate([pair[0], pair[1], pair[0]], axis=0)


def eye(count):
    return (
        lax.broadcasted_iota(jnp.int32, (count, count), 0)
        == lax.broadcasted_iota(jnp.int32, (count, count), 1)
    ).astype(F32)


def row_places(z_lanes):
    places = []
    for zc in range(4):
        for x in range(4):
            for y in range(2):
                places.append((zc, x, y))
    return places


def take_basis(view_ref, rows_ref):
    for place, (zc, x, y) in enumerate(row_places(0)):
        for half in range(2):
            rows_ref[pl.ds(place * 32, 32), pl.ds(half * 128, 128)] = view_ref[
                pl.ds(512 * x + 4 * zc + 2 * half + y, 32, stride=16), :
            ]


def give_basis(rows, view_ref, first):
    for step in range(8):
        zc, x, y = row_places(0)[first + step]
        for half in range(2):
            view_ref[pl.ds(512 * x + 4 * zc + 2 * half + y, 32, stride=16), :] = rows[
                step * 32 : step * 32 + 32, half * 128 : half * 128 + 128
            ]


def cholesky(gram):
    count = gram.shape[0]
    row_index = lax.broadcasted_iota(jnp.int32, (count, count), 0)
    col_index = lax.broadcasted_iota(jnp.int32, (count, count), 1)
    left = gram
    right = eye(count)
    for j in range(count):
        pivot = left[j : j + 1, j : j + 1]
        scale = lax.rsqrt(pivot)
        scale = scale * (1.5 - 0.5 * pivot * scale * scale)
        column = left[:, j : j + 1] * scale
        row_l = left[j : j + 1, :] * scale
        row_r = right[j : j + 1, :] * scale
        below = row_index > j
        here = row_index == j
        left = jnp.where(below, left - column * row_l, jnp.where(here, row_l, left))
        right = jnp.where(below, right - column * row_r, jnp.where(here, row_r, right))
    return jnp.where(row_index <= col_index, left, 0.0), right


def product(left_v, left_d, right_v, right_d):
    modes = left_v.shape[1]
    lv = halves(left_v)
    rv = halves(right_v)
    ra = (rv[0][:modes], rv[1][:modes])
    lb = (lv[0][modes:], lv[1][modes:])
    rb = (rv[0][modes:], rv[1][modes:])
    main = dot_three(lv, ra)
    right48 = tripled_right(rb)
    top = dot(tripled_left(lb), right48, TN)
    low = dot(tripled_left(halves(left_d)), right48, TN)
    out_d = dot_three(lb, rb, NT) + dot_high(left_d, right_d)
    return main + jnp.concatenate([top, low], axis=0), out_d


def tail_kernel(core_ref, coeffs_ref, gram_ref, resid_ref, basis_hbm, out_basis, out_core,
                v_ref, d_ref, basis_view, basis_rows, sem):
    modes = core_ref.shape[0]
    fetch = pltpu.make_async_copy(basis_hbm, basis_view, sem)
    fetch.start()
    factor_t, inverse = cholesky(gram_ref[...] + gram_eps * eye(16))
    coeffs = coeffs_ref[...]
    unit = eye(modes)
    unit_d = eye(16)
    corr_a = core_ref[...] + dot_high(coeffs, coeffs, TN)
    corr_b = dot_high(factor_t, coeffs)
    corr_d = dot_high(factor_t, factor_t, NT)
    shift_a = corr_a - unit
    shift_d = corr_d - unit_d
    total = (
        jnp.sum(shift_a * shift_a, keepdims=True)
        + 2.0 * jnp.sum(corr_b * corr_b, keepdims=True)
        + jnp.sum(shift_d * shift_d, keepdims=True)
    )
    scale = 1.0 / jnp.sqrt(total)
    v_ref[:modes] = shift_a * scale
    v_ref[modes:] = corr_b * scale
    d_ref[...] = shift_d * scale
    unit_v = jnp.concatenate([unit, jnp.zeros((16, modes), F32)], axis=0)

    def sign_step(step, carry):
        v = v_ref[...]
        d = d_ref[...]
        square_v, square_d = product(v, d, v, d)
        next_v, next_d = product(
            v, d, 1.5 * unit_v - 0.5 * square_v, 1.5 * unit_d - 0.5 * square_d
        )
        v_ref[...] = next_v
        d_ref[...] = next_d
        return carry

    lax.fori_loop(0, SIGN_STEPS, sign_step, 0)

    fetch.wait()
    take_basis(basis_view, basis_rows)

    rot = 0.5 * (unit_v + v_ref[...])
    for _ in range(POLAR_STEPS):
        rh, rl = halves(rot)
        inner = dot_three((rh, rl), (rh, rl), TN)
        rot = 1.5 * rot - 0.5 * dot_three((rh, rl), halves(inner))
    rp = halves(rot)
    corr_v = jnp.concatenate([corr_a, corr_b], axis=0)
    moved = dot_three(halves(corr_v), (rp[0][:modes], rp[1][:modes]))
    rb48 = tripled_right((rp[0][modes:], rp[1][modes:]))
    moved = moved + jnp.concatenate(
        [
            dot(tripled_left(halves(corr_b)), rb48, TN),
            dot(tripled_left(halves(corr_d)), rb48, TN),
        ],
        axis=0,
    )
    out_core[...] = dot_three(rp, halves(moved), TN)

    mix = dot_high(inverse, rot[modes:], TN)
    mix48 = tripled_right(halves(mix))
    ra = (rp[0][:modes], rp[1][:modes])
    for part in range(4):
        rows = basis_rows[pl.ds(part * 256, 256), :]
        left = tripled_left(halves(resid_ref[:, part * 256 : part * 256 + 256]))
        give_basis(dot_three(halves(rows), ra) + dot(left, mix48, TN), out_basis, part * 8)


def tail(core, coeffs, gram, resid, basis_view):
    vmem = pl.BlockSpec(memory_space=pltpu.VMEM)
    return pl.pallas_call(
        tail_kernel,
        out_shape=(
            jax.ShapeDtypeStruct((2048, 128), F32),
            jax.ShapeDtypeStruct((256, 256), F32),
        ),
        in_specs=[vmem, vmem, vmem, vmem, pl.BlockSpec(memory_space=pl.ANY)],
        out_specs=(vmem, vmem),
        scratch_shapes=[
            pltpu.VMEM((272, 256), F32),
            pltpu.VMEM((16, 16), F32),
            pltpu.VMEM((2048, 128), F32),
            pltpu.VMEM((1024, 256), F32),
            pltpu.SemaphoreType.DMA,
        ],
        compiler_params=pltpu.CompilerParams(vmem_limit_bytes=32 * 1024 * 1024),
    )(core, coeffs, gram, resid, basis_view)


def view_of(basis):
    return basis.reshape(4, 128, 2, 2, 128).transpose(0, 1, 3, 2, 4).reshape(2048, 128)


def basis_of(view):
    return view.reshape(4, 128, 2, 2, 128).transpose(0, 1, 3, 2, 4).reshape(4, 128, 2, 256)


def on_device(fields, courant, shear_rate, gradient, earlier, basis_modes, core_matrix):
    basis_rows = basis_modes.reshape(-1, basis_modes.shape[-1])
    rows_total = jnp.float32(basis_rows.shape[0] * lax.axis_size("gx") * lax.axis_size("gz"))
    width_z = fields.shape[2] // 4
    height = fields.shape[3] // 4
    buffered = earlier.reshape(earlier.shape[0], earlier.shape[1], width_z, height)
    halfway = advance_with_rim(fields, courant, shear_rate, gradient)
    snap_first = coarsen(halfway[0])[None]
    finished = advance_with_rim(halfway, courant, shear_rate, gradient)
    snap_second = coarsen(finished[0])[None]
    snapshots = lax.all_to_all(
        jnp.concatenate([buffered, snap_first, snap_second], axis=0),
        "gz",
        split_axis=3,
        concat_axis=2,
        tiled=True,
    )
    snapshots = snapshots.reshape(snapshots.shape[0], -1)
    local_proj = jnp.dot(snapshots, basis_rows, precision=lax.Precision.HIGHEST)
    c_one = lax.psum(local_proj, ("gx", "gz")) / rows_total
    p_one = snapshots - jnp.dot(c_one, basis_rows.T, precision=lax.Precision.HIGHEST)
    local_cross = jnp.dot(p_one, basis_rows, precision=lax.Precision.HIGHEST)
    c_two = lax.psum(local_cross, ("gx", "gz")) / rows_total
    residual = p_one - jnp.dot(c_two, basis_rows.T, precision=lax.Precision.HIGHEST)
    local_gram = jnp.dot(residual, residual.T, precision=lax.Precision.HIGHEST)
    gram_total = lax.psum(local_gram, ("gx", "gz")) / rows_total
    coeffs = c_one + c_two
    ordered = residual.reshape(16, 4, 32, 4, 2).transpose(0, 3, 1, 4, 2).reshape(16, 1024)
    view, new_core = tail(core_matrix, coeffs, gram_total, ordered, view_of(basis_modes))
    return (finished, basis_of(view), new_core)


def solution(mesh):
    return jax.shard_map(
        on_device,
        mesh=mesh,
        in_specs=(
            P(None, "gx", "gz", None),
            P(),
            P(),
            P(),
            P(None, "gx", "gz"),
            P("gx", None, "gz", None),
            P(),
        ),
        out_specs=(P(None, "gx", "gz", None), P("gx", None, "gz", None), P()),
        check_vma=False,
    )
```

```python
import functools

import jax
import jax.numpy as jnp
from jax import lax
from jax.experimental import pallas as pl
from jax.experimental.pallas import tpu as pltpu
from jax.sharding import PartitionSpec as P

F32, BF16 = jnp.float32, jnp.bfloat16
HIGH = lax.Precision.HIGHEST
SIGN_STEPS = 10
POLAR_STEPS = 3
gram_eps = 1e-06


def halves(values):
    head = values.astype(BF16)
    return head, (values - head.astype(F32)).astype(BF16)


def dot(left, right, over=((1,), (0,))):
    return lax.dot_general(left, right, (over, ((), ())), preferred_element_type=F32)


def dot_three(left, right, over=((1,), (0,))):
    (lh, ll), (rh, rl) = left, right
    return dot(lh, rh, over) + (dot(lh, rl, over) + dot(ll, rh, over))


def dot_high(left, right, over=((1,), (0,))):
    return lax.dot_general(
        left, right, (over, ((), ())), precision=HIGH, preferred_element_type=F32
    )


TN = ((0,), (0,))
NT = ((1,), (1,))


def tripled_left(pair):
    return jnp.concatenate([pair[0], pair[0], pair[1]], axis=0)


def tripled_right(pair):
    return jnp.concatenate([pair[0], pair[1], pair[0]], axis=0)


def eye(count):
    return (
        lax.broadcasted_iota(jnp.int32, (count, count), 0)
        == lax.broadcasted_iota(jnp.int32, (count, count), 1)
    ).astype(F32)


def row_places(z_lanes):
    places = []
    for zc in range(4):
        for x in range(4):
            for y in range(2):
                places.append((zc, x, y))
    return places


def take_basis(view_ref, rows_ref):
    for place, (zc, x, y) in enumerate(row_places(0)):
        for half in range(2):
            rows_ref[pl.ds(place * 32, 32), pl.ds(half * 128, 128)] = view_ref[
                pl.ds(512 * x + 4 * zc + 2 * half + y, 32, stride=16), :
            ]


def give_basis(rows, view_ref, first):
    for step in range(8):
        zc, x, y = row_places(0)[first + step]
        for half in range(2):
            view_ref[pl.ds(512 * x + 4 * zc + 2 * half + y, 32, stride=16), :] = rows[
                step * 32 : step * 32 + 32, half * 128 : half * 128 + 128
            ]


def cholesky(gram):
    count = gram.shape[0]
    row_index = lax.broadcasted_iota(jnp.int32, (count, count), 0)
    col_index = lax.broadcasted_iota(jnp.int32, (count, count), 1)
    left = gram
    right = eye(count)
    for j in range(count):
        pivot = left[j : j + 1, j : j + 1]
        scale = lax.rsqrt(pivot)
        scale = scale * (1.5 - 0.5 * pivot * scale * scale)
        column = left[:, j : j + 1] * scale
        row_l = left[j : j + 1, :] * scale
        row_r = right[j : j + 1, :] * scale
        below = row_index > j
        here = row_index == j
        left = jnp.where(below, left - column * row_l, jnp.where(here, row_l, left))
        right = jnp.where(below, right - column * row_r, jnp.where(here, row_r, right))
    return jnp.where(row_index <= col_index, left, 0.0), right


def product(left_v, left_d, right_v, right_d):
    modes = left_v.shape[1]
    lv = halves(left_v)
    rv = halves(right_v)
    ra = (rv[0][:modes], rv[1][:modes])
    lb = (lv[0][modes:], lv[1][modes:])
    rb = (rv[0][modes:], rv[1][modes:])
    main = dot_three(lv, ra)
    right48 = tripled_right(rb)
    top = dot(tripled_left(lb), right48, TN)
    low = dot(tripled_left(halves(left_d)), right48, TN)
    out_d = dot_three(lb, rb, NT) + dot_high(left_d, right_d)
    return main + jnp.concatenate([top, low], axis=0), out_d


def tail_kernel(core_ref, coeffs_ref, gram_ref, resid_ref, basis_hbm, fields_hbm,
                out_fields, out_basis, out_core, v_ref, d_ref, basis_view, basis_rows, sem, field_sem):
    modes = core_ref.shape[0]
    fetch = pltpu.make_async_copy(basis_hbm, basis_view, sem)
    fetch.start()
    passing = pltpu.make_async_copy(fields_hbm, out_fields, field_sem)
    passing.start()
    factor_t, inverse = cholesky(gram_ref[...] + gram_eps * eye(16))
    coeffs = coeffs_ref[...]
    unit = eye(modes)
    unit_d = eye(16)
    corr_a = core_ref[...] + dot_high(coeffs, coeffs, TN)
    corr_b = dot_high(factor_t, coeffs)
    corr_d = dot_high(factor_t, factor_t, NT)
    shift_a = corr_a - unit
    shift_d = corr_d - unit_d
    total = (
        jnp.sum(shift_a * shift_a, keepdims=True)
        + 2.0 * jnp.sum(corr_b * corr_b, keepdims=True)
        + jnp.sum(shift_d * shift_d, keepdims=True)
    )
    scale = 1.0 / jnp.sqrt(total)
    v_ref[:modes] = shift_a * scale
    v_ref[modes:] = corr_b * scale
    d_ref[...] = shift_d * scale
    unit_v = jnp.concatenate([unit, jnp.zeros((16, modes), F32)], axis=0)

    def sign_step(step, carry):
        v = v_ref[...]
        d = d_ref[...]
        square_v, square_d = product(v, d, v, d)
        next_v, next_d = product(
            v, d, 1.5 * unit_v - 0.5 * square_v, 1.5 * unit_d - 0.5 * square_d
        )
        v_ref[...] = next_v
        d_ref[...] = next_d
        return carry

    lax.fori_loop(0, SIGN_STEPS, sign_step, 0)

    fetch.wait()
    take_basis(basis_view, basis_rows)

    rot = 0.5 * (unit_v + v_ref[...])
    for _ in range(POLAR_STEPS):
        rh, rl = halves(rot)
        inner = dot_three((rh, rl), (rh, rl), TN)
        rot = 1.5 * rot - 0.5 * dot_three((rh, rl), halves(inner))
    rp = halves(rot)
    corr_v = jnp.concatenate([corr_a, corr_b], axis=0)
    moved = dot_three(halves(corr_v), (rp[0][:modes], rp[1][:modes]))
    rb48 = tripled_right((rp[0][modes:], rp[1][modes:]))
    moved = moved + jnp.concatenate(
        [
            dot(tripled_left(halves(corr_b)), rb48, TN),
            dot(tripled_left(halves(corr_d)), rb48, TN),
        ],
        axis=0,
    )
    out_core[...] = dot_three(rp, halves(moved), TN)

    mix = dot_high(inverse, rot[modes:], TN)
    mix48 = tripled_right(halves(mix))
    ra = (rp[0][:modes], rp[1][:modes])
    for part in range(4):
        rows = basis_rows[pl.ds(part * 256, 256), :]
        left = tripled_left(halves(resid_ref[:, part * 256 : part * 256 + 256]))
        give_basis(dot_three(halves(rows), ra) + dot(left, mix48, TN), out_basis, part * 8)
    passing.wait()


def tail(core, coeffs, gram, resid, basis_view, fields):
    vmem = pl.BlockSpec(memory_space=pltpu.VMEM)
    hbm = pl.BlockSpec(memory_space=pl.ANY)
    return pl.pallas_call(
        tail_kernel,
        out_shape=(
            jax.ShapeDtypeStruct(fields.shape, F32),
            jax.ShapeDtypeStruct((2048, 128), F32),
            jax.ShapeDtypeStruct((256, 256), F32),
        ),
        in_specs=[vmem, vmem, vmem, vmem, hbm, hbm],
        out_specs=(hbm, vmem, vmem),
        scratch_shapes=[
            pltpu.VMEM((272, 256), F32),
            pltpu.VMEM((16, 16), F32),
            pltpu.VMEM((2048, 128), F32),
            pltpu.VMEM((1024, 256), F32),
            pltpu.SemaphoreType.DMA,
            pltpu.SemaphoreType.DMA,
        ],
        compiler_params=pltpu.CompilerParams(vmem_limit_bytes=32 * 1024 * 1024),
    )(core, coeffs, gram, resid, basis_view, fields)


def view_of(basis):
    return basis.reshape(4, 128, 2, 2, 128).transpose(0, 1, 3, 2, 4).reshape(2048, 128)


def basis_of(view):
    return view.reshape(4, 128, 2, 2, 128).transpose(0, 1, 3, 2, 4).reshape(4, 128, 2, 256)


MESH = pl.DeviceIdType.MESH
press_coef = 0.25
compress_coef = 0.25
visc_coef = 0.05
heat_coef = 0.03
FIELDS = 5


def shifted(values):
    width = values.shape[-1]
    lane = lax.broadcasted_iota(jnp.int32, values.shape, 1)
    lower = jnp.where(lane == 0, 0.0, pltpu.roll(values, 1, 1))
    upper = jnp.where(lane == width - 1, 0.0, pltpu.roll(values, width - 1, 1))
    return lower, upper


def update(centre, xl, xu, zl, zu, profiles):
    courant, shear_rate, gradient = profiles
    beside = [shifted(c) for c in centre]
    keep = [1.0 - 6.0 * visc_coef - courant] * 3 + [1.0 - 6.0 * visc_coef]
    keep = keep + [1.0 - 6.0 * heat_coef - courant]
    bring = [visc_coef + courant] * 3 + [visc_coef, heat_coef + courant]
    spread = [visc_coef] * 4 + [heat_coef]
    new = []
    for f in range(FIELDS):
        around = (xu[f] + zl[f]) + (zu[f] + beside[f][0]) + beside[f][1]
        new.append(keep[f] * centre[f] + bring[f] * xl[f] + spread[f] * around)
    half_press = 0.5 * press_coef
    new[0] = new[0] - shear_rate * centre[1] - half_press * (xu[3] - xl[3])
    new[1] = new[1] - half_press * (beside[3][1] - beside[3][0])
    new[2] = new[2] - half_press * (zu[3] - zl[3])
    divergence = (xu[0] - xl[0]) + (beside[1][1] - beside[1][0]) + (zu[2] - zl[2])
    new[3] = new[3] - 0.5 * compress_coef * divergence
    new[4] = new[4] - gradient * centre[1]
    return new


def front_kernel(sizes, fields_hbm, profiles_ref, earlier_ref, basis_hbm,
                 out_fields, out_coeffs, out_gram, out_resid,
                 P, H, F, Zs, Zr, Cs, Cr, V, basis_view, basis_rows, basis_h, basis_l,
                 E2, early_send, early_slots, late_send, late_slots, S,
                 sum_send, sum_slots, sum_mid, sum_mid_slots, sum_out, sum_all,
                 c_send, c_slots, c_mid, c_mid_slots,
                 g_send, g_slots, g_mid, g_mid_slots,
                 load_sem, basis_sem, out_sem, halo_send, halo_recv,
                 group_send, group_recv):
    nx, nz = sizes
    gx = lax.axis_index("gx")
    gz = lax.axis_index("gz")
    rows_total = 1024.0 * nx * nz

    load = pltpu.make_async_copy(fields_hbm, P.at[:, 2:18, 8:24, :], load_sem)
    load.start()
    fetch = pltpu.make_async_copy(basis_hbm, basis_view, basis_sem)
    fetch.start()

    barrier = pltpu.get_barrier_semaphore()

    def greet_z(d, carry):
        pl.semaphore_signal(barrier, inc=1, device_id=(gx, lax.rem(gz + d, nz)), device_id_type=MESH)
        return carry

    lax.fori_loop(1, nz, greet_z, 0)
    for d in range(1, nx):
        pl.semaphore_signal(barrier, inc=1, device_id=(lax.rem(gx + d, nx), gz), device_id_type=MESH)
    x_beside = (lax.rem(gx + nx - 1, nx), lax.rem(gx + 1, nx))
    z_beside = (lax.rem(gz + nz - 1, nz), lax.rem(gz + 1, nz))
    for xs in range(2):
        for zs in range(2):
            pl.semaphore_signal(
                barrier, inc=1, device_id=(x_beside[xs], z_beside[zs]), device_id_type=MESH
            )

    load.wait()
    flat = P.reshape(FIELDS * 20 * 32, 256)
    for side in range(2):
        for layer in range(2):
            z = 8 + 14 * side + layer
            for f in range(FIELDS):
                for half in range(2):
                    lanes = pl.ds(128 * half, 128)
                    Zs[side, layer, f, :, lanes] = P[f, 2:18, z, lanes]
    for xs in range(2):
        for zs in range(2):
            for f in range(FIELDS):
                Cs[2 * xs + zs, f : f + 1, :] = P[f, 2 + 15 * xs, 8 + 15 * zs : 9 + 15 * zs, :]

    pl.semaphore_wait(barrier, nz - 1 + nx - 1 + 4)

    halos = []

    def send_halo(source, target, where):
        place = len(halos)
        copy = pltpu.make_async_remote_copy(
            src_ref=source, dst_ref=target, send_sem=halo_send.at[place],
            recv_sem=halo_recv.at[place], device_id=where, device_id_type=MESH,
        )
        copy.start()
        halos.append(copy)

    for side in range(2):
        send_halo(Zs.at[side], Zr.at[1 - side, :, :, 8:24, :], (gx, z_beside[side]))
    for side in range(2):
        send_halo(
            fields_hbm.at[:, 14 * side : 14 * side + 2],
            P.at[:, 18 - 18 * side : 20 - 18 * side, 8:24, :],
            (x_beside[side], gz),
        )
    for xs in range(2):
        for zs in range(2):
            send_halo(
                Cs.at[2 * xs + zs], Cr.at[2 * (1 - xs) + 1 - zs], (x_beside[xs], z_beside[zs])
            )

    def spread_z(place, source, slots):
        def body(d, carry):
            peer = lax.rem(gz + d, nz)
            pltpu.make_async_remote_copy(
                src_ref=source(peer), dst_ref=slots.at[gz], send_sem=group_send.at[place],
                recv_sem=group_recv.at[place], device_id=(gx, peer), device_id_type=MESH,
            ).start()
            return carry

        lax.fori_loop(1, nz, body, 0)

    def spread_x(place, source, slots):
        for d in range(1, nx):
            peer = lax.rem(gx + d, nx)
            pltpu.make_async_remote_copy(
                src_ref=source, dst_ref=slots.at[gx], send_sem=group_send.at[place],
                recv_sem=group_recv.at[place], device_id=(peer, gz), device_id_type=MESH,
            ).start()

    def wait_all(sems, place, slots):
        some = slots.at[pl.ds(0, slots.shape[0] - 1)]
        pltpu.make_async_copy(some, some, sems.at[place]).wait()

    E2[...] = jnp.zeros_like(E2)
    for m in range(14):
        for x in range(4):
            E2[x * 16 + m : x * 16 + m + 1, :] = earlier_ref[m, x : x + 1, :]
    turned = E2[...].T
    turned = jnp.concatenate([turned[64 * z : 64 * z + 64] for z in range(4)], axis=1)
    for i in range(32):
        early_send[i] = turned[2 * i : 2 * i + 2]
    spread_z(0, lambda peer: early_send.at[peer], early_slots)
    early_slots[gz] = early_send[gz]

    fetch.wait()
    take_basis(basis_view, basis_rows)
    rows = basis_rows[...]
    head = rows.astype(BF16)
    basis_h[...] = head
    basis_l[...] = (rows - head.astype(F32)).astype(BF16)

    def pair():
        return basis_h[...], basis_l[...]

    inner = dot_three(pair(), pair(), TN)
    sum_send[:, :, 256:] = jnp.zeros((32, 8, 128), F32)
    for i in range(32):
        sum_send[i, :, :256] = inner[8 * i : 8 * i + 8]

    wait_all(group_recv, 0, early_slots)
    got = jnp.concatenate([early_slots[:, 0, :], early_slots[:, 1, :]], axis=0).T
    for zx in range(16):
        S[:, zx * 64 : zx * 64 + 64] = got[zx * 16 : zx * 16 + 16]
    c_early = dot_three(halves(S[...]), pair())
    for m in range(16):
        for half in range(2):
            sum_send[2 * m + half, 0:1, 256:] = c_early[m : m + 1, 128 * half : 128 * half + 128]
    spread_z(1, lambda peer: sum_send.at[peer], sum_slots)
    sum_slots[gz] = sum_send[gz]

    profiles = [profiles_ref[k : k + 1, :] for k in range(3)]
    for copy in halos:
        copy.wait_recv()
    for f in range(FIELDS):
        for xs in range(2):
            row = 7 + 17 * xs
            for zs in range(2):
                Zr[zs, 1 - zs, f, row : row + 1, :] = Cr[2 * xs + zs, f : f + 1, :]
        for zs in range(2):
            z = 7 + 17 * zs
            P[f, 1:19, z, :] = Zr[zs, 1 - zs, f, 7:25, :]

    def first(i, carry):
        centre = [P[f, i + 1, 8:24, :] for f in range(FIELDS)]
        xl = [P[f, i, 8:24, :] for f in range(FIELDS)]
        xu = [P[f, i + 2, 8:24, :] for f in range(FIELDS)]
        zl = [P[f, i + 1, 7:23, :] for f in range(FIELDS)]
        zu = [P[f, i + 1, 9:25, :] for f in range(FIELDS)]
        new = update(centre, xl, xu, zl, zu, profiles)
        for f in range(FIELDS):
            H[f, i, 8:24, :] = new[f]
        return carry

    lax.fori_loop(0, 18, first, 0)
    for side in range(2):
        centre = [Zr[side, 1 - side, f, 8:24, :] for f in range(FIELDS)]
        xl = [Zr[side, 1 - side, f, 7:23, :] for f in range(FIELDS)]
        xu = [Zr[side, 1 - side, f, 9:25, :] for f in range(FIELDS)]
        outer = [Zr[side, side, f, 8:24, :] for f in range(FIELDS)]
        inside = [Zs[side, side, f, :, :] for f in range(FIELDS)]
        zl, zu = (outer, inside) if side == 0 else (inside, outer)
        new = update(centre, xl, xu, zl, zu, profiles)
        for f in range(FIELDS):
            H[f, 1:17, 7 + 17 * side, :] = new[f]

    def second(i, carry):
        centre = [H[f, i + 1, 8:24, :] for f in range(FIELDS)]
        xl = [H[f, i, 8:24, :] for f in range(FIELDS)]
        xu = [H[f, i + 2, 8:24, :] for f in range(FIELDS)]
        zl = [H[f, i + 1, 7:23, :] for f in range(FIELDS)]
        zu = [H[f, i + 1, 9:25, :] for f in range(FIELDS)]
        new = update(centre, xl, xu, zl, zu, profiles)
        for f in range(FIELDS):
            F[f, i, :, :] = new[f]
        return carry

    lax.fori_loop(0, 16, second, 0)
    store = pltpu.make_async_copy(F, out_fields, out_sem)
    store.start()

    for xg in range(4):
        V[16 * xg : 16 * xg + 16, :] = (H[0, 4 * xg + 1, 8:24, :] + H[0, 4 * xg + 2, 8:24, :]) + (
            H[0, 4 * xg + 3, 8:24, :] + H[0, 4 * xg + 4, 8:24, :]
        )
        V[64 + 16 * xg : 80 + 16 * xg, :] = (F[0, 4 * xg] + F[0, 4 * xg + 1]) + (
            F[0, 4 * xg + 2] + F[0, 4 * xg + 3]
        )
    to = lax.broadcasted_iota(jnp.int32, (128, 128), 0)
    of = lax.broadcasted_iota(jnp.int32, (128, 128), 1)
    wanted = ((lax.rem(of, 16) // 4) * 4 + lax.rem(of, 64) // 16) * 8 + 6 + of // 64
    gathered = dot_high((to == wanted).astype(F32), V[...])
    block = (
        lax.broadcasted_iota(jnp.int32, (64, 256), 0)
        == lax.broadcasted_iota(jnp.int32, (64, 256), 1) // 4
    ).astype(F32) * (1.0 / 64.0)
    coarse = dot_high(block, gathered, NT)
    for i in range(32):
        late_send[i] = coarse[2 * i : 2 * i + 2]
    spread_z(2, lambda peer: late_send.at[peer], late_slots)
    late_slots[gz] = late_send[gz]

    wait_all(group_recv, 1, sum_slots)
    total = sum_slots[0]
    for j in range(1, 32):
        total = total + sum_slots[j]
    sum_mid[...] = total
    spread_x(3, sum_mid, sum_mid_slots)
    sum_mid_slots[gx] = total

    wait_all(group_recv, 2, late_slots)
    got = jnp.concatenate([late_slots[:, 0, :], late_slots[:, 1, :]], axis=0).T
    for zx in range(16):
        S[8:16, zx * 64 : zx * 64 + 64] = S[8:16, zx * 64 : zx * 64 + 64] + got[zx * 8 : zx * 8 + 8]
    low = S[8:16, :]
    low = jnp.where(lax.broadcasted_iota(jnp.int32, low.shape, 0) >= 6, low, 0.0)
    c_late = dot_three(halves(jnp.concatenate([jnp.zeros_like(low), low], axis=0)), pair())[14:16]
    c_send[...] = c_late
    spread_z(4, lambda peer: c_send, c_slots)
    c_slots[gz] = c_late

    wait_all(group_recv, 3, sum_mid_slots)
    total = ((sum_mid_slots[0] + sum_mid_slots[1]) + sum_mid_slots[2]) + sum_mid_slots[3]
    sum_out[...] = total
    spread_z(5, lambda peer: sum_out, sum_all)
    sum_all[gz] = total

    wait_all(group_recv, 4, c_slots)
    total = c_slots[0]
    for j in range(1, 32):
        total = total + c_slots[j]
    c_mid[...] = total
    spread_x(6, c_mid, c_mid_slots)
    c_mid_slots[gx] = total

    wait_all(group_recv, 5, sum_all)
    metric = sum_all[:, :, :256].reshape(256, 256) * (1.0 / rows_total)
    early_rows = [
        jnp.concatenate([sum_all[2 * m, 0:1, 256:], sum_all[2 * m + 1, 0:1, 256:]], axis=1)
        for m in range(14)
    ]
    wait_all(group_recv, 6, c_mid_slots)
    total = ((c_mid_slots[0] + c_mid_slots[1]) + c_mid_slots[2]) + c_mid_slots[3]
    c_one = jnp.concatenate(early_rows + [total], axis=0) * (1.0 / rows_total)
    coeffs = c_one + (c_one - dot_high(c_one, metric))
    out_coeffs[...] = coeffs
    resid = S[...] - dot_three(halves(coeffs), pair(), NT)
    out_resid[...] = resid
    gram = dot_high(resid, resid, NT) * (1.0 / rows_total)
    g_send[...] = gram
    spread_z(7, lambda peer: g_send, g_slots)
    g_slots[gz] = gram
    wait_all(group_recv, 7, g_slots)
    total = g_slots[0]
    for j in range(1, 32):
        total = total + g_slots[j]
    g_mid[...] = total
    spread_x(8, g_mid, g_mid_slots)
    g_mid_slots[gx] = total
    wait_all(group_recv, 8, g_mid_slots)
    out_gram[...] = ((g_mid_slots[0] + g_mid_slots[1]) + g_mid_slots[2]) + g_mid_slots[3]

    for copy in halos:
        copy.wait_send()
    for place, slots in enumerate([
        early_slots, sum_slots, late_slots, sum_mid_slots, c_slots, sum_all, c_mid_slots,
        g_slots, g_mid_slots,
    ]):
        wait_all(group_send, place, slots)
    store.wait()


def front(sizes, fields, profiles, earlier, basis_view):
    nx, nz = sizes
    vmem = pl.BlockSpec(memory_space=pltpu.VMEM)
    hbm = pl.BlockSpec(memory_space=pl.ANY)
    v = pltpu.VMEM
    return pl.pallas_call(
        functools.partial(front_kernel, sizes),
        out_shape=(
            jax.ShapeDtypeStruct(fields.shape, F32),
            jax.ShapeDtypeStruct((16, 256), F32),
            jax.ShapeDtypeStruct((16, 16), F32),
            jax.ShapeDtypeStruct((16, 1024), F32),
        ),
        in_specs=[hbm, vmem, vmem, hbm],
        out_specs=(hbm, vmem, vmem, vmem),
        scratch_shapes=[
            v((5, 20, 32, 256), F32),
            v((5, 18, 32, 256), F32),
            v((5, 16, 16, 256), F32),
            v((2, 2, 5, 16, 256), F32),
            v((2, 2, 5, 32, 256), F32),
            v((4, 8, 256), F32),
            v((4, 8, 256), F32),
            v((128, 256), F32),
            v((2048, 128), F32),
            v((1024, 256), F32),
            v((1024, 256), BF16),
            v((1024, 256), BF16),
            v((64, 256), F32),
            v((32, 2, 256), F32),
            v((32, 2, 256), F32),
            v((32, 2, 128), F32),
            v((32, 2, 128), F32),
            v((16, 1024), F32),
            v((32, 8, 384), F32),
            v((32, 8, 384), F32),
            v((8, 384), F32),
            v((4, 8, 384), F32),
            v((8, 384), F32),
            v((32, 8, 384), F32),
            v((2, 256), F32),
            v((32, 2, 256), F32),
            v((2, 256), F32),
            v((4, 2, 256), F32),
            v((16, 16), F32),
            v((32, 16, 16), F32),
            v((16, 16), F32),
            v((4, 16, 16), F32),
            pltpu.SemaphoreType.DMA,
            pltpu.SemaphoreType.DMA,
            pltpu.SemaphoreType.DMA,
            pltpu.SemaphoreType.DMA((8,)),
            pltpu.SemaphoreType.DMA((8,)),
            pltpu.SemaphoreType.DMA((9,)),
            pltpu.SemaphoreType.DMA((9,)),
        ],
        compiler_params=pltpu.CompilerParams(
            collective_id=0, has_side_effects=True, vmem_limit_bytes=48 * 1024 * 1024
        ),
    )(fields, profiles, earlier, basis_view)


def on_device(fields, courant, shear_rate, gradient, earlier, basis_modes, core_matrix):
    sizes = (lax.axis_size("gx"), lax.axis_size("gz"))
    view = view_of(basis_modes)
    profiles = jnp.stack([courant, shear_rate, gradient])
    finished, coeffs, gram, resid = front(sizes, fields, profiles, earlier, view)
    finished, new_view, new_core = tail(core_matrix, coeffs, gram, resid, view, finished)
    return (finished, basis_of(new_view), new_core)


def solution(mesh):
    return jax.shard_map(
        on_device,
        mesh=mesh,
        in_specs=(
            P(None, "gx", "gz", None),
            P(),
            P(),
            P(),
            P(None, "gx", "gz"),
            P("gx", None, "gz", None),
            P(),
        ),
        out_specs=(P(None, "gx", "gz", None), P("gx", None, "gz", None), P()),
        check_vma=False,
    )
```

```python
import functools

import jax
import jax.numpy as jnp
from jax import lax
from jax.experimental import pallas as pl
from jax.experimental.pallas import tpu as pltpu
from jax.sharding import PartitionSpec as P

F32, BF16 = jnp.float32, jnp.bfloat16
HIGH = lax.Precision.HIGHEST
SIGN_STEPS = 10
POLAR_STEPS = 3
gram_eps = 1e-06


def halves(values):
    head = values.astype(BF16)
    return head, (values - head.astype(F32)).astype(BF16)


def dot(left, right, over=((1,), (0,))):
    return lax.dot_general(left, right, (over, ((), ())), preferred_element_type=F32)


def dot_three(left, right, over=((1,), (0,))):
    (lh, ll), (rh, rl) = left, right
    return dot(lh, rh, over) + (dot(lh, rl, over) + dot(ll, rh, over))


def dot_high(left, right, over=((1,), (0,))):
    return lax.dot_general(
        left, right, (over, ((), ())), precision=HIGH, preferred_element_type=F32
    )


TN = ((0,), (0,))
NT = ((1,), (1,))


def tripled_left(pair):
    return jnp.concatenate([pair[0], pair[0], pair[1]], axis=0)


def tripled_right(pair):
    return jnp.concatenate([pair[0], pair[1], pair[0]], axis=0)


def eye(count):
    return (
        lax.broadcasted_iota(jnp.int32, (count, count), 0)
        == lax.broadcasted_iota(jnp.int32, (count, count), 1)
    ).astype(F32)


def row_places(z_lanes):
    places = []
    for zc in range(4):
        for x in range(4):
            for y in range(2):
                places.append((zc, x, y))
    return places


def take_basis(view_ref, rows_ref):
    for place, (zc, x, y) in enumerate(row_places(0)):
        for half in range(2):
            rows_ref[pl.ds(place * 32, 32), pl.ds(half * 128, 128)] = view_ref[
                pl.ds(512 * x + 4 * zc + 2 * half + y, 32, stride=16), :
            ]


def give_basis(rows, view_ref, first):
    for step in range(8):
        zc, x, y = row_places(0)[first + step]
        for half in range(2):
            view_ref[pl.ds(512 * x + 4 * zc + 2 * half + y, 32, stride=16), :] = rows[
                step * 32 : step * 32 + 32, half * 128 : half * 128 + 128
            ]


def cholesky(gram):
    count = gram.shape[0]
    row_index = lax.broadcasted_iota(jnp.int32, (count, count), 0)
    col_index = lax.broadcasted_iota(jnp.int32, (count, count), 1)
    left = gram
    right = eye(count)
    pivots = jnp.zeros((1, count), F32)
    for j in range(count):
        pivot = left[j : j + 1, j : j + 1]
        pivots = jnp.where(col_index[:1] == j, pivot, pivots)
        scale = lax.rsqrt(pivot)
        scale = scale * (1.5 - 0.5 * pivot * scale * scale)
        column = left[:, j : j + 1] * scale
        row_l = left[j : j + 1, :] * scale
        row_r = right[j : j + 1, :] * scale
        below = row_index > j
        here = row_index == j
        left = jnp.where(below, left - column * row_l, jnp.where(here, row_l, left))
        right = jnp.where(below, right - column * row_r, jnp.where(here, row_r, right))
    return jnp.where(row_index <= col_index, left, 0.0), right, pivots


def product(left_v, left_d, right_v, right_d):
    modes = left_v.shape[1]
    lv = halves(left_v)
    rv = halves(right_v)
    ra = (rv[0][:modes], rv[1][:modes])
    lb = (lv[0][modes:], lv[1][modes:])
    rb = (rv[0][modes:], rv[1][modes:])
    main = dot_three(lv, ra)
    right48 = tripled_right(rb)
    top = dot(tripled_left(lb), right48, TN)
    low = dot(tripled_left(halves(left_d)), right48, TN)
    out_d = dot_three(lb, rb, NT) + dot_high(left_d, right_d)
    return main + jnp.concatenate([top, low], axis=0), out_d


def tail_kernel(core_ref, coeffs_ref, factor_ref, inverse_ref, resid_ref, basis_hbm, fields_hbm,
                out_fields, out_basis, out_core, v_ref, d_ref, basis_view, basis_rows, held, sem, field_sem):
    modes = core_ref.shape[0]
    fetch = pltpu.make_async_copy(basis_hbm, basis_view, sem)
    fetch.start()
    taking = pltpu.make_async_copy(fields_hbm, held, field_sem)
    taking.start()
    factor_t = factor_ref[...]
    inverse = inverse_ref[...]
    coeffs = coeffs_ref[...]
    unit = eye(modes)
    unit_d = eye(16)
    corr_a = core_ref[...] + dot_high(coeffs, coeffs, TN)
    corr_b = dot_high(factor_t, coeffs)
    corr_d = dot_high(factor_t, factor_t, NT)
    shift_a = corr_a - unit
    shift_d = corr_d - unit_d
    total = (
        jnp.sum(shift_a * shift_a, keepdims=True)
        + 2.0 * jnp.sum(corr_b * corr_b, keepdims=True)
        + jnp.sum(shift_d * shift_d, keepdims=True)
    )
    scale = 1.0 / jnp.sqrt(total)
    v_ref[:modes] = shift_a * scale
    v_ref[modes:] = corr_b * scale
    d_ref[...] = shift_d * scale
    unit_v = jnp.concatenate([unit, jnp.zeros((16, modes), F32)], axis=0)

    def sign_step(step, carry):
        v = v_ref[...]
        d = d_ref[...]
        square_v, square_d = product(v, d, v, d)
        next_v, next_d = product(
            v, d, 1.5 * unit_v - 0.5 * square_v, 1.5 * unit_d - 0.5 * square_d
        )
        v_ref[...] = next_v
        d_ref[...] = next_d
        return carry

    lax.fori_loop(0, SIGN_STEPS, sign_step, 0)

    fetch.wait()
    taking.wait()
    passing = pltpu.make_async_copy(held, out_fields, field_sem)
    passing.start()
    take_basis(basis_view, basis_rows)

    rot = 0.5 * (unit_v + v_ref[...])
    for _ in range(POLAR_STEPS):
        rh, rl = halves(rot)
        inner = dot_three((rh, rl), (rh, rl), TN)
        rot = 1.5 * rot - 0.5 * dot_three((rh, rl), halves(inner))
    rp = halves(rot)
    corr_v = jnp.concatenate([corr_a, corr_b], axis=0)
    moved = dot_three(halves(corr_v), (rp[0][:modes], rp[1][:modes]))
    rb48 = tripled_right((rp[0][modes:], rp[1][modes:]))
    moved = moved + jnp.concatenate(
        [
            dot(tripled_left(halves(corr_b)), rb48, TN),
            dot(tripled_left(halves(corr_d)), rb48, TN),
        ],
        axis=0,
    )
    out_core[...] = dot_three(rp, halves(moved), TN)

    mix = dot_high(inverse, rot[modes:], TN)
    mix48 = tripled_right(halves(mix))
    ra = (rp[0][:modes], rp[1][:modes])
    for part in range(4):
        rows = basis_rows[pl.ds(part * 256, 256), :]
        left = tripled_left(halves(resid_ref[:, part * 256 : part * 256 + 256]))
        give_basis(dot_three(halves(rows), ra) + dot(left, mix48, TN), out_basis, part * 8)
    passing.wait()


def tail(core, coeffs, factor_t, inverse, resid, basis_view, fields):
    vmem = pl.BlockSpec(memory_space=pltpu.VMEM)
    hbm = pl.BlockSpec(memory_space=pltpu.HBM)
    return pl.pallas_call(
        tail_kernel,
        out_shape=(
            jax.ShapeDtypeStruct(fields.shape, F32),
            jax.ShapeDtypeStruct((2048, 128), F32),
            jax.ShapeDtypeStruct((256, 256), F32),
        ),
        in_specs=[vmem, vmem, vmem, vmem, vmem, hbm, hbm],
        out_specs=(hbm, vmem, vmem),
        scratch_shapes=[
            pltpu.VMEM((272, 256), F32),
            pltpu.VMEM((16, 16), F32),
            pltpu.VMEM((2048, 128), F32),
            pltpu.VMEM((1024, 256), F32),
            pltpu.VMEM(fields.shape, F32),
            pltpu.SemaphoreType.DMA,
            pltpu.SemaphoreType.DMA,
        ],
        compiler_params=pltpu.CompilerParams(vmem_limit_bytes=60 * 1024 * 1024),
    )(core, coeffs, factor_t, inverse, resid, basis_view, fields)


def view_of(basis):
    return basis.reshape(4, 128, 2, 2, 128).transpose(0, 1, 3, 2, 4).reshape(2048, 128)


def basis_of(view):
    return view.reshape(4, 128, 2, 2, 128).transpose(0, 1, 3, 2, 4).reshape(4, 128, 2, 256)


MESH = pl.DeviceIdType.MESH
press_coef = 0.25
compress_coef = 0.25
visc_coef = 0.05
heat_coef = 0.03
FIELDS = 5
least_pivot = 2.0**-7


def shifted(values):
    width = values.shape[-1]
    lane = lax.broadcasted_iota(jnp.int32, values.shape, 1)
    lower = jnp.where(lane == 0, 0.0, pltpu.roll(values, 1, 1))
    upper = jnp.where(lane == width - 1, 0.0, pltpu.roll(values, width - 1, 1))
    return lower, upper


def update(centre, xl, xu, zl, zu, profiles):
    courant, shear_rate, gradient = profiles
    beside = [shifted(c) for c in centre]
    keep = [1.0 - 6.0 * visc_coef - courant] * 3 + [1.0 - 6.0 * visc_coef]
    keep = keep + [1.0 - 6.0 * heat_coef - courant]
    bring = [visc_coef + courant] * 3 + [visc_coef, heat_coef + courant]
    spread = [visc_coef] * 4 + [heat_coef]
    new = []
    for f in range(FIELDS):
        around = (xu[f] + zl[f]) + (zu[f] + beside[f][0]) + beside[f][1]
        new.append(keep[f] * centre[f] + bring[f] * xl[f] + spread[f] * around)
    half_press = 0.5 * press_coef
    new[0] = new[0] - shear_rate * centre[1] - half_press * (xu[3] - xl[3])
    new[1] = new[1] - half_press * (beside[3][1] - beside[3][0])
    new[2] = new[2] - half_press * (zu[3] - zl[3])
    divergence = (xu[0] - xl[0]) + (beside[1][1] - beside[1][0]) + (zu[2] - zl[2])
    new[3] = new[3] - 0.5 * compress_coef * divergence
    new[4] = new[4] - gradient * centre[1]
    return new


def front_kernel(sizes, fields_hbm, courant_hbm, shear_hbm, gradient_hbm, earlier_hbm, basis_hbm,
                 out_fields, out_coeffs, out_factor, out_inverse, out_sound, out_resid,
                 P, H, F, Zs, Zr, Cs, Cr, V, basis_view, basis_rows, basis_h, basis_l,
                 E2, early_send, early_slots, late_send, late_slots, S,
                 sum_send, sum_slots, sum_mid, sum_mid_slots, sum_out, sum_all,
                 c_send, c_other, c_mid, c_slots,
                 earlier_ref, profile_rows, small_sem, load_sem, basis_sem, out_sem, halo_send, halo_recv,
                 group_send, group_recv):
    nx, nz = sizes
    gx = lax.axis_index("gx")
    gz = lax.axis_index("gz")
    rows_total = 1024.0 * nx * nz

    barrier = pltpu.get_barrier_semaphore()
    x_beside = (lax.rem(gx + nx - 1, nx), lax.rem(gx + 1, nx))
    z_beside = (lax.rem(gz + nz - 1, nz), lax.rem(gz + 1, nz))

    def greet(where):
        pl.semaphore_signal(barrier, inc=1, device_id=where, device_id_type=MESH)

    def greet_z(d, carry):
        greet((gx, lax.rem(gz + d, nz)))
        return carry

    load = pltpu.make_async_copy(fields_hbm, P.at[:, 2:18, 8:24, :], load_sem)
    load.start()
    fetch = pltpu.make_async_copy(basis_hbm, basis_view, basis_sem)
    fetch.start()
    small = [
        pltpu.make_async_copy(earlier_hbm, earlier_ref, small_sem.at[0]),
        pltpu.make_async_copy(courant_hbm, profile_rows.at[0], small_sem.at[1]),
        pltpu.make_async_copy(shear_hbm, profile_rows.at[1], small_sem.at[2]),
        pltpu.make_async_copy(gradient_hbm, profile_rows.at[2], small_sem.at[3]),
    ]
    for copy in small:
        copy.start()
    for d in range(1, nx):
        greet((lax.rem(gx + d, nx), gz))
    for xs in range(2):
        for zs in range(2):
            greet((x_beside[xs], z_beside[zs]))
    lax.fori_loop(1, nz, greet_z, 0)

    load.wait()
    pl.semaphore_wait(barrier, nz - 1 + nx - 1 + 4)

    halos = []

    def send_halo(source, target, where):
        place = len(halos)
        copy = pltpu.make_async_remote_copy(
            src_ref=source, dst_ref=target, send_sem=halo_send.at[place],
            recv_sem=halo_recv.at[place], device_id=where, device_id_type=MESH,
        )
        copy.start()
        halos.append(copy)

    for side in range(2):
        send_halo(
            P.at[:, 2 + 14 * side : 4 + 14 * side, 8:24, :],
            P.at[:, 18 - 18 * side : 20 - 18 * side, 8:24, :],
            (x_beside[side], gz),
        )

    for side in range(2):
        for layer in range(2):
            z = 8 + 14 * side + layer
            for f in range(FIELDS):
                for half in range(2):
                    lanes = pl.ds(128 * half, 128)
                    Zs[side, layer, f, :, lanes] = P[f, 2:18, z, lanes]
    for xs in range(2):
        for zs in range(2):
            for f in range(FIELDS):
                Cs[2 * xs + zs, f : f + 1, :] = P[f, 2 + 15 * xs, 8 + 15 * zs : 9 + 15 * zs, :]

    for side in range(2):
        send_halo(Zs.at[side], Zr.at[1 - side, :, :, 8:24, :], (gx, z_beside[side]))
    for xs in range(2):
        for zs in range(2):
            send_halo(
                Cs.at[2 * xs + zs], Cr.at[2 * (1 - xs) + 1 - zs], (x_beside[xs], z_beside[zs])
            )

    def spread_z(place, source, slots):
        def body(d, carry):
            peer = lax.rem(gz + d, nz)
            pltpu.make_async_remote_copy(
                src_ref=source(peer), dst_ref=slots.at[gz], send_sem=group_send.at[place],
                recv_sem=group_recv.at[place], device_id=(gx, peer), device_id_type=MESH,
            ).start()
            return carry

        lax.fori_loop(1, nz, body, 0)

    def spread_x(place, source, slots):
        for d in range(1, nx):
            peer = lax.rem(gx + d, nx)
            pltpu.make_async_remote_copy(
                src_ref=source, dst_ref=slots.at[gx], send_sem=group_send.at[place],
                recv_sem=group_recv.at[place], device_id=(peer, gz), device_id_type=MESH,
            ).start()

    core = lax.rem(gx, 2)
    chip = (gx // 2) * nz + gz
    chips = (nx // 2) * nz

    def send_core(place, source, target):
        pltpu.make_async_remote_copy(
            src_ref=source, dst_ref=target, send_sem=group_send.at[place],
            recv_sem=group_recv.at[place], device_id=(gx + 1 - 2 * core, gz), device_id_type=MESH,
        ).start()

    def spread_chips(place, source, slots):
        def body(d, carry):
            peer = lax.rem(chip + d, chips)
            where = (2 * (peer // nz) + core, lax.rem(peer, nz))
            pltpu.make_async_remote_copy(
                src_ref=source, dst_ref=slots.at[chip], send_sem=group_send.at[place],
                recv_sem=group_recv.at[place], device_id=where, device_id_type=MESH,
            ).start()
            return carry

        lax.fori_loop(1, chips, body, 0)

    def wait_one(sems, place, part):
        pltpu.make_async_copy(part, part, sems.at[place]).wait()

    def sum_slots_of(slots):
        terms = [slots[j] for j in range(slots.shape[0])]
        while len(terms) > 1:
            terms = [a + b for a, b in zip(terms[::2], terms[1::2])] + terms[len(terms) & ~1 :]
        return terms[0]

    def wait_all(sems, place, slots):
        some = slots.at[pl.ds(0, slots.shape[0] - 1)]
        pltpu.make_async_copy(some, some, sems.at[place]).wait()

    for copy in small:
        copy.wait()
    E2[...] = jnp.zeros_like(E2)
    for m in range(14):
        for x in range(4):
            E2[x * 16 + m : x * 16 + m + 1, :] = earlier_ref[m, x : x + 1, :]
    turned = E2[...].T
    turned = jnp.concatenate([turned[64 * z : 64 * z + 64] for z in range(4)], axis=1)
    for i in range(32):
        early_send[i] = turned[2 * i : 2 * i + 2]
    spread_z(0, lambda peer: early_send.at[peer], early_slots)
    early_slots[gz] = early_send[gz]

    fetch.wait()
    take_basis(basis_view, basis_rows)
    rows = basis_rows[...]
    head = rows.astype(BF16)
    basis_h[...] = head
    basis_l[...] = (rows - head.astype(F32)).astype(BF16)

    def pair():
        return basis_h[...], basis_l[...]

    inner = dot_three(pair(), pair(), TN)
    for i in range(32):
        sum_send[i, :, :256] = inner[4 * i : 4 * i + 4]
        sum_send[i, :, 256:384] = inner[128 + 4 * i : 132 + 4 * i, 128:]

    wait_all(group_recv, 0, early_slots)
    got = jnp.concatenate([early_slots[:, 0, :], early_slots[:, 1, :]], axis=0).T
    for zx in range(16):
        S[:, zx * 64 : zx * 64 + 64] = got[zx * 16 : zx * 16 + 16]
    c_early = dot_three(halves(S[...]), pair())
    k_early = dot_three(halves(S[...]), halves(S[...]), NT)
    k_early = jnp.concatenate([k_early, jnp.zeros((16, 112), F32)], axis=1)
    lane = lax.broadcasted_iota(jnp.int32, (4, 128), 1)
    for i in range(32):
        part = c_early[4 * (i // 8) : 4 * (i // 8) + 4, 128 * (i % 8 // 4) : 128 * (i % 8 // 4) + 128]
        part = part if i % 4 == 0 else pltpu.roll(part, 128 - 32 * (i % 4), 1)
        if i % 8 == 0:
            beyond = pltpu.roll(k_early[i // 2 : i // 2 + 4], 32, 1)
            part = jnp.where(lane < 32, part, beyond)
        sum_send[i, :, 384:] = part
    spread_z(1, lambda peer: sum_send.at[peer], sum_slots)
    sum_slots[gz] = sum_send[gz]

    profiles = [profile_rows[k] for k in range(3)]
    for copy in halos:
        copy.wait_recv()
    for f in range(FIELDS):
        for xs in range(2):
            row = 7 + 17 * xs
            for zs in range(2):
                Zr[zs, 1 - zs, f, row : row + 1, :] = Cr[2 * xs + zs, f : f + 1, :]
        for zs in range(2):
            z = 7 + 17 * zs
            P[f, 1:19, z, :] = Zr[zs, 1 - zs, f, 7:25, :]

    def first(i, carry):
        centre = [P[f, i + 1, 8:24, :] for f in range(FIELDS)]
        xl = [P[f, i, 8:24, :] for f in range(FIELDS)]
        xu = [P[f, i + 2, 8:24, :] for f in range(FIELDS)]
        zl = [P[f, i + 1, 7:23, :] for f in range(FIELDS)]
        zu = [P[f, i + 1, 9:25, :] for f in range(FIELDS)]
        new = update(centre, xl, xu, zl, zu, profiles)
        for f in range(FIELDS):
            H[f, i, 8:24, :] = new[f]
        return carry

    lax.fori_loop(0, 18, first, 0)
    for side in range(2):
        centre = [Zr[side, 1 - side, f, 8:24, :] for f in range(FIELDS)]
        xl = [Zr[side, 1 - side, f, 7:23, :] for f in range(FIELDS)]
        xu = [Zr[side, 1 - side, f, 9:25, :] for f in range(FIELDS)]
        outer = [Zr[side, side, f, 8:24, :] for f in range(FIELDS)]
        inside = [Zs[side, side, f, :, :] for f in range(FIELDS)]
        zl, zu = (outer, inside) if side == 0 else (inside, outer)
        new = update(centre, xl, xu, zl, zu, profiles)
        for f in range(FIELDS):
            H[f, 1:17, 7 + 17 * side, :] = new[f]

    def second(i, carry):
        centre = [H[f, i + 1, 8:24, :] for f in range(FIELDS)]
        xl = [H[f, i, 8:24, :] for f in range(FIELDS)]
        xu = [H[f, i + 2, 8:24, :] for f in range(FIELDS)]
        zl = [H[f, i + 1, 7:23, :] for f in range(FIELDS)]
        zu = [H[f, i + 1, 9:25, :] for f in range(FIELDS)]
        new = update(centre, xl, xu, zl, zu, profiles)
        for f in range(FIELDS):
            F[f, i, :, :] = new[f]
        return carry

    lax.fori_loop(0, 16, second, 0)
    store = pltpu.make_async_copy(F, out_fields, out_sem)
    store.start()

    for xg in range(4):
        V[16 * xg : 16 * xg + 16, :] = (H[0, 4 * xg + 1, 8:24, :] + H[0, 4 * xg + 2, 8:24, :]) + (
            H[0, 4 * xg + 3, 8:24, :] + H[0, 4 * xg + 4, 8:24, :]
        )
        V[64 + 16 * xg : 80 + 16 * xg, :] = (F[0, 4 * xg] + F[0, 4 * xg + 1]) + (
            F[0, 4 * xg + 2] + F[0, 4 * xg + 3]
        )
    to = lax.broadcasted_iota(jnp.int32, (128, 128), 0)
    of = lax.broadcasted_iota(jnp.int32, (128, 128), 1)
    wanted = ((lax.rem(of, 16) // 4) * 4 + lax.rem(of, 64) // 16) * 8 + 6 + of // 64
    gathered = dot_high((to == wanted).astype(F32), V[...])
    block = (
        lax.broadcasted_iota(jnp.int32, (64, 256), 0)
        == lax.broadcasted_iota(jnp.int32, (64, 256), 1) // 4
    ).astype(F32) * (1.0 / 64.0)
    coarse = dot_high(block, gathered, NT)
    for i in range(32):
        late_send[i] = coarse[2 * i : 2 * i + 2]
    spread_z(2, lambda peer: late_send.at[peer], late_slots)
    late_slots[gz] = late_send[gz]

    wait_all(group_recv, 1, sum_slots)
    total = sum_slots_of(sum_slots)
    sum_mid[...] = total
    spread_x(3, sum_mid, sum_mid_slots)
    sum_mid_slots[gx] = total

    wait_all(group_recv, 3, sum_mid_slots)
    total = ((sum_mid_slots[0] + sum_mid_slots[1]) + sum_mid_slots[2]) + sum_mid_slots[3]
    sum_out[...] = total
    spread_z(5, lambda peer: sum_out, sum_all)
    sum_all[gz] = total

    wait_all(group_recv, 2, late_slots)
    got = jnp.concatenate([late_slots[:, 0, :], late_slots[:, 1, :]], axis=0).T
    for zx in range(16):
        S[8:16, zx * 64 : zx * 64 + 64] = S[8:16, zx * 64 : zx * 64 + 64] + got[zx * 8 : zx * 8 + 8]
    low = S[8:16, :]
    low = jnp.where(lax.broadcasted_iota(jnp.int32, low.shape, 0) >= 6, low, 0.0)
    late = halves(jnp.concatenate([jnp.zeros_like(low), low], axis=0))
    c_late = dot_three(late, pair())[14:16]
    k_late = dot_three(late, halves(S[...]), NT)[14:16]
    late = jnp.concatenate([c_late, k_late, jnp.zeros((2, 112), F32)], axis=1)
    c_send[...] = late
    send_core(4, c_send, c_other)
    wait_one(group_recv, 4, c_other)
    both = late + c_other[...]
    c_mid[...] = both
    spread_chips(6, c_mid, c_slots)
    c_slots[chip] = both

    wait_all(group_recv, 5, sum_all)
    every = sum_all[...].reshape(128, 512)
    cross = every[:, 128:256]
    metric = jnp.concatenate(
        [every[:, :256], jnp.concatenate([cross.T, every[:, 256:384]], axis=1)], axis=0
    ) * (1.0 / rows_total)
    early = []
    for block in range(4):
        row = [every[4 * (8 * block + i) : 4 * (8 * block + i) + 4, 384:416] for i in range(8)]
        row.append(every[32 * block : 32 * block + 4, 416:432])
        row.append(jnp.zeros((4, 112), F32))
        early.append(jnp.concatenate(row, axis=1))
    early = jnp.concatenate(early, axis=0)
    wait_all(group_recv, 6, c_slots)
    total = jnp.concatenate([early[:14], sum_slots_of(c_slots)], axis=0) * (1.0 / rows_total)
    c_one = total[:, :256]
    gram = total[:, 256:272]
    low_row = lax.broadcasted_iota(jnp.int32, (16, 16), 0) >= 14
    low_col = lax.broadcasted_iota(jnp.int32, (16, 16), 1) >= 14
    below = jnp.where(low_row, gram, 0.0)
    size = jnp.where(low_col & ~low_row, below.T, gram)
    c_metric = dot_high(c_one, metric)
    coeffs = 2.0 * c_one - c_metric
    out_coeffs[...] = coeffs
    beyond = 2.0 * c_metric - dot_high(c_metric, metric) - c_one
    gram = size + dot_high(beyond, coeffs, NT) - dot_high(coeffs, c_one, NT)
    factor_t, inverse, pivots = cholesky(gram + gram_eps * eye(16))
    out_factor[...] = factor_t
    out_inverse[...] = inverse
    diagonal = eye(16) > 0.0
    scale = jnp.sum(jnp.where(diagonal, size, 0.0), axis=0, keepdims=True)
    sound = jnp.where(pivots > least_pivot * scale, 1, 0)
    out_sound[0, 0] = jnp.min(sound)
    out_resid[...] = S[...] - dot_three(halves(coeffs), pair(), NT)

    for copy in halos:
        copy.wait_send()
    for place, slots in (
        (0, early_slots), (1, sum_slots), (2, late_slots), (3, sum_mid_slots), (5, sum_all),
        (6, c_slots),
    ):
        wait_all(group_send, place, slots)
    wait_one(group_send, 4, c_other)
    store.wait()


def front(sizes, fields, profiles, earlier, basis_view):
    nx, nz = sizes
    vmem = pl.BlockSpec(memory_space=pltpu.VMEM)
    hbm = pl.BlockSpec(memory_space=pltpu.HBM)
    smem = pl.BlockSpec(memory_space=pltpu.SMEM)
    v = pltpu.VMEM
    return pl.pallas_call(
        functools.partial(front_kernel, sizes),
        out_shape=(
            jax.ShapeDtypeStruct(fields.shape, F32),
            jax.ShapeDtypeStruct((16, 256), F32),
            jax.ShapeDtypeStruct((16, 16), F32),
            jax.ShapeDtypeStruct((16, 16), F32),
            jax.ShapeDtypeStruct((1, 1), jnp.int32),
            jax.ShapeDtypeStruct((16, 1024), F32),
        ),
        in_specs=[hbm] * 6,
        out_specs=(hbm, vmem, vmem, vmem, smem, vmem),
        scratch_shapes=[
            v((5, 20, 32, 256), F32),
            v((5, 18, 32, 256), F32),
            v((5, 16, 16, 256), F32),
            v((2, 2, 5, 16, 256), F32),
            v((2, 2, 5, 32, 256), F32),
            v((4, 8, 256), F32),
            v((4, 8, 256), F32),
            v((128, 256), F32),
            v((2048, 128), F32),
            v((1024, 256), F32),
            v((1024, 256), BF16),
            v((1024, 256), BF16),
            v((64, 256), F32),
            v((32, 2, 256), F32),
            v((32, 2, 256), F32),
            v((32, 2, 128), F32),
            v((32, 2, 128), F32),
            v((16, 1024), F32),
            v((32, 4, 512), F32),
            v((32, 4, 512), F32),
            v((4, 512), F32),
            v((4, 4, 512), F32),
            v((4, 512), F32),
            v((32, 4, 512), F32),
            v((2, 384), F32),
            v((2, 384), F32),
            v((2, 384), F32),
            v((64, 2, 384), F32),
            v((14, 4, 256), F32),
            v((3, 1, 256), F32),
            pltpu.SemaphoreType.DMA((4,)),
            pltpu.SemaphoreType.DMA,
            pltpu.SemaphoreType.DMA,
            pltpu.SemaphoreType.DMA,
            pltpu.SemaphoreType.DMA((8,)),
            pltpu.SemaphoreType.DMA((8,)),
            pltpu.SemaphoreType.DMA((7,)),
            pltpu.SemaphoreType.DMA((7,)),
        ],
        compiler_params=pltpu.CompilerParams(
            collective_id=0, has_side_effects=True, vmem_limit_bytes=62 * 1024 * 1024
        ),
    )(fields, *profiles, earlier, basis_view)


def direct_factor(resid):
    rows_total = 1024.0 * lax.axis_size("gx") * lax.axis_size("gz")
    gram = lax.psum(jnp.dot(resid, resid.T, precision=HIGH), ("gx", "gz")) / rows_total
    identity = jnp.eye(16, dtype=F32)
    factor = jnp.linalg.cholesky(gram + gram_eps * identity)
    return factor.T, jax.scipy.linalg.solve_triangular(factor, identity, lower=True)


def on_device(fields, courant, shear_rate, gradient, earlier, basis_modes, core_matrix):
    sizes = (lax.axis_size("gx"), lax.axis_size("gz"))
    view = view_of(basis_modes)
    profiles = [p.reshape(1, -1) for p in (courant, shear_rate, gradient)]
    finished, coeffs, factor_t, inverse, sound, resid = front(
        sizes, fields, profiles, earlier, view
    )
    factor_t, inverse = lax.cond(
        sound[0, 0] > 0,
        lambda resid, factor_t, inverse: (factor_t, inverse),
        lambda resid, factor_t, inverse: direct_factor(resid),
        resid, factor_t, inverse,
    )
    finished, new_view, new_core = tail(
        core_matrix, coeffs, factor_t, inverse, resid, view, finished
    )
    return (finished, basis_of(new_view), new_core)


def solution(mesh):
    return jax.shard_map(
        on_device,
        mesh=mesh,
        in_specs=(
            P(None, "gx", "gz", None),
            P(),
            P(),
            P(),
            P(None, "gx", "gz"),
            P("gx", None, "gz", None),
            P(),
        ),
        out_specs=(P(None, "gx", "gz", None), P("gx", None, "gz", None), P()),
        check_vma=False,
    )
```

```python
import functools

import jax
import jax.numpy as jnp
from jax import lax
from jax.experimental import pallas as pl
from jax.experimental.pallas import tpu as pltpu
from jax.sharding import PartitionSpec as P

F32, BF16 = jnp.float32, jnp.bfloat16
HIGH = lax.Precision.HIGHEST
SIGN_STEPS = 10
POLAR_STEPS = 3
gram_eps = 1e-06


def halves(values):
    head = values.astype(BF16)
    return head, (values - head.astype(F32)).astype(BF16)


def dot(left, right, over=((1,), (0,))):
    return lax.dot_general(left, right, (over, ((), ())), preferred_element_type=F32)


def dot_three(left, right, over=((1,), (0,))):
    (lh, ll), (rh, rl) = left, right
    return dot(lh, rh, over) + (dot(lh, rl, over) + dot(ll, rh, over))


def dot_high(left, right, over=((1,), (0,))):
    return lax.dot_general(
        left, right, (over, ((), ())), precision=HIGH, preferred_element_type=F32
    )


TN = ((0,), (0,))
NT = ((1,), (1,))


def tripled_left(pair):
    return jnp.concatenate([pair[0], pair[0], pair[1]], axis=0)


def tripled_right(pair):
    return jnp.concatenate([pair[0], pair[1], pair[0]], axis=0)


def eye(count):
    return (
        lax.broadcasted_iota(jnp.int32, (count, count), 0)
        == lax.broadcasted_iota(jnp.int32, (count, count), 1)
    ).astype(F32)


def row_places(z_lanes):
    places = []
    for zc in range(4):
        for x in range(4):
            for y in range(2):
                places.append((zc, x, y))
    return places


def take_basis(view_ref, rows_ref):
    for place, (zc, x, y) in enumerate(row_places(0)):
        for half in range(2):
            rows_ref[pl.ds(place * 32, 32), pl.ds(half * 128, 128)] = view_ref[
                pl.ds(512 * x + 4 * zc + 2 * half + y, 32, stride=16), :
            ]


def give_basis(rows, view_ref, first):
    for step in range(8):
        zc, x, y = row_places(0)[first + step]
        for half in range(2):
            view_ref[pl.ds(512 * x + 4 * zc + 2 * half + y, 32, stride=16), :] = rows[
                step * 32 : step * 32 + 32, half * 128 : half * 128 + 128
            ]


def cholesky(gram):
    count = gram.shape[0]
    row_index = lax.broadcasted_iota(jnp.int32, (count, count), 0)
    col_index = lax.broadcasted_iota(jnp.int32, (count, count), 1)
    left = gram
    right = eye(count)
    pivots = jnp.zeros((1, count), F32)
    for j in range(count):
        pivot = left[j : j + 1, j : j + 1]
        pivots = jnp.where(col_index[:1] == j, pivot, pivots)
        scale = lax.rsqrt(pivot)
        scale = scale * (1.5 - 0.5 * pivot * scale * scale)
        column = left[:, j : j + 1] * scale
        row_l = left[j : j + 1, :] * scale
        row_r = right[j : j + 1, :] * scale
        below = row_index > j
        here = row_index == j
        left = jnp.where(below, left - column * row_l, jnp.where(here, row_l, left))
        right = jnp.where(below, right - column * row_r, jnp.where(here, row_r, right))
    return jnp.where(row_index <= col_index, left, 0.0), right, pivots


def wide_left(v, d):
    modes = v.shape[1]
    vh, vl = halves(v)
    dh, dl = halves(d)
    bh, bl = vh[modes:].astype(F32), vl[modes:].astype(F32)
    turned = jnp.concatenate([bh, bh, bl], axis=0).T.astype(BF16)
    edge = jnp.concatenate([turned, jnp.concatenate([dh, dh, dl], axis=1)], axis=0)
    return vh, vl, edge, jnp.concatenate([vh[modes:], vh[modes:], vl[modes:], edge[modes:]], axis=1)


def product(left, right_v, right_d):
    modes = right_v.shape[1]
    rh, rl = halves(right_v)
    dh, dl = halves(right_d)
    ah, bh = rh[:modes], rh[modes:]
    al, bl = rl[:modes], rl[modes:]
    stacked = jnp.concatenate([ah, al, ah, bh, bl, bh], axis=0)
    low = jnp.concatenate([bh, bl, bh, dh, dl, dh], axis=1)
    vh, vl, edge, wide = left
    thin = jnp.concatenate([bh, bl, bh], axis=0)
    top = (dot(vh[:modes], ah) + dot(vh[:modes], al)) + (dot(vl[:modes], ah) + dot(edge[:modes], thin))
    bottom = dot(wide, jnp.concatenate([ah, al, ah, thin], axis=0))
    return jnp.concatenate([top, bottom], axis=0), dot(wide, low, NT)


def tail_kernel(core_ref, coeffs_ref, factor_ref, inverse_ref, resid_ref, basis_hbm, fields_hbm,
                out_fields, out_basis, out_core, v_ref, d_ref, basis_view, basis_rows, held, sem, field_sem):
    modes = core_ref.shape[0]
    fetch = pltpu.make_async_copy(basis_hbm, basis_view, sem)
    fetch.start()
    taking = pltpu.make_async_copy(fields_hbm, held, field_sem)
    taking.start()
    factor_t = factor_ref[...]
    inverse = inverse_ref[...]
    coeffs = coeffs_ref[...]
    unit = eye(modes)
    unit_d = eye(16)
    parts = halves(coeffs)
    corr_a = core_ref[...] + dot(tripled_left(parts), tripled_right(parts), TN)
    corr_b = dot_high(factor_t, coeffs)
    corr_d = dot_high(factor_t, factor_t, NT)
    shift_a = corr_a - unit
    shift_d = corr_d - unit_d
    total = (
        jnp.sum(shift_a * shift_a, keepdims=True)
        + 2.0 * jnp.sum(corr_b * corr_b, keepdims=True)
        + jnp.sum(shift_d * shift_d, keepdims=True)
    )
    scale = 1.0 / jnp.sqrt(total)
    v_ref[:modes] = shift_a * scale
    v_ref[modes:] = corr_b * scale
    d_ref[...] = shift_d * scale
    unit_v = jnp.concatenate([unit, jnp.zeros((16, modes), F32)], axis=0)

    def sign_step(step, carry):
        v = v_ref[...]
        d = d_ref[...]
        left = wide_left(v, d)
        square_v, square_d = product(left, v, d)
        next_v, next_d = product(
            left, 1.5 * unit_v - 0.5 * square_v, 1.5 * unit_d - 0.5 * square_d
        )
        v_ref[...] = next_v
        d_ref[...] = next_d
        return carry

    lax.fori_loop(0, SIGN_STEPS, sign_step, 0)

    fetch.wait()
    taking.wait()
    passing = pltpu.make_async_copy(held, out_fields, field_sem)
    passing.start()
    take_basis(basis_view, basis_rows)

    rot = 0.5 * (unit_v + v_ref[...])
    pair = halves(rot)
    top = (pair[0][:modes], pair[1][:modes])
    low = (pair[0][modes:], pair[1][modes:])
    inner = dot_three(top, top) + dot(tripled_left(low), tripled_right(low), TN)
    for step in range(POLAR_STEPS):
        factor = 1.5 * unit - 0.5 * inner
        fp = halves(factor)
        rot = dot_three(halves(rot), fp)
        if step < POLAR_STEPS - 1:
            inner = dot_three(halves(dot_three(halves(inner), fp)), fp)
    rp = halves(rot)
    corr_v = jnp.concatenate([corr_a, corr_b], axis=0)
    moved = dot_three(halves(corr_v), (rp[0][:modes], rp[1][:modes]))
    rb48 = tripled_right((rp[0][modes:], rp[1][modes:]))
    moved = moved + jnp.concatenate(
        [
            dot(tripled_left(halves(corr_b)), rb48, TN),
            dot(tripled_left(halves(corr_d)), rb48, TN),
        ],
        axis=0,
    )
    out_core[...] = dot_three(rp, halves(moved), TN)

    mix = dot_high(inverse, rot[modes:], TN)
    mix48 = tripled_right(halves(mix))
    ra = (rp[0][:modes], rp[1][:modes])
    for part in range(4):
        rows = basis_rows[pl.ds(part * 256, 256), :]
        left = tripled_left(halves(resid_ref[:, part * 256 : part * 256 + 256]))
        give_basis(dot_three(halves(rows), ra) + dot(left, mix48, TN), out_basis, part * 8)
    passing.wait()


def tail(core, coeffs, factor_t, inverse, resid, basis_view, fields):
    vmem = pl.BlockSpec(memory_space=pltpu.VMEM)
    hbm = pl.BlockSpec(memory_space=pltpu.HBM)
    return pl.pallas_call(
        tail_kernel,
        out_shape=(
            jax.ShapeDtypeStruct(fields.shape, F32),
            jax.ShapeDtypeStruct((2048, 128), F32),
            jax.ShapeDtypeStruct((256, 256), F32),
        ),
        in_specs=[vmem, vmem, vmem, vmem, vmem, hbm, hbm],
        out_specs=(hbm, vmem, vmem),
        scratch_shapes=[
            pltpu.VMEM((272, 256), F32),
            pltpu.VMEM((16, 16), F32),
            pltpu.VMEM((2048, 128), F32),
            pltpu.VMEM((1024, 256), F32),
            pltpu.VMEM(fields.shape, F32),
            pltpu.SemaphoreType.DMA,
            pltpu.SemaphoreType.DMA,
        ],
        compiler_params=pltpu.CompilerParams(vmem_limit_bytes=60 * 1024 * 1024),
    )(core, coeffs, factor_t, inverse, resid, basis_view, fields)


def view_of(basis):
    return basis.reshape(4, 128, 2, 2, 128).transpose(0, 1, 3, 2, 4).reshape(2048, 128)


def basis_of(view):
    return view.reshape(4, 128, 2, 2, 128).transpose(0, 1, 3, 2, 4).reshape(4, 128, 2, 256)


MESH = pl.DeviceIdType.MESH
press_coef = 0.25
compress_coef = 0.25
visc_coef = 0.05
heat_coef = 0.03
FIELDS = 5
least_pivot = 2.0**-7


def shifted(values):
    width = values.shape[-1]
    lane = lax.broadcasted_iota(jnp.int32, values.shape, 1)
    lower = jnp.where(lane == 0, 0.0, pltpu.roll(values, 1, 1))
    upper = jnp.where(lane == width - 1, 0.0, pltpu.roll(values, width - 1, 1))
    return lower, upper


def update(centre, xl, xu, zl, zu, profiles):
    courant, shear_rate, gradient = profiles
    beside = [shifted(c) for c in centre]
    keep = [1.0 - 6.0 * visc_coef - courant] * 3 + [1.0 - 6.0 * visc_coef]
    keep = keep + [1.0 - 6.0 * heat_coef - courant]
    bring = [visc_coef + courant] * 3 + [visc_coef, heat_coef + courant]
    spread = [visc_coef] * 4 + [heat_coef]
    new = []
    for f in range(FIELDS):
        around = (xu[f] + zl[f]) + (zu[f] + beside[f][0]) + beside[f][1]
        new.append(keep[f] * centre[f] + bring[f] * xl[f] + spread[f] * around)
    half_press = 0.5 * press_coef
    new[0] = new[0] - shear_rate * centre[1] - half_press * (xu[3] - xl[3])
    new[1] = new[1] - half_press * (beside[3][1] - beside[3][0])
    new[2] = new[2] - half_press * (zu[3] - zl[3])
    divergence = (xu[0] - xl[0]) + (beside[1][1] - beside[1][0]) + (zu[2] - zl[2])
    new[3] = new[3] - 0.5 * compress_coef * divergence
    new[4] = new[4] - gradient * centre[1]
    return new


def front_kernel(sizes, fields_hbm, courant_hbm, shear_hbm, gradient_hbm, earlier_hbm, basis_hbm,
                 out_fields, out_coeffs, out_factor, out_inverse, out_sound, out_resid,
                 P, H, F, Zs, Zr, Cs, Cr, V, basis_view, basis_rows, basis_h, basis_l,
                 E2, early_send, early_slots, late_send, late_slots, S,
                 g_send, g_slots, g_mid, g_mid_slots, g_part, g_parts, g_whole, g_all,
                 e_send, e_slots, e_mid, e_mid_slots, e_part, e_all,
                 c_send, c_other, c_mid, c_slots,
                 earlier_ref, profile_rows, small_sem, load_sem, basis_sem, out_sem, halo_send, halo_recv,
                 group_send, group_recv):
    nx, nz = sizes
    gx = lax.axis_index("gx")
    gz = lax.axis_index("gz")
    rows_total = 1024.0 * nx * nz

    barrier = pltpu.get_barrier_semaphore()
    x_beside = (lax.rem(gx + nx - 1, nx), lax.rem(gx + 1, nx))
    z_beside = (lax.rem(gz + nz - 1, nz), lax.rem(gz + 1, nz))

    def greet(where):
        pl.semaphore_signal(barrier, inc=1, device_id=where, device_id_type=MESH)

    def greet_z(d, carry):
        greet((gx, lax.rem(gz + d, nz)))
        return carry

    load = pltpu.make_async_copy(fields_hbm, P.at[:, 2:18, 8:24, :], load_sem)
    load.start()
    fetch = pltpu.make_async_copy(basis_hbm, basis_view, basis_sem)
    fetch.start()
    small = [
        pltpu.make_async_copy(earlier_hbm, earlier_ref, small_sem.at[0]),
        pltpu.make_async_copy(courant_hbm, profile_rows.at[0], small_sem.at[1]),
        pltpu.make_async_copy(shear_hbm, profile_rows.at[1], small_sem.at[2]),
        pltpu.make_async_copy(gradient_hbm, profile_rows.at[2], small_sem.at[3]),
    ]
    for copy in small:
        copy.start()
    for d in range(1, nx):
        greet((lax.rem(gx + d, nx), gz))
    for xs in range(2):
        for zs in range(2):
            greet((x_beside[xs], z_beside[zs]))
    for d in range(1, nx):
        greet((lax.rem(gx + d, nx), gz + 1 - 2 * lax.rem(gz, 2)))
    lax.fori_loop(1, nz, greet_z, 0)

    for copy in small:
        copy.wait()
    E2[...] = jnp.zeros_like(E2)
    for m in range(14):
        for x in range(4):
            E2[x * 16 + m : x * 16 + m + 1, :] = earlier_ref[m, x : x + 1, :]
    turned = E2[...].T
    turned = jnp.concatenate([turned[64 * z : 64 * z + 64] for z in range(4)], axis=1)
    for i in range(32):
        early_send[i] = turned[2 * i : 2 * i + 2]
    load.wait()
    pl.semaphore_wait(barrier, nz - 1 + 2 * (nx - 1) + 4)

    halos = []

    def send_halo(source, target, where):
        place = len(halos)
        copy = pltpu.make_async_remote_copy(
            src_ref=source, dst_ref=target, send_sem=halo_send.at[place],
            recv_sem=halo_recv.at[place], device_id=where, device_id_type=MESH,
        )
        copy.start()
        halos.append(copy)

    for side in range(2):
        send_halo(
            P.at[:, 2 + 14 * side : 4 + 14 * side, 8:24, :],
            P.at[:, 18 - 18 * side : 20 - 18 * side, 8:24, :],
            (x_beside[side], gz),
        )

    for side in range(2):
        for layer in range(2):
            z = 8 + 14 * side + layer
            for f in range(FIELDS):
                for half in range(2):
                    lanes = pl.ds(128 * half, 128)
                    Zs[side, layer, f, 8:24, lanes] = P[f, 2:18, z, lanes]
    for xs in range(2):
        for zs in range(2):
            for f in range(FIELDS):
                Cs[2 * xs + zs, f : f + 1, :] = P[f, 2 + 15 * xs, 8 + 15 * zs : 9 + 15 * zs, :]

    for side in range(2):
        send_halo(Zs.at[side, :, :, 8:24, :], Zr.at[1 - side, :, :, 8:24, :], (gx, z_beside[side]))
    for xs in range(2):
        for zs in range(2):
            send_halo(
                Cs.at[2 * xs + zs], Cr.at[2 * (1 - xs) + 1 - zs], (x_beside[xs], z_beside[zs])
            )

    def spread_z(place, source, slots):
        def body(d, carry):
            peer = lax.rem(gz + d, nz)
            pltpu.make_async_remote_copy(
                src_ref=source(peer), dst_ref=slots.at[gz], send_sem=group_send.at[place],
                recv_sem=group_recv.at[place], device_id=(gx, peer), device_id_type=MESH,
            ).start()
            return carry

        lax.fori_loop(1, nz, body, 0)

    yz = gz // 2
    places = nz // 2
    along = (lax.rem(gz, 2) * (nx // 2) + gx // 2) * 2 + lax.rem(gx, 2)
    line = 2 * nx

    def spread_yz(place, source, slots):
        def body(d, carry):
            peer = lax.rem(yz + d, places)
            pltpu.make_async_remote_copy(
                src_ref=source(peer), dst_ref=slots.at[yz], send_sem=group_send.at[place],
                recv_sem=group_recv.at[place], device_id=(gx, 2 * peer + lax.rem(gz, 2)),
                device_id_type=MESH,
            ).start()
            return carry

        lax.fori_loop(1, places, body, 0)

    def spread_line(place, source, slots):
        def body(d, carry):
            peer = lax.rem(along + d, line)
            where = (lax.rem(peer, nx), 2 * yz + peer // nx)
            pltpu.make_async_remote_copy(
                src_ref=source(peer), dst_ref=slots.at[along], send_sem=group_send.at[place],
                recv_sem=group_recv.at[place], device_id=where, device_id_type=MESH,
            ).start()
            return carry

        lax.fori_loop(1, line, body, 0)

    core = lax.rem(gx, 2)
    chip = (gx // 2) * nz + gz
    chips = (nx // 2) * nz

    def send_core(place, source, target):
        pltpu.make_async_remote_copy(
            src_ref=source, dst_ref=target, send_sem=group_send.at[place],
            recv_sem=group_recv.at[place], device_id=(gx + 1 - 2 * core, gz), device_id_type=MESH,
        ).start()

    def spread_chips(place, source, slots):
        def body(d, carry):
            peer = lax.rem(chip + d, chips)
            where = (2 * (peer // nz) + core, lax.rem(peer, nz))
            pltpu.make_async_remote_copy(
                src_ref=source, dst_ref=slots.at[chip], send_sem=group_send.at[place],
                recv_sem=group_recv.at[place], device_id=where, device_id_type=MESH,
            ).start()
            return carry

        lax.fori_loop(1, chips, body, 0)

    def wait_one(sems, place, part):
        pltpu.make_async_copy(part, part, sems.at[place]).wait()

    def sum_slots_of(slots):
        terms = [slots[j] for j in range(slots.shape[0])]
        while len(terms) > 1:
            terms = [a + b for a, b in zip(terms[::2], terms[1::2])] + terms[len(terms) & ~1 :]
        return terms[0]

    def wait_all(sems, place, slots):
        some = slots.at[pl.ds(0, slots.shape[0] - 1)]
        pltpu.make_async_copy(some, some, sems.at[place]).wait()

    spread_z(0, lambda peer: early_send.at[peer], early_slots)
    early_slots[gz] = early_send[gz]

    fetch.wait()
    take_basis(basis_view, basis_rows)
    rows = basis_rows[...]
    head = rows.astype(BF16)
    basis_h[...] = head
    basis_l[...] = (rows - head.astype(F32)).astype(BF16)

    def pair():
        return basis_h[...], basis_l[...]

    inner = dot_three(pair(), pair(), TN)
    for i in range(16):
        g_send[i, :, :256] = inner[8 * i : 8 * i + 8]
        g_send[i, :, 256:] = inner[128 + 8 * i : 136 + 8 * i, 128:]
    spread_yz(1, lambda peer: g_send.at[peer], g_slots)
    g_slots[yz] = g_send[yz]

    profiles = [profile_rows[k] for k in range(3)]

    def first(i, carry):
        centre = [P[f, i + 1, 8:24, :] for f in range(FIELDS)]
        xl = [P[f, i, 8:24, :] for f in range(FIELDS)]
        xu = [P[f, i + 2, 8:24, :] for f in range(FIELDS)]
        zl = [P[f, i + 1, 7:23, :] for f in range(FIELDS)]
        zu = [P[f, i + 1, 9:25, :] for f in range(FIELDS)]
        new = update(centre, xl, xu, zl, zu, profiles)
        for f in range(FIELDS):
            H[f, i, 8:24, :] = new[f]
        return carry

    lax.fori_loop(2, 16, first, 0)

    wait_all(group_recv, 0, early_slots)
    got = jnp.concatenate([early_slots[:, 0, :], early_slots[:, 1, :]], axis=0).T
    for zx in range(16):
        S[:, zx * 64 : zx * 64 + 64] = got[zx * 16 : zx * 16 + 16]
    snaps = halves(S[...])
    c_early = dot_three(snaps, pair())
    k_early = dot_three(snaps, snaps, NT)
    early = jnp.concatenate([c_early, k_early, jnp.zeros((16, 112), F32)], axis=1)
    for m in range(16):
        e_send[m] = early[m : m + 1]
    spread_yz(8, lambda peer: e_send.at[peer], e_slots)
    e_slots[yz] = e_send[yz]

    for copy in halos:
        copy.wait_recv()
    for f in range(FIELDS):
        for xs in range(2):
            row = 7 + 17 * xs
            x = 1 + 17 * xs
            for zs in range(2):
                corner = Cr[2 * xs + zs, f : f + 1, :]
                Zr[zs, 1 - zs, f, row : row + 1, :] = corner
                P[f, x, 7 + 17 * zs : 8 + 17 * zs, :] = corner
                Zs[zs, zs, f, row : row + 1, :] = P[f, x, 8 + 15 * zs : 9 + 15 * zs, :]
    lax.fori_loop(0, 4, lambda k, carry: first(k + 14 * (k // 2), carry), 0)
    for side in range(2):
        layers = [Zr.at[side, side], Zr.at[side, 1 - side], Zs.at[side, side], Zs.at[side, 1 - side]]
        for edge in range(2):
            outer, mid, inside = layers[edge : edge + 3]
            centre = [mid[f, 8:24, :] for f in range(FIELDS)]
            xl = [mid[f, 7:23, :] for f in range(FIELDS)]
            xu = [mid[f, 9:25, :] for f in range(FIELDS)]
            out = [outer[f, 8:24, :] for f in range(FIELDS)]
            within = [inside[f, 8:24, :] for f in range(FIELDS)]
            zl, zu = (out, within) if side == 0 else (within, out)
            new = update(centre, xl, xu, zl, zu, profiles)
            z = 7 + edge if side == 0 else 24 - edge
            for f in range(FIELDS):
                H[f, 1:17, z, :] = new[f]

    wait_all(group_recv, 1, g_slots)
    total = sum_slots_of(g_slots)
    for r in range(8):
        g_mid[r] = total[r : r + 1]
    spread_line(3, lambda peer: g_mid.at[peer], g_mid_slots)
    g_mid_slots[along] = g_mid[along]

    def second(i, carry):
        centre = [H[f, i + 1, 8:24, :] for f in range(FIELDS)]
        xl = [H[f, i, 8:24, :] for f in range(FIELDS)]
        xu = [H[f, i + 2, 8:24, :] for f in range(FIELDS)]
        zl = [H[f, i + 1, 7:23, :] for f in range(FIELDS)]
        zu = [H[f, i + 1, 9:25, :] for f in range(FIELDS)]
        new = update(centre, xl, xu, zl, zu, profiles)
        for f in range(FIELDS):
            F[f, i, :, :] = new[f]
        return carry

    lax.fori_loop(0, 16, second, 0)
    store = pltpu.make_async_copy(F, out_fields, out_sem)
    store.start()

    for xg in range(4):
        V[16 * xg : 16 * xg + 16, :] = (H[0, 4 * xg + 1, 8:24, :] + H[0, 4 * xg + 2, 8:24, :]) + (
            H[0, 4 * xg + 3, 8:24, :] + H[0, 4 * xg + 4, 8:24, :]
        )
        V[64 + 16 * xg : 80 + 16 * xg, :] = (F[0, 4 * xg] + F[0, 4 * xg + 1]) + (
            F[0, 4 * xg + 2] + F[0, 4 * xg + 3]
        )
    to = lax.broadcasted_iota(jnp.int32, (128, 128), 0)
    of = lax.broadcasted_iota(jnp.int32, (128, 128), 1)
    wanted = ((lax.rem(of, 16) // 4) * 4 + lax.rem(of, 64) // 16) * 8 + 6 + of // 64
    place_to = (to == wanted).astype(BF16)
    sums = halves(V[...])
    gathered = dot(
        jnp.concatenate([place_to, place_to], axis=1), jnp.concatenate(sums, axis=0)
    )
    block = (
        lax.broadcasted_iota(jnp.int32, (64, 256), 0)
        == lax.broadcasted_iota(jnp.int32, (64, 256), 1) // 4
    ).astype(BF16) * BF16(1.0 / 64.0)
    coarse = dot(
        jnp.concatenate([block, block], axis=1), jnp.concatenate(halves(gathered), axis=1), NT
    )
    for i in range(32):
        late_send[i] = coarse[2 * i : 2 * i + 2]
    spread_z(2, lambda peer: late_send.at[peer], late_slots)
    late_slots[gz] = late_send[gz]

    wait_all(group_recv, 8, e_slots)
    e_mid[...] = sum_slots_of(e_slots)
    spread_line(9, lambda peer: e_mid, e_mid_slots)
    e_mid_slots[along] = e_mid[...]

    wait_all(group_recv, 3, g_mid_slots)
    g_part[...] = sum_slots_of(g_mid_slots)
    spread_line(5, lambda peer: g_part, g_parts)
    g_parts[along] = g_part[...]

    wait_all(group_recv, 5, g_parts)
    for r in range(8):
        g_whole[r : r + 1, :] = g_parts[r]
    spread_yz(7, lambda peer: g_whole, g_all)
    g_all[yz] = g_whole[...]

    wait_all(group_recv, 9, e_mid_slots)
    e_part[...] = sum_slots_of(e_mid_slots)
    spread_yz(10, lambda peer: e_part, e_all)
    e_all[yz] = e_part[...]

    wait_all(group_recv, 2, late_slots)
    got = jnp.concatenate([late_slots[:, 0, :], late_slots[:, 1, :]], axis=0).T
    for zx in range(16):
        S[8:16, zx * 64 : zx * 64 + 64] = S[8:16, zx * 64 : zx * 64 + 64] + got[zx * 8 : zx * 8 + 8]
    low = S[8:16, :]
    low = jnp.where(lax.broadcasted_iota(jnp.int32, low.shape, 0) >= 6, low, 0.0)
    late = halves(jnp.concatenate([jnp.zeros_like(low), low], axis=0))
    both = dot(jnp.concatenate(late, axis=0), basis_h[...])
    c_late = (both[:16] + both[16:] + dot(late[0], basis_l[...]))[14:16]
    k_late = dot_three(late, halves(S[...]), NT)[14:16]
    late = jnp.concatenate([c_late, k_late, jnp.zeros((2, 112), F32)], axis=1)
    c_send[...] = late
    send_core(4, c_send, c_other)
    wait_one(group_recv, 4, c_other)
    both = late + c_other[...]
    c_mid[...] = both
    spread_chips(6, c_mid, c_slots)
    c_slots[chip] = both

    wait_all(group_recv, 7, g_all)
    every = g_all[...].reshape(128, 384)
    cross = every[:, 128:256]
    metric = jnp.concatenate(
        [every[:, :256], jnp.concatenate([cross.T, every[:, 256:]], axis=1)], axis=0
    ) * (1.0 / rows_total)
    unit = eye(256)
    removed = 4.0 * unit - 6.0 * metric + dot_high(dot_high(metric, metric), 4.0 * unit - metric)
    wait_all(group_recv, 10, e_all)
    early = e_all[...].reshape(16, 384)
    wait_all(group_recv, 6, c_slots)
    total = jnp.concatenate([early[:14], sum_slots_of(c_slots)], axis=0) * (1.0 / rows_total)
    c_one = total[:, :256]
    gram = total[:, 256:272]
    low_row = lax.broadcasted_iota(jnp.int32, (16, 16), 0) >= 14
    low_col = lax.broadcasted_iota(jnp.int32, (16, 16), 1) >= 14
    below = jnp.where(low_row, gram, 0.0)
    size = jnp.where(low_col & ~low_row, below.T, gram)
    gram = size - dot_high(dot_high(c_one, removed), c_one, NT)
    coeffs = 2.0 * c_one - dot_high(c_one, metric)
    out_coeffs[...] = coeffs
    factor_t, inverse, pivots = cholesky(gram + gram_eps * eye(16))
    out_factor[...] = factor_t
    out_inverse[...] = inverse
    diagonal = eye(16) > 0.0
    scale = jnp.sum(jnp.where(diagonal, size, 0.0), axis=0, keepdims=True)
    sound = jnp.where(pivots > least_pivot * scale, 1, 0)
    out_sound[0, 0] = jnp.min(sound)
    out_resid[...] = S[...] - dot_three(halves(coeffs), pair(), NT)

    for copy in halos:
        copy.wait_send()
    for place, slots in (
        (0, early_slots), (1, g_slots), (2, late_slots), (3, g_mid_slots), (5, g_parts),
        (6, c_slots), (7, g_all), (8, e_slots), (9, e_mid_slots), (10, e_all),
    ):
        wait_all(group_send, place, slots)
    wait_one(group_send, 4, c_other)
    store.wait()


def front(sizes, fields, profiles, earlier, basis_view):
    nx, nz = sizes
    vmem = pl.BlockSpec(memory_space=pltpu.VMEM)
    hbm = pl.BlockSpec(memory_space=pltpu.HBM)
    smem = pl.BlockSpec(memory_space=pltpu.SMEM)
    v = pltpu.VMEM
    return pl.pallas_call(
        functools.partial(front_kernel, sizes),
        out_shape=(
            jax.ShapeDtypeStruct(fields.shape, F32),
            jax.ShapeDtypeStruct((16, 256), F32),
            jax.ShapeDtypeStruct((16, 16), F32),
            jax.ShapeDtypeStruct((16, 16), F32),
            jax.ShapeDtypeStruct((1, 1), jnp.int32),
            jax.ShapeDtypeStruct((16, 1024), F32),
        ),
        in_specs=[hbm] * 6,
        out_specs=(hbm, vmem, vmem, vmem, smem, vmem),
        scratch_shapes=[
            v((5, 20, 32, 256), F32),
            v((5, 18, 32, 256), F32),
            v((5, 16, 16, 256), F32),
            v((2, 2, 5, 32, 256), F32),
            v((2, 2, 5, 32, 256), F32),
            v((4, 8, 256), F32),
            v((4, 8, 256), F32),
            v((128, 256), F32),
            v((2048, 128), F32),
            v((1024, 256), F32),
            v((1024, 256), BF16),
            v((1024, 256), BF16),
            v((64, 256), F32),
            v((32, 2, 256), F32),
            v((32, 2, 256), F32),
            v((32, 2, 128), F32),
            v((32, 2, 128), F32),
            v((16, 1024), F32),
            v((16, 8, 384), F32),
            v((16, 8, 384), F32),
            v((8, 1, 384), F32),
            v((8, 1, 384), F32),
            v((1, 384), F32),
            v((8, 1, 384), F32),
            v((8, 384), F32),
            v((16, 8, 384), F32),
            v((16, 1, 384), F32),
            v((16, 1, 384), F32),
            v((1, 384), F32),
            v((8, 1, 384), F32),
            v((1, 384), F32),
            v((16, 1, 384), F32),
            v((2, 384), F32),
            v((2, 384), F32),
            v((2, 384), F32),
            v((64, 2, 384), F32),
            v((14, 4, 256), F32),
            v((3, 1, 256), F32),
            pltpu.SemaphoreType.DMA((4,)),
            pltpu.SemaphoreType.DMA,
            pltpu.SemaphoreType.DMA,
            pltpu.SemaphoreType.DMA,
            pltpu.SemaphoreType.DMA((8,)),
            pltpu.SemaphoreType.DMA((8,)),
            pltpu.SemaphoreType.DMA((11,)),
            pltpu.SemaphoreType.DMA((11,)),
        ],
        compiler_params=pltpu.CompilerParams(
            collective_id=0, has_side_effects=True, vmem_limit_bytes=62 * 1024 * 1024
        ),
    )(fields, *profiles, earlier, basis_view)


def direct_factor(resid):
    rows_total = 1024.0 * lax.axis_size("gx") * lax.axis_size("gz")
    gram = lax.psum(jnp.dot(resid, resid.T, precision=HIGH), ("gx", "gz")) / rows_total
    identity = jnp.eye(16, dtype=F32)
    factor = jnp.linalg.cholesky(gram + gram_eps * identity)
    return factor.T, jax.scipy.linalg.solve_triangular(factor, identity, lower=True)


def on_device(fields, courant, shear_rate, gradient, earlier, basis_modes, core_matrix):
    sizes = (lax.axis_size("gx"), lax.axis_size("gz"))
    view = view_of(basis_modes)
    profiles = [p.reshape(1, -1) for p in (courant, shear_rate, gradient)]
    finished, coeffs, factor_t, inverse, sound, resid = front(
        sizes, fields, profiles, earlier, view
    )
    factor_t, inverse = lax.cond(
        sound[0, 0] > 0,
        lambda resid, factor_t, inverse: (factor_t, inverse),
        lambda resid, factor_t, inverse: direct_factor(resid),
        resid, factor_t, inverse,
    )
    finished, new_view, new_core = tail(
        core_matrix, coeffs, factor_t, inverse, resid, view, finished
    )
    return (finished, basis_of(new_view), new_core)


def solution(mesh):
    return jax.shard_map(
        on_device,
        mesh=mesh,
        in_specs=(
            P(None, "gx", "gz", None),
            P(),
            P(),
            P(),
            P(None, "gx", "gz"),
            P("gx", None, "gz", None),
            P(),
        ),
        out_specs=(P(None, "gx", "gz", None), P("gx", None, "gz", None), P()),
        check_vma=False,
    )
```

```python
import functools

import jax
import jax.numpy as jnp
from jax import lax
from jax.experimental import pallas as pl
from jax.experimental.pallas import tpu as pltpu
from jax.sharding import PartitionSpec as P

F32, BF16 = jnp.float32, jnp.bfloat16
HIGH = lax.Precision.HIGHEST
SIGN_STEPS = 10
POLAR_STEPS = 3
gram_eps = 1e-06


def halves(values):
    head = values.astype(BF16)
    return head, (values - head.astype(F32)).astype(BF16)


def dot(left, right, over=((1,), (0,))):
    return lax.dot_general(left, right, (over, ((), ())), preferred_element_type=F32)


def dot_three(left, right, over=((1,), (0,))):
    (lh, ll), (rh, rl) = left, right
    return dot(lh, rh, over) + (dot(lh, rl, over) + dot(ll, rh, over))


def dot_high(left, right, over=((1,), (0,))):
    return lax.dot_general(
        left, right, (over, ((), ())), precision=HIGH, preferred_element_type=F32
    )


TN = ((0,), (0,))
NT = ((1,), (1,))


def tripled_left(pair):
    return jnp.concatenate([pair[0], pair[0], pair[1]], axis=0)


def tripled_right(pair):
    return jnp.concatenate([pair[0], pair[1], pair[0]], axis=0)


def eye(count):
    return (
        lax.broadcasted_iota(jnp.int32, (count, count), 0)
        == lax.broadcasted_iota(jnp.int32, (count, count), 1)
    ).astype(F32)


def row_places(z_lanes):
    places = []
    for zc in range(4):
        for x in range(4):
            for y in range(2):
                places.append((zc, x, y))
    return places


def take_basis(view_ref, rows_ref):
    for place, (zc, x, y) in enumerate(row_places(0)):
        for half in range(2):
            rows_ref[pl.ds(place * 32, 32), pl.ds(half * 128, 128)] = view_ref[
                pl.ds(512 * x + 4 * zc + 2 * half + y, 32, stride=16), :
            ]


def give_basis(rows, view_ref, first):
    for step in range(8):
        zc, x, y = row_places(0)[first + step]
        for half in range(2):
            view_ref[pl.ds(512 * x + 4 * zc + 2 * half + y, 32, stride=16), :] = rows[
                step * 32 : step * 32 + 32, half * 128 : half * 128 + 128
            ]


def cholesky(gram):
    count = gram.shape[0]
    row_index = lax.broadcasted_iota(jnp.int32, (count, count), 0)
    col_index = lax.broadcasted_iota(jnp.int32, (count, count), 1)
    left = gram
    right = eye(count)
    pivots = jnp.zeros((1, count), F32)
    for j in range(count):
        pivot = left[j : j + 1, j : j + 1]
        pivots = jnp.where(col_index[:1] == j, pivot, pivots)
        scale = lax.rsqrt(pivot)
        scale = scale * (1.5 - 0.5 * pivot * scale * scale)
        column = left[:, j : j + 1] * scale
        row_l = left[j : j + 1, :] * scale
        row_r = right[j : j + 1, :] * scale
        below = row_index > j
        here = row_index == j
        left = jnp.where(below, left - column * row_l, jnp.where(here, row_l, left))
        right = jnp.where(below, right - column * row_r, jnp.where(here, row_r, right))
    return jnp.where(row_index <= col_index, left, 0.0), right, pivots


def wide_left(v, d):
    modes = v.shape[1]
    vh, vl = halves(v)
    dh, dl = halves(d)
    bh, bl = vh[modes:].astype(F32), vl[modes:].astype(F32)
    turned = jnp.concatenate([bh, bh, bl], axis=0).T.astype(BF16)
    edge = jnp.concatenate([turned, jnp.concatenate([dh, dh, dl], axis=1)], axis=0)
    return vh, vl, edge, jnp.concatenate([vh[modes:], vh[modes:], vl[modes:], edge[modes:]], axis=1)


def product(left, right_v, right_d):
    modes = right_v.shape[1]
    rh, rl = halves(right_v)
    dh, dl = halves(right_d)
    ah, bh = rh[:modes], rh[modes:]
    al, bl = rl[:modes], rl[modes:]
    stacked = jnp.concatenate([ah, al, ah, bh, bl, bh], axis=0)
    low = jnp.concatenate([bh, bl, bh, dh, dl, dh], axis=1)
    vh, vl, edge, wide = left
    thin = jnp.concatenate([bh, bl, bh], axis=0)
    top = (dot(vh[:modes], ah) + dot(vh[:modes], al)) + (dot(vl[:modes], ah) + dot(edge[:modes], thin))
    bottom = dot(wide, jnp.concatenate([ah, al, ah, thin], axis=0))
    return jnp.concatenate([top, bottom], axis=0), dot(wide, low, NT)


def tail_kernel(core_ref, coeffs_ref, factor_ref, inverse_ref, resid_ref, basis_hbm, fields_hbm,
                out_fields, out_basis, out_core, v_ref, d_ref, basis_view, basis_rows, held, sem, field_sem):
    modes = core_ref.shape[0]
    fetch = pltpu.make_async_copy(basis_hbm, basis_view, sem)
    fetch.start()
    taking = pltpu.make_async_copy(fields_hbm, held, field_sem)
    taking.start()
    factor_t = factor_ref[...]
    inverse = inverse_ref[...]
    coeffs = coeffs_ref[...]
    unit = eye(modes)
    unit_d = eye(16)
    parts = halves(coeffs)
    corr_a = core_ref[...] + dot(tripled_left(parts), tripled_right(parts), TN)
    corr_b = dot_high(factor_t, coeffs)
    corr_d = dot_high(factor_t, factor_t, NT)
    shift_a = corr_a - unit
    shift_d = corr_d - unit_d
    total = (
        jnp.sum(shift_a * shift_a, keepdims=True)
        + 2.0 * jnp.sum(corr_b * corr_b, keepdims=True)
        + jnp.sum(shift_d * shift_d, keepdims=True)
    )
    scale = 1.0 / jnp.sqrt(total)
    v_ref[:modes] = shift_a * scale
    v_ref[modes:] = corr_b * scale
    d_ref[...] = shift_d * scale
    unit_v = jnp.concatenate([unit, jnp.zeros((16, modes), F32)], axis=0)

    def sign_step(step, carry):
        v = v_ref[...]
        d = d_ref[...]
        left = wide_left(v, d)
        square_v, square_d = product(left, v, d)
        next_v, next_d = product(
            left, 1.5 * unit_v - 0.5 * square_v, 1.5 * unit_d - 0.5 * square_d
        )
        v_ref[...] = next_v
        d_ref[...] = next_d
        return carry

    lax.fori_loop(0, SIGN_STEPS, sign_step, 0)

    fetch.wait()
    taking.wait()
    passing = pltpu.make_async_copy(held, out_fields, field_sem)
    passing.start()
    take_basis(basis_view, basis_rows)

    rot = 0.5 * (unit_v + v_ref[...])
    pair = halves(rot)
    top = (pair[0][:modes], pair[1][:modes])
    low = (pair[0][modes:], pair[1][modes:])
    inner = dot_three(top, top) + dot(tripled_left(low), tripled_right(low), TN)
    for step in range(POLAR_STEPS):
        factor = 1.5 * unit - 0.5 * inner
        fp = halves(factor)
        rot = dot_three(halves(rot), fp)
        if step < POLAR_STEPS - 1:
            inner = dot_three(halves(dot_three(halves(inner), fp)), fp)
    rp = halves(rot)
    corr_v = jnp.concatenate([corr_a, corr_b], axis=0)
    moved = dot_three(halves(corr_v), (rp[0][:modes], rp[1][:modes]))
    rb48 = tripled_right((rp[0][modes:], rp[1][modes:]))
    moved = moved + jnp.concatenate(
        [
            dot(tripled_left(halves(corr_b)), rb48, TN),
            dot(tripled_left(halves(corr_d)), rb48, TN),
        ],
        axis=0,
    )
    out_core[...] = dot_three(rp, halves(moved), TN)

    mix = dot_high(inverse, rot[modes:], TN)
    mix48 = tripled_right(halves(mix))
    ra = (rp[0][:modes], rp[1][:modes])
    for part in range(4):
        rows = basis_rows[pl.ds(part * 256, 256), :]
        left = tripled_left(halves(resid_ref[:, part * 256 : part * 256 + 256]))
        give_basis(dot_three(halves(rows), ra) + dot(left, mix48, TN), out_basis, part * 8)
    passing.wait()


def tail(core, coeffs, factor_t, inverse, resid, basis_view, fields):
    vmem = pl.BlockSpec(memory_space=pltpu.VMEM)
    hbm = pl.BlockSpec(memory_space=pltpu.HBM)
    return pl.pallas_call(
        tail_kernel,
        out_shape=(
            jax.ShapeDtypeStruct(fields.shape, F32),
            jax.ShapeDtypeStruct((2048, 128), F32),
            jax.ShapeDtypeStruct((256, 256), F32),
        ),
        in_specs=[vmem, vmem, vmem, vmem, vmem, hbm, hbm],
        out_specs=(hbm, vmem, vmem),
        scratch_shapes=[
            pltpu.VMEM((272, 256), F32),
            pltpu.VMEM((16, 16), F32),
            pltpu.VMEM((2048, 128), F32),
            pltpu.VMEM((1024, 256), F32),
            pltpu.VMEM(fields.shape, F32),
            pltpu.SemaphoreType.DMA,
            pltpu.SemaphoreType.DMA,
        ],
        compiler_params=pltpu.CompilerParams(vmem_limit_bytes=60 * 1024 * 1024),
    )(core, coeffs, factor_t, inverse, resid, basis_view, fields)


def view_of(basis):
    return basis.reshape(4, 128, 2, 2, 128).transpose(0, 1, 3, 2, 4).reshape(2048, 128)


def basis_of(view):
    return view.reshape(4, 128, 2, 2, 128).transpose(0, 1, 3, 2, 4).reshape(4, 128, 2, 256)


MESH = pl.DeviceIdType.MESH
press_coef = 0.25
compress_coef = 0.25
visc_coef = 0.05
heat_coef = 0.03
FIELDS = 5
least_pivot = 2.0**-7


def shifted(values):
    width = values.shape[-1]
    lane = lax.broadcasted_iota(jnp.int32, values.shape, 1)
    lower = jnp.where(lane == 0, 0.0, pltpu.roll(values, 1, 1))
    upper = jnp.where(lane == width - 1, 0.0, pltpu.roll(values, width - 1, 1))
    return lower, upper


def update(centre, xl, xu, zl, zu, profiles):
    courant, shear_rate, gradient = profiles
    beside = [shifted(c) for c in centre]
    keep = [1.0 - 6.0 * visc_coef - courant] * 3 + [1.0 - 6.0 * visc_coef]
    keep = keep + [1.0 - 6.0 * heat_coef - courant]
    bring = [visc_coef + courant] * 3 + [visc_coef, heat_coef + courant]
    spread = [visc_coef] * 4 + [heat_coef]
    new = []
    for f in range(FIELDS):
        around = (xu[f] + zl[f]) + (zu[f] + beside[f][0]) + beside[f][1]
        new.append(keep[f] * centre[f] + bring[f] * xl[f] + spread[f] * around)
    half_press = 0.5 * press_coef
    new[0] = new[0] - shear_rate * centre[1] - half_press * (xu[3] - xl[3])
    new[1] = new[1] - half_press * (beside[3][1] - beside[3][0])
    new[2] = new[2] - half_press * (zu[3] - zl[3])
    divergence = (xu[0] - xl[0]) + (beside[1][1] - beside[1][0]) + (zu[2] - zl[2])
    new[3] = new[3] - 0.5 * compress_coef * divergence
    new[4] = new[4] - gradient * centre[1]
    return new


def front_kernel(sizes, fields_hbm, courant_hbm, shear_hbm, gradient_hbm, earlier_hbm, basis_hbm,
                 out_fields, out_coeffs, out_factor, out_inverse, out_sound, out_resid,
                 P, H, F, Zs, Zr, Cs, Cr, V, basis_view, basis_rows, basis_h, basis_l,
                 E2, early_send, early_slots, late_send, late_slots, S,
                 g_send, g_slots, g_mid, g_mid_slots, g_part, g_parts, g_whole, g_all,
                 e_send, e_slots, e_mid, e_mid_slots, e_part, e_all,
                 c_send, c_other, c_mid, c_slots,
                 earlier_ref, profile_rows, small_sem, load_sem, basis_sem, out_sem, halo_send, halo_recv,
                 group_send, group_recv):
    nx, nz = sizes
    gx = lax.axis_index("gx")
    gz = lax.axis_index("gz")
    rows_total = 1024.0 * nx * nz

    barrier = pltpu.get_barrier_semaphore()
    x_beside = (lax.rem(gx + nx - 1, nx), lax.rem(gx + 1, nx))
    z_beside = (lax.rem(gz + nz - 1, nz), lax.rem(gz + 1, nz))

    def greet(where):
        pl.semaphore_signal(barrier, inc=1, device_id=where, device_id_type=MESH)

    def greet_z(d, carry):
        greet((gx, lax.rem(gz + d, nz)))
        return carry

    load = pltpu.make_async_copy(fields_hbm, P.at[:, 2:18, 8:24, :], load_sem)
    load.start()
    fetch = pltpu.make_async_copy(basis_hbm, basis_view, basis_sem)
    fetch.start()
    small = [
        pltpu.make_async_copy(earlier_hbm, earlier_ref, small_sem.at[0]),
        pltpu.make_async_copy(courant_hbm, profile_rows.at[0], small_sem.at[1]),
        pltpu.make_async_copy(shear_hbm, profile_rows.at[1], small_sem.at[2]),
        pltpu.make_async_copy(gradient_hbm, profile_rows.at[2], small_sem.at[3]),
    ]
    for copy in small:
        copy.start()
    for d in range(1, nx):
        greet((lax.rem(gx + d, nx), gz))
    for xs in range(2):
        for zs in range(2):
            greet((x_beside[xs], z_beside[zs]))
    for d in range(1, nx):
        greet((lax.rem(gx + d, nx), gz + 1 - 2 * lax.rem(gz, 2)))
    lax.fori_loop(1, nz, greet_z, 0)

    for copy in small:
        copy.wait()
    E2[...] = jnp.zeros_like(E2)
    for m in range(14):
        for x in range(4):
            E2[x * 16 + m : x * 16 + m + 1, :] = earlier_ref[m, x : x + 1, :]
    turned = E2[...].T
    turned = jnp.concatenate([turned[64 * z : 64 * z + 64] for z in range(4)], axis=1)
    for i in range(32):
        early_send[i] = turned[2 * i : 2 * i + 2]
    pl.semaphore_wait(barrier, nz - 1 + 2 * (nx - 1) + 4)

    def spread_z(place, source, slots):
        def body(d, carry):
            peer = lax.rem(gz + d, nz)
            pltpu.make_async_remote_copy(
                src_ref=source(peer), dst_ref=slots.at[gz], send_sem=group_send.at[place],
                recv_sem=group_recv.at[place], device_id=(gx, peer), device_id_type=MESH,
            ).start()
            return carry

        lax.fori_loop(1, nz, body, 0)

    spread_z(0, lambda peer: early_send.at[peer], early_slots)
    early_slots[gz] = early_send[gz]

    load.wait()

    halos = []

    def send_halo(source, target, where):
        place = len(halos)
        copy = pltpu.make_async_remote_copy(
            src_ref=source, dst_ref=target, send_sem=halo_send.at[place],
            recv_sem=halo_recv.at[place], device_id=where, device_id_type=MESH,
        )
        copy.start()
        halos.append(copy)

    for side in range(2):
        send_halo(
            P.at[:, 2 + 14 * side : 4 + 14 * side, 8:24, :],
            P.at[:, 18 - 18 * side : 20 - 18 * side, 8:24, :],
            (x_beside[side], gz),
        )

    for side in range(2):
        for layer in range(2):
            z = 8 + 14 * side + layer
            for f in range(FIELDS):
                for half in range(2):
                    lanes = pl.ds(128 * half, 128)
                    Zs[side, layer, f, 8:24, lanes] = P[f, 2:18, z, lanes]
    for xs in range(2):
        for zs in range(2):
            for f in range(FIELDS):
                Cs[2 * xs + zs, f : f + 1, :] = P[f, 2 + 15 * xs, 8 + 15 * zs : 9 + 15 * zs, :]

    for side in range(2):
        send_halo(Zs.at[side, :, :, 8:24, :], Zr.at[1 - side, :, :, 8:24, :], (gx, z_beside[side]))
    for xs in range(2):
        for zs in range(2):
            send_halo(
                Cs.at[2 * xs + zs], Cr.at[2 * (1 - xs) + 1 - zs], (x_beside[xs], z_beside[zs])
            )

    yz = gz // 2
    places = nz // 2
    along = (lax.rem(gz, 2) * (nx // 2) + gx // 2) * 2 + lax.rem(gx, 2)
    line = 2 * nx

    def spread_yz(place, source, slots):
        def body(d, carry):
            peer = lax.rem(yz + d, places)
            pltpu.make_async_remote_copy(
                src_ref=source(peer), dst_ref=slots.at[yz], send_sem=group_send.at[place],
                recv_sem=group_recv.at[place], device_id=(gx, 2 * peer + lax.rem(gz, 2)),
                device_id_type=MESH,
            ).start()
            return carry

        lax.fori_loop(1, places, body, 0)

    def spread_line(place, source, slots):
        def body(d, carry):
            peer = lax.rem(along + d, line)
            where = (lax.rem(peer, nx), 2 * yz + peer // nx)
            pltpu.make_async_remote_copy(
                src_ref=source(peer), dst_ref=slots.at[along], send_sem=group_send.at[place],
                recv_sem=group_recv.at[place], device_id=where, device_id_type=MESH,
            ).start()
            return carry

        lax.fori_loop(1, line, body, 0)

    core = lax.rem(gx, 2)
    chip = (gx // 2) * nz + gz
    chips = (nx // 2) * nz

    def send_core(place, source, target):
        pltpu.make_async_remote_copy(
            src_ref=source, dst_ref=target, send_sem=group_send.at[place],
            recv_sem=group_recv.at[place], device_id=(gx + 1 - 2 * core, gz), device_id_type=MESH,
        ).start()

    def spread_chips(place, source, slots):
        def body(d, carry):
            peer = lax.rem(chip + d, chips)
            where = (2 * (peer // nz) + core, lax.rem(peer, nz))
            pltpu.make_async_remote_copy(
                src_ref=source, dst_ref=slots.at[chip], send_sem=group_send.at[place],
                recv_sem=group_recv.at[place], device_id=where, device_id_type=MESH,
            ).start()
            return carry

        lax.fori_loop(1, chips, body, 0)

    def wait_one(sems, place, part):
        pltpu.make_async_copy(part, part, sems.at[place]).wait()

    def sum_slots_of(slots):
        terms = [slots[j] for j in range(slots.shape[0])]
        while len(terms) > 1:
            terms = [a + b for a, b in zip(terms[::2], terms[1::2])] + terms[len(terms) & ~1 :]
        return terms[0]

    def wait_all(sems, place, slots):
        some = slots.at[pl.ds(0, slots.shape[0] - 1)]
        pltpu.make_async_copy(some, some, sems.at[place]).wait()

    fetch.wait()
    take_basis(basis_view, basis_rows)
    rows = basis_rows[...]
    head = rows.astype(BF16)
    basis_h[...] = head
    basis_l[...] = (rows - head.astype(F32)).astype(BF16)

    def pair():
        return basis_h[...], basis_l[...]

    inner = dot_three(pair(), pair(), TN)
    for i in range(16):
        g_send[i, :, :256] = inner[8 * i : 8 * i + 8]
        g_send[i, :, 256:] = inner[128 + 8 * i : 136 + 8 * i, 128:]
    spread_yz(1, lambda peer: g_send.at[peer], g_slots)
    g_slots[yz] = g_send[yz]

    profiles = [profile_rows[k] for k in range(3)]

    def first(i, carry):
        centre = [P[f, i + 1, 8:24, :] for f in range(FIELDS)]
        xl = [P[f, i, 8:24, :] for f in range(FIELDS)]
        xu = [P[f, i + 2, 8:24, :] for f in range(FIELDS)]
        zl = [P[f, i + 1, 7:23, :] for f in range(FIELDS)]
        zu = [P[f, i + 1, 9:25, :] for f in range(FIELDS)]
        new = update(centre, xl, xu, zl, zu, profiles)
        for f in range(FIELDS):
            H[f, i, 8:24, :] = new[f]
        return carry

    lax.fori_loop(2, 16, first, 0)

    wait_all(group_recv, 0, early_slots)
    got = jnp.concatenate([early_slots[:, 0, :], early_slots[:, 1, :]], axis=0).T
    for zx in range(16):
        S[:, zx * 64 : zx * 64 + 64] = got[zx * 16 : zx * 16 + 16]
    snaps = halves(S[...])
    c_early = dot_three(snaps, pair())
    k_early = dot_three(snaps, snaps, NT)
    early = jnp.concatenate([c_early, k_early, jnp.zeros((16, 112), F32)], axis=1)
    for m in range(16):
        e_send[m] = early[m : m + 1]
    spread_yz(8, lambda peer: e_send.at[peer], e_slots)
    e_slots[yz] = e_send[yz]

    for copy in halos:
        copy.wait_recv()
    for f in range(FIELDS):
        for xs in range(2):
            row = 7 + 17 * xs
            x = 1 + 17 * xs
            for zs in range(2):
                corner = Cr[2 * xs + zs, f : f + 1, :]
                Zr[zs, 1 - zs, f, row : row + 1, :] = corner
                P[f, x, 7 + 17 * zs : 8 + 17 * zs, :] = corner
                Zs[zs, zs, f, row : row + 1, :] = P[f, x, 8 + 15 * zs : 9 + 15 * zs, :]
    lax.fori_loop(0, 4, lambda k, carry: first(k + 14 * (k // 2), carry), 0)
    for side in range(2):
        layers = [Zr.at[side, side], Zr.at[side, 1 - side], Zs.at[side, side], Zs.at[side, 1 - side]]
        for edge in range(2):
            outer, mid, inside = layers[edge : edge + 3]
            centre = [mid[f, 8:24, :] for f in range(FIELDS)]
            xl = [mid[f, 7:23, :] for f in range(FIELDS)]
            xu = [mid[f, 9:25, :] for f in range(FIELDS)]
            out = [outer[f, 8:24, :] for f in range(FIELDS)]
            within = [inside[f, 8:24, :] for f in range(FIELDS)]
            zl, zu = (out, within) if side == 0 else (within, out)
            new = update(centre, xl, xu, zl, zu, profiles)
            z = 7 + edge if side == 0 else 24 - edge
            for f in range(FIELDS):
                H[f, 1:17, z, :] = new[f]

    wait_all(group_recv, 1, g_slots)
    total = sum_slots_of(g_slots)
    for r in range(8):
        g_mid[r] = total[r : r + 1]
    spread_line(3, lambda peer: g_mid.at[peer], g_mid_slots)
    g_mid_slots[along] = g_mid[along]

    def second(i, carry):
        centre = [H[f, i + 1, 8:24, :] for f in range(FIELDS)]
        xl = [H[f, i, 8:24, :] for f in range(FIELDS)]
        xu = [H[f, i + 2, 8:24, :] for f in range(FIELDS)]
        zl = [H[f, i + 1, 7:23, :] for f in range(FIELDS)]
        zu = [H[f, i + 1, 9:25, :] for f in range(FIELDS)]
        new = update(centre, xl, xu, zl, zu, profiles)
        for f in range(FIELDS):
            F[f, i, :, :] = new[f]
        return carry

    lax.fori_loop(0, 16, second, 0)
    store = pltpu.make_async_copy(F, out_fields, out_sem)
    store.start()

    for xg in range(4):
        V[16 * xg : 16 * xg + 16, :] = (H[0, 4 * xg + 1, 8:24, :] + H[0, 4 * xg + 2, 8:24, :]) + (
            H[0, 4 * xg + 3, 8:24, :] + H[0, 4 * xg + 4, 8:24, :]
        )
        V[64 + 16 * xg : 80 + 16 * xg, :] = (F[0, 4 * xg] + F[0, 4 * xg + 1]) + (
            F[0, 4 * xg + 2] + F[0, 4 * xg + 3]
        )
    to = lax.broadcasted_iota(jnp.int32, (128, 128), 0)
    of = lax.broadcasted_iota(jnp.int32, (128, 128), 1)
    wanted = ((lax.rem(of, 16) // 4) * 4 + lax.rem(of, 64) // 16) * 8 + 6 + of // 64
    place_to = (to == wanted).astype(BF16)
    sums = halves(V[...])
    gathered = dot(
        jnp.concatenate([place_to, place_to], axis=1), jnp.concatenate(sums, axis=0)
    )
    block = (
        lax.broadcasted_iota(jnp.int32, (64, 256), 0)
        == lax.broadcasted_iota(jnp.int32, (64, 256), 1) // 4
    ).astype(BF16) * BF16(1.0 / 64.0)
    coarse = dot(
        jnp.concatenate([block, block], axis=1), jnp.concatenate(halves(gathered), axis=1), NT
    )
    for i in range(32):
        late_send[i] = coarse[2 * i : 2 * i + 2]
    spread_z(2, lambda peer: late_send.at[peer], late_slots)
    late_slots[gz] = late_send[gz]

    wait_all(group_recv, 8, e_slots)
    e_mid[...] = sum_slots_of(e_slots)
    spread_line(9, lambda peer: e_mid, e_mid_slots)
    e_mid_slots[along] = e_mid[...]

    wait_all(group_recv, 3, g_mid_slots)
    g_part[...] = sum_slots_of(g_mid_slots)
    spread_line(5, lambda peer: g_part, g_parts)
    g_parts[along] = g_part[...]

    wait_all(group_recv, 5, g_parts)
    for r in range(8):
        g_whole[r : r + 1, :] = g_parts[r]
    spread_yz(7, lambda peer: g_whole, g_all)
    g_all[yz] = g_whole[...]

    wait_all(group_recv, 9, e_mid_slots)
    e_part[...] = sum_slots_of(e_mid_slots)
    spread_yz(10, lambda peer: e_part, e_all)
    e_all[yz] = e_part[...]

    wait_all(group_recv, 2, late_slots)
    got = jnp.concatenate([late_slots[:, 0, :], late_slots[:, 1, :]], axis=0).T
    for zx in range(16):
        S[8:16, zx * 64 : zx * 64 + 64] = S[8:16, zx * 64 : zx * 64 + 64] + got[zx * 8 : zx * 8 + 8]
    low = S[8:16, :]
    low = jnp.where(lax.broadcasted_iota(jnp.int32, low.shape, 0) >= 6, low, 0.0)
    late = halves(jnp.concatenate([jnp.zeros_like(low), low], axis=0))
    both = dot(jnp.concatenate(late, axis=0), basis_h[...])
    c_late = (both[:16] + both[16:] + dot(late[0], basis_l[...]))[14:16]
    k_late = dot_three(late, halves(S[...]), NT)[14:16]
    late = jnp.concatenate([c_late, k_late, jnp.zeros((2, 112), F32)], axis=1)
    c_send[...] = late
    send_core(4, c_send, c_other)
    wait_one(group_recv, 4, c_other)
    both = late + c_other[...]
    c_mid[...] = both
    spread_chips(6, c_mid, c_slots)
    c_slots[chip] = both

    wait_all(group_recv, 7, g_all)
    every = g_all[...].reshape(128, 384)
    cross = every[:, 128:256]
    metric = jnp.concatenate(
        [every[:, :256], jnp.concatenate([cross.T, every[:, 256:]], axis=1)], axis=0
    ) * (1.0 / rows_total)
    unit = eye(256)
    removed = 4.0 * unit - 6.0 * metric + dot_high(dot_high(metric, metric), 4.0 * unit - metric)
    wait_all(group_recv, 10, e_all)
    early = e_all[...].reshape(16, 384)
    wait_all(group_recv, 6, c_slots)
    total = jnp.concatenate([early[:14], sum_slots_of(c_slots)], axis=0) * (1.0 / rows_total)
    c_one = total[:, :256]
    gram = total[:, 256:272]
    low_row = lax.broadcasted_iota(jnp.int32, (16, 16), 0) >= 14
    low_col = lax.broadcasted_iota(jnp.int32, (16, 16), 1) >= 14
    below = jnp.where(low_row, gram, 0.0)
    size = jnp.where(low_col & ~low_row, below.T, gram)
    gram = size - dot_high(dot_high(c_one, removed), c_one, NT)
    coeffs = 2.0 * c_one - dot_high(c_one, metric)
    out_coeffs[...] = coeffs
    factor_t, inverse, pivots = cholesky(gram + gram_eps * eye(16))
    out_factor[...] = factor_t
    out_inverse[...] = inverse
    diagonal = eye(16) > 0.0
    scale = jnp.sum(jnp.where(diagonal, size, 0.0), axis=0, keepdims=True)
    sound = jnp.where(pivots > least_pivot * scale, 1, 0)
    out_sound[0, 0] = jnp.min(sound)
    out_resid[...] = S[...] - dot_three(halves(coeffs), pair(), NT)

    for copy in halos:
        copy.wait_send()
    for place, slots in (
        (0, early_slots), (1, g_slots), (2, late_slots), (3, g_mid_slots), (5, g_parts),
        (6, c_slots), (7, g_all), (8, e_slots), (9, e_mid_slots), (10, e_all),
    ):
        wait_all(group_send, place, slots)
    wait_one(group_send, 4, c_other)
    store.wait()


def front(sizes, fields, profiles, earlier, basis_view):
    nx, nz = sizes
    vmem = pl.BlockSpec(memory_space=pltpu.VMEM)
    hbm = pl.BlockSpec(memory_space=pltpu.HBM)
    smem = pl.BlockSpec(memory_space=pltpu.SMEM)
    v = pltpu.VMEM
    return pl.pallas_call(
        functools.partial(front_kernel, sizes),
        out_shape=(
            jax.ShapeDtypeStruct(fields.shape, F32),
            jax.ShapeDtypeStruct((16, 256), F32),
            jax.ShapeDtypeStruct((16, 16), F32),
            jax.ShapeDtypeStruct((16, 16), F32),
            jax.ShapeDtypeStruct((1, 1), jnp.int32),
            jax.ShapeDtypeStruct((16, 1024), F32),
        ),
        in_specs=[hbm] * 6,
        out_specs=(hbm, vmem, vmem, vmem, smem, vmem),
        scratch_shapes=[
            v((5, 20, 32, 256), F32),
            v((5, 18, 32, 256), F32),
            v((5, 16, 16, 256), F32),
            v((2, 2, 5, 32, 256), F32),
            v((2, 2, 5, 32, 256), F32),
            v((4, 8, 256), F32),
            v((4, 8, 256), F32),
            v((128, 256), F32),
            v((2048, 128), F32),
            v((1024, 256), F32),
            v((1024, 256), BF16),
            v((1024, 256), BF16),
            v((64, 256), F32),
            v((32, 2, 256), F32),
            v((32, 2, 256), F32),
            v((32, 2, 128), F32),
            v((32, 2, 128), F32),
            v((16, 1024), F32),
            v((16, 8, 384), F32),
            v((16, 8, 384), F32),
            v((8, 1, 384), F32),
            v((8, 1, 384), F32),
            v((1, 384), F32),
            v((8, 1, 384), F32),
            v((8, 384), F32),
            v((16, 8, 384), F32),
            v((16, 1, 384), F32),
            v((16, 1, 384), F32),
            v((1, 384), F32),
            v((8, 1, 384), F32),
            v((1, 384), F32),
            v((16, 1, 384), F32),
            v((2, 384), F32),
            v((2, 384), F32),
            v((2, 384), F32),
            v((64, 2, 384), F32),
            v((14, 4, 256), F32),
            v((3, 1, 256), F32),
            pltpu.SemaphoreType.DMA((4,)),
            pltpu.SemaphoreType.DMA,
            pltpu.SemaphoreType.DMA,
            pltpu.SemaphoreType.DMA,
            pltpu.SemaphoreType.DMA((8,)),
            pltpu.SemaphoreType.DMA((8,)),
            pltpu.SemaphoreType.DMA((11,)),
            pltpu.SemaphoreType.DMA((11,)),
        ],
        compiler_params=pltpu.CompilerParams(
            collective_id=0, has_side_effects=True, vmem_limit_bytes=62 * 1024 * 1024
        ),
    )(fields, *profiles, earlier, basis_view)


def direct_factor(resid):
    rows_total = 1024.0 * lax.axis_size("gx") * lax.axis_size("gz")
    gram = lax.psum(jnp.dot(resid, resid.T, precision=HIGH), ("gx", "gz")) / rows_total
    identity = jnp.eye(16, dtype=F32)
    factor = jnp.linalg.cholesky(gram + gram_eps * identity)
    return factor.T, jax.scipy.linalg.solve_triangular(factor, identity, lower=True)


def on_device(fields, courant, shear_rate, gradient, earlier, basis_modes, core_matrix):
    sizes = (lax.axis_size("gx"), lax.axis_size("gz"))
    view = view_of(basis_modes)
    profiles = [p.reshape(1, -1) for p in (courant, shear_rate, gradient)]
    finished, coeffs, factor_t, inverse, sound, resid = front(
        sizes, fields, profiles, earlier, view
    )
    factor_t, inverse = lax.cond(
        sound[0, 0] > 0,
        lambda resid, factor_t, inverse: (factor_t, inverse),
        lambda resid, factor_t, inverse: direct_factor(resid),
        resid, factor_t, inverse,
    )
    finished, new_view, new_core = tail(
        core_matrix, coeffs, factor_t, inverse, resid, view, finished
    )
    return (finished, basis_of(new_view), new_core)


def solution(mesh):
    return jax.shard_map(
        on_device,
        mesh=mesh,
        in_specs=(
            P(None, "gx", "gz", None),
            P(),
            P(),
            P(),
            P(None, "gx", "gz"),
            P("gx", None, "gz", None),
            P(),
        ),
        out_specs=(P(None, "gx", "gz", None), P("gx", None, "gz", None), P()),
        check_vma=False,
    )
```

```python
import functools

import jax
import jax.numpy as jnp
from jax import lax
from jax.experimental import pallas as pl
from jax.experimental.pallas import tpu as pltpu
from jax.sharding import PartitionSpec as P

F32, BF16 = jnp.float32, jnp.bfloat16
HIGH = lax.Precision.HIGHEST
SIGN_STEPS = 10
POLAR_STEPS = 3
gram_eps = 1e-06


def halves(values):
    head = values.astype(BF16)
    return head, (values - head.astype(F32)).astype(BF16)


def dot(left, right, over=((1,), (0,))):
    return lax.dot_general(left, right, (over, ((), ())), preferred_element_type=F32)


def dot_three(left, right, over=((1,), (0,))):
    (lh, ll), (rh, rl) = left, right
    return dot(lh, rh, over) + (dot(lh, rl, over) + dot(ll, rh, over))


def dot_high(left, right, over=((1,), (0,))):
    return lax.dot_general(
        left, right, (over, ((), ())), precision=HIGH, preferred_element_type=F32
    )


TN = ((0,), (0,))
NT = ((1,), (1,))


def tripled_left(pair):
    return jnp.concatenate([pair[0], pair[0], pair[1]], axis=0)


def tripled_right(pair):
    return jnp.concatenate([pair[0], pair[1], pair[0]], axis=0)


def eye(count):
    return (
        lax.broadcasted_iota(jnp.int32, (count, count), 0)
        == lax.broadcasted_iota(jnp.int32, (count, count), 1)
    ).astype(F32)


def row_places(z_lanes):
    places = []
    for zc in range(4):
        for x in range(4):
            for y in range(2):
                places.append((zc, x, y))
    return places


def take_basis(view_ref, rows_ref):
    for place, (zc, x, y) in enumerate(row_places(0)):
        for half in range(2):
            rows_ref[pl.ds(place * 32, 32), pl.ds(half * 128, 128)] = view_ref[
                pl.ds(512 * x + 4 * zc + 2 * half + y, 32, stride=16), :
            ]


def give_basis(rows, view_ref, first):
    for step in range(8):
        zc, x, y = row_places(0)[first + step]
        for half in range(2):
            view_ref[pl.ds(512 * x + 4 * zc + 2 * half + y, 32, stride=16), :] = rows[
                step * 32 : step * 32 + 32, half * 128 : half * 128 + 128
            ]


def cholesky(gram):
    count = gram.shape[0]
    row_index = lax.broadcasted_iota(jnp.int32, (count, count), 0)
    col_index = lax.broadcasted_iota(jnp.int32, (count, count), 1)
    left = gram
    right = eye(count)
    pivots = jnp.zeros((1, count), F32)
    for j in range(count):
        pivot = left[j : j + 1, j : j + 1]
        pivots = jnp.where(col_index[:1] == j, pivot, pivots)
        scale = lax.rsqrt(pivot)
        scale = scale * (1.5 - 0.5 * pivot * scale * scale)
        column = left[:, j : j + 1] * scale
        row_l = left[j : j + 1, :] * scale
        row_r = right[j : j + 1, :] * scale
        below = row_index > j
        here = row_index == j
        left = jnp.where(below, left - column * row_l, jnp.where(here, row_l, left))
        right = jnp.where(below, right - column * row_r, jnp.where(here, row_r, right))
    return jnp.where(row_index <= col_index, left, 0.0), right, pivots


def wide_left(v, d):
    modes = v.shape[1]
    vh, vl = halves(v)
    dh, dl = halves(d)
    bh, bl = vh[modes:].astype(F32), vl[modes:].astype(F32)
    turned = jnp.concatenate([bh, bh, bl], axis=0).T.astype(BF16)
    edge = jnp.concatenate([turned, jnp.concatenate([dh, dh, dl], axis=1)], axis=0)
    return vh, vl, edge, jnp.concatenate([vh[modes:], vh[modes:], vl[modes:], edge[modes:]], axis=1)


def product(left, right_v, right_d):
    modes = right_v.shape[1]
    rh, rl = halves(right_v)
    dh, dl = halves(right_d)
    ah, bh = rh[:modes], rh[modes:]
    al, bl = rl[:modes], rl[modes:]
    stacked = jnp.concatenate([ah, al, ah, bh, bl, bh], axis=0)
    low = jnp.concatenate([bh, bl, bh, dh, dl, dh], axis=1)
    vh, vl, edge, wide = left
    thin = jnp.concatenate([bh, bl, bh], axis=0)
    top = (dot(vh[:modes], ah) + dot(vh[:modes], al)) + (dot(vl[:modes], ah) + dot(edge[:modes], thin))
    bottom = dot(wide, jnp.concatenate([ah, al, ah, thin], axis=0))
    return jnp.concatenate([top, bottom], axis=0), dot(wide, low, NT)


def tail_kernel(core_ref, coeffs_ref, factor_ref, inverse_ref, resid_ref, basis_hbm, fields_hbm,
                out_fields, out_basis, out_core, v_ref, d_ref, basis_view, basis_rows, held, sem, field_sem):
    modes = core_ref.shape[0]
    fetch = pltpu.make_async_copy(basis_hbm, basis_view, sem)
    fetch.start()
    taking = pltpu.make_async_copy(fields_hbm, held, field_sem)
    taking.start()
    factor_t = factor_ref[...]
    inverse = inverse_ref[...]
    coeffs = coeffs_ref[...]
    unit = eye(modes)
    unit_d = eye(16)
    parts = halves(coeffs)
    corr_a = core_ref[...] + dot(tripled_left(parts), tripled_right(parts), TN)
    corr_b = dot_high(factor_t, coeffs)
    corr_d = dot_high(factor_t, factor_t, NT)
    shift_a = corr_a - unit
    shift_d = corr_d - unit_d
    total = (
        jnp.sum(shift_a * shift_a, keepdims=True)
        + 2.0 * jnp.sum(corr_b * corr_b, keepdims=True)
        + jnp.sum(shift_d * shift_d, keepdims=True)
    )
    scale = 1.0 / jnp.sqrt(total)
    v_ref[:modes] = shift_a * scale
    v_ref[modes:] = corr_b * scale
    d_ref[...] = shift_d * scale
    unit_v = jnp.concatenate([unit, jnp.zeros((16, modes), F32)], axis=0)

    def sign_step(step, carry):
        v = v_ref[...]
        d = d_ref[...]
        left = wide_left(v, d)
        square_v, square_d = product(left, v, d)
        next_v, next_d = product(
            left, 1.5 * unit_v - 0.5 * square_v, 1.5 * unit_d - 0.5 * square_d
        )
        v_ref[...] = next_v
        d_ref[...] = next_d
        return carry

    lax.fori_loop(0, SIGN_STEPS, sign_step, 0)

    fetch.wait()
    taking.wait()
    passing = pltpu.make_async_copy(held, out_fields, field_sem)
    passing.start()
    take_basis(basis_view, basis_rows)

    rot = 0.5 * (unit_v + v_ref[...])
    pair = halves(rot)
    top = (pair[0][:modes], pair[1][:modes])
    low = (pair[0][modes:], pair[1][modes:])
    inner = dot_three(top, top) + dot(tripled_left(low), tripled_right(low), TN)
    for step in range(POLAR_STEPS):
        factor = 1.5 * unit - 0.5 * inner
        fp = halves(factor)
        rot = dot_three(halves(rot), fp)
        if step < POLAR_STEPS - 1:
            inner = dot_three(halves(dot_three(halves(inner), fp)), fp)
    rp = halves(rot)
    corr_v = jnp.concatenate([corr_a, corr_b], axis=0)
    moved = dot_three(halves(corr_v), (rp[0][:modes], rp[1][:modes]))
    rb48 = tripled_right((rp[0][modes:], rp[1][modes:]))
    moved = moved + jnp.concatenate(
        [
            dot(tripled_left(halves(corr_b)), rb48, TN),
            dot(tripled_left(halves(corr_d)), rb48, TN),
        ],
        axis=0,
    )
    out_core[...] = dot_three(rp, halves(moved), TN)

    mix = dot_high(inverse, rot[modes:], TN)
    mix48 = tripled_right(halves(mix))
    ra = (rp[0][:modes], rp[1][:modes])
    for part in range(4):
        rows = basis_rows[pl.ds(part * 256, 256), :]
        left = tripled_left(halves(resid_ref[:, part * 256 : part * 256 + 256]))
        give_basis(dot_three(halves(rows), ra) + dot(left, mix48, TN), out_basis, part * 8)
    passing.wait()


def tail(core, coeffs, factor_t, inverse, resid, basis_view, fields):
    vmem = pl.BlockSpec(memory_space=pltpu.VMEM)
    hbm = pl.BlockSpec(memory_space=pltpu.HBM)
    return pl.pallas_call(
        tail_kernel,
        out_shape=(
            jax.ShapeDtypeStruct(fields.shape, F32),
            jax.ShapeDtypeStruct((2048, 128), F32),
            jax.ShapeDtypeStruct((256, 256), F32),
        ),
        in_specs=[vmem, vmem, vmem, vmem, vmem, hbm, hbm],
        out_specs=(hbm, vmem, vmem),
        scratch_shapes=[
            pltpu.VMEM((272, 256), F32),
            pltpu.VMEM((16, 16), F32),
            pltpu.VMEM((2048, 128), F32),
            pltpu.VMEM((1024, 256), F32),
            pltpu.VMEM(fields.shape, F32),
            pltpu.SemaphoreType.DMA,
            pltpu.SemaphoreType.DMA,
        ],
        compiler_params=pltpu.CompilerParams(vmem_limit_bytes=60 * 1024 * 1024),
    )(core, coeffs, factor_t, inverse, resid, basis_view, fields)


def view_of(basis):
    return basis.reshape(4, 128, 2, 2, 128).transpose(0, 1, 3, 2, 4).reshape(2048, 128)


def basis_of(view):
    return view.reshape(4, 128, 2, 2, 128).transpose(0, 1, 3, 2, 4).reshape(4, 128, 2, 256)


MESH = pl.DeviceIdType.MESH
press_coef = 0.25
compress_coef = 0.25
visc_coef = 0.05
heat_coef = 0.03
FIELDS = 5
least_pivot = 2.0**-7


def shifted(values):
    width = values.shape[-1]
    lane = lax.broadcasted_iota(jnp.int32, values.shape, 1)
    lower = jnp.where(lane == 0, 0.0, pltpu.roll(values, 1, 1))
    upper = jnp.where(lane == width - 1, 0.0, pltpu.roll(values, width - 1, 1))
    return lower, upper


def update(centre, xl, xu, zl, zu, profiles, wanted=range(FIELDS)):
    courant, shear_rate, gradient = profiles
    beside = [shifted(c) for c in centre]
    keep = [1.0 - 6.0 * visc_coef - courant] * 3 + [1.0 - 6.0 * visc_coef]
    keep = keep + [1.0 - 6.0 * heat_coef - courant]
    bring = [visc_coef + courant] * 3 + [visc_coef, heat_coef + courant]
    spread = [visc_coef] * 4 + [heat_coef]
    half_press = 0.5 * press_coef
    divergence = (xu[0] - xl[0]) + (beside[1][1] - beside[1][0]) + (zu[2] - zl[2])
    sources = [
        shear_rate * centre[1] + half_press * (xu[3] - xl[3]),
        half_press * (beside[3][1] - beside[3][0]),
        half_press * (zu[3] - zl[3]),
        0.5 * compress_coef * divergence,
        gradient * centre[1],
    ]
    new = {}
    for f in wanted:
        around = (xu[f] + zl[f]) + (zu[f] + beside[f][0]) + beside[f][1]
        new[f] = keep[f] * centre[f] + bring[f] * xl[f] + spread[f] * around - sources[f]
    return new


def front_kernel(sizes, fields_hbm, courant_hbm, shear_hbm, gradient_hbm, earlier_hbm, basis_hbm,
                 out_fields, out_coeffs, out_factor, out_inverse, out_sound, out_resid,
                 P, H, F, Zs, Zr, Cs, Cr, V, basis_view, basis_rows, basis_h, basis_l,
                 E2, early_send, early_slots, late_send, late_slots, S,
                 g_send, g_slots, g_mid, g_mid_slots, g_part, g_parts, g_whole, g_all,
                 e_send, e_slots, e_mid, e_mid_slots, e_part, e_all,
                 c_send, c_other, c_mid, c_slots,
                 earlier_ref, profile_rows, small_sem, load_sem, basis_sem, out_sem, halo_send, halo_recv,
                 group_send, group_recv):
    nx, nz = sizes
    gx = lax.axis_index("gx")
    gz = lax.axis_index("gz")
    rows_total = 1024.0 * nx * nz

    barrier = pltpu.get_barrier_semaphore()
    x_beside = (lax.rem(gx + nx - 1, nx), lax.rem(gx + 1, nx))
    z_beside = (lax.rem(gz + nz - 1, nz), lax.rem(gz + 1, nz))

    def greet(where):
        pl.semaphore_signal(barrier, inc=1, device_id=where, device_id_type=MESH)

    def greet_z(d, carry):
        greet((gx, lax.rem(gz + d, nz)))
        return carry

    load = pltpu.make_async_copy(fields_hbm, P.at[:, 2:18, 8:24, :], load_sem)
    load.start()
    fetch = pltpu.make_async_copy(basis_hbm, basis_view, basis_sem)
    fetch.start()
    small = [
        pltpu.make_async_copy(earlier_hbm, earlier_ref, small_sem.at[0]),
        pltpu.make_async_copy(courant_hbm, profile_rows.at[0], small_sem.at[1]),
        pltpu.make_async_copy(shear_hbm, profile_rows.at[1], small_sem.at[2]),
        pltpu.make_async_copy(gradient_hbm, profile_rows.at[2], small_sem.at[3]),
    ]
    for copy in small:
        copy.start()
    for d in range(1, nx):
        greet((lax.rem(gx + d, nx), gz))
    for xs in range(2):
        for zs in range(2):
            greet((x_beside[xs], z_beside[zs]))
    for d in range(1, nx):
        greet((lax.rem(gx + d, nx), gz + 1 - 2 * lax.rem(gz, 2)))
    lax.fori_loop(1, nz, greet_z, 0)

    for copy in small:
        copy.wait()
    E2[...] = jnp.zeros_like(E2)
    for m in range(14):
        for x in range(4):
            E2[x * 16 + m : x * 16 + m + 1, :] = earlier_ref[m, x : x + 1, :]
    turned = E2[...].T
    turned = jnp.concatenate([turned[64 * z : 64 * z + 64] for z in range(4)], axis=1)
    for i in range(32):
        early_send[i] = turned[2 * i : 2 * i + 2]
    pl.semaphore_wait(barrier, nz - 1 + 2 * (nx - 1) + 4)

    def spread_z(place, source, slots):
        def body(d, carry):
            peer = lax.rem(gz + d, nz)
            pltpu.make_async_remote_copy(
                src_ref=source(peer), dst_ref=slots.at[gz], send_sem=group_send.at[place],
                recv_sem=group_recv.at[place], device_id=(gx, peer), device_id_type=MESH,
            ).start()
            return carry

        lax.fori_loop(1, nz, body, 0)

    spread_z(0, lambda peer: early_send.at[peer], early_slots)
    early_slots[gz] = early_send[gz]

    load.wait()

    halos = []

    def send_halo(source, target, where):
        place = len(halos)
        copy = pltpu.make_async_remote_copy(
            src_ref=source, dst_ref=target, send_sem=halo_send.at[place],
            recv_sem=halo_recv.at[place], device_id=where, device_id_type=MESH,
        )
        copy.start()
        halos.append(copy)

    for side in range(2):
        send_halo(
            P.at[:, 2 + 14 * side : 4 + 14 * side, 8:24, :],
            P.at[:, 18 - 18 * side : 20 - 18 * side, 8:24, :],
            (x_beside[side], gz),
        )

    for side in range(2):
        for layer in range(2):
            z = 8 + 14 * side + layer
            for f in range(FIELDS):
                for half in range(2):
                    lanes = pl.ds(128 * half, 128)
                    Zs[side, layer, f, 8:24, lanes] = P[f, 2:18, z, lanes]
    for xs in range(2):
        for zs in range(2):
            for f in range(FIELDS):
                Cs[2 * xs + zs, f : f + 1, :] = P[f, 2 + 15 * xs, 8 + 15 * zs : 9 + 15 * zs, :]

    for side in range(2):
        send_halo(Zs.at[side, :, :, 8:24, :], Zr.at[1 - side, :, :, 8:24, :], (gx, z_beside[side]))
    for xs in range(2):
        for zs in range(2):
            send_halo(
                Cs.at[2 * xs + zs], Cr.at[2 * (1 - xs) + 1 - zs], (x_beside[xs], z_beside[zs])
            )

    yz = gz // 2
    places = nz // 2
    along = (lax.rem(gz, 2) * (nx // 2) + gx // 2) * 2 + lax.rem(gx, 2)
    line = 2 * nx

    def spread_yz(place, source, slots):
        def body(d, carry):
            peer = lax.rem(yz + d, places)
            pltpu.make_async_remote_copy(
                src_ref=source(peer), dst_ref=slots.at[yz], send_sem=group_send.at[place],
                recv_sem=group_recv.at[place], device_id=(gx, 2 * peer + lax.rem(gz, 2)),
                device_id_type=MESH,
            ).start()
            return carry

        lax.fori_loop(1, places, body, 0)

    def spread_line(place, source, slots):
        def body(d, carry):
            peer = lax.rem(along + d, line)
            where = (lax.rem(peer, nx), 2 * yz + peer // nx)
            pltpu.make_async_remote_copy(
                src_ref=source(peer), dst_ref=slots.at[along], send_sem=group_send.at[place],
                recv_sem=group_recv.at[place], device_id=where, device_id_type=MESH,
            ).start()
            return carry

        lax.fori_loop(1, line, body, 0)

    core = lax.rem(gx, 2)
    chip = (gx // 2) * nz + gz
    chips = (nx // 2) * nz

    def send_core(place, source, target):
        pltpu.make_async_remote_copy(
            src_ref=source, dst_ref=target, send_sem=group_send.at[place],
            recv_sem=group_recv.at[place], device_id=(gx + 1 - 2 * core, gz), device_id_type=MESH,
        ).start()

    def spread_chips(place, source, slots):
        def body(d, carry):
            peer = lax.rem(chip + d, chips)
            where = (2 * (peer // nz) + core, lax.rem(peer, nz))
            pltpu.make_async_remote_copy(
                src_ref=source, dst_ref=slots.at[chip], send_sem=group_send.at[place],
                recv_sem=group_recv.at[place], device_id=where, device_id_type=MESH,
            ).start()
            return carry

        lax.fori_loop(1, chips, body, 0)

    def wait_one(sems, place, part):
        pltpu.make_async_copy(part, part, sems.at[place]).wait()

    def sum_slots_of(slots):
        terms = [slots[j] for j in range(slots.shape[0])]
        while len(terms) > 1:
            terms = [a + b for a, b in zip(terms[::2], terms[1::2])] + terms[len(terms) & ~1 :]
        return terms[0]

    def wait_all(sems, place, slots):
        some = slots.at[pl.ds(0, slots.shape[0] - 1)]
        pltpu.make_async_copy(some, some, sems.at[place]).wait()

    fetch.wait()
    take_basis(basis_view, basis_rows)
    rows = basis_rows[...]
    head = rows.astype(BF16)
    basis_h[...] = head
    basis_l[...] = (rows - head.astype(F32)).astype(BF16)

    def pair():
        return basis_h[...], basis_l[...]

    inner = dot_three(pair(), pair(), TN)
    for i in range(16):
        g_send[i, :, :256] = inner[8 * i : 8 * i + 8]
        g_send[i, :, 256:] = inner[128 + 8 * i : 136 + 8 * i, 128:]
    spread_yz(1, lambda peer: g_send.at[peer], g_slots)
    g_slots[yz] = g_send[yz]

    profiles = [profile_rows[k] for k in range(3)]

    def first(i, wanted=range(FIELDS)):
        centre = [P[f, i + 1, 8:24, :] for f in range(FIELDS)]
        xl = [P[f, i, 8:24, :] for f in range(FIELDS)]
        xu = [P[f, i + 2, 8:24, :] for f in range(FIELDS)]
        zl = [P[f, i + 1, 7:23, :] for f in range(FIELDS)]
        zu = [P[f, i + 1, 9:25, :] for f in range(FIELDS)]
        for f, new in update(centre, xl, xu, zl, zu, profiles, wanted).items():
            H[f, i, 8:24, :] = new

    def first_inside(i, carry):
        first(i)
        return carry

    lax.fori_loop(2, 16, first_inside, 0)

    wait_all(group_recv, 0, early_slots)
    got = jnp.concatenate([early_slots[:, 0, :], early_slots[:, 1, :]], axis=0).T
    for zx in range(16):
        S[:, zx * 64 : zx * 64 + 64] = got[zx * 16 : zx * 16 + 16]
    snaps = halves(S[...])
    c_early = dot_three(snaps, pair())
    k_early = dot_three(snaps, snaps, NT)
    early = jnp.concatenate([c_early, k_early, jnp.zeros((16, 112), F32)], axis=1)
    for m in range(16):
        e_send[m] = early[m : m + 1]
    spread_yz(8, lambda peer: e_send.at[peer], e_slots)
    e_slots[yz] = e_send[yz]

    for copy in halos:
        copy.wait_recv()
    for f in range(FIELDS):
        for xs in range(2):
            row = 7 + 17 * xs
            x = 1 + 17 * xs
            for zs in range(2):
                corner = Cr[2 * xs + zs, f : f + 1, :]
                Zr[zs, 1 - zs, f, row : row + 1, :] = corner
                P[f, x, 7 + 17 * zs : 8 + 17 * zs, :] = corner
                Zs[zs, zs, f, row : row + 1, :] = P[f, x, 8 + 15 * zs : 9 + 15 * zs, :]

    def first_edges(wanted):
        def rows(k, carry):
            first(k + 14 * (k // 2), wanted)
            return carry

        lax.fori_loop(0, 4, rows, 0)
        for side in range(2):
            layers = [
                Zr.at[side, side], Zr.at[side, 1 - side], Zs.at[side, side], Zs.at[side, 1 - side]
            ]
            for edge in range(2):
                outer, mid, inside = layers[edge : edge + 3]
                centre = [mid[f, 8:24, :] for f in range(FIELDS)]
                xl = [mid[f, 7:23, :] for f in range(FIELDS)]
                xu = [mid[f, 9:25, :] for f in range(FIELDS)]
                out = [outer[f, 8:24, :] for f in range(FIELDS)]
                within = [inside[f, 8:24, :] for f in range(FIELDS)]
                zl, zu = (out, within) if side == 0 else (within, out)
                z = 7 + edge if side == 0 else 24 - edge
                for f, new in update(centre, xl, xu, zl, zu, profiles, wanted).items():
                    H[f, 1:17, z, :] = new

    first_edges((0, 1, 3))

    wait_all(group_recv, 1, g_slots)
    total = sum_slots_of(g_slots)
    for r in range(8):
        g_mid[r] = total[r : r + 1]
    spread_line(3, lambda peer: g_mid.at[peer], g_mid_slots)
    g_mid_slots[along] = g_mid[along]

    def second(wanted):
        def row(i, carry):
            centre = [H[f, i + 1, 8:24, :] for f in range(FIELDS)]
            xl = [H[f, i, 8:24, :] for f in range(FIELDS)]
            xu = [H[f, i + 2, 8:24, :] for f in range(FIELDS)]
            zl = [H[f, i + 1, 7:23, :] for f in range(FIELDS)]
            zu = [H[f, i + 1, 9:25, :] for f in range(FIELDS)]
            for f, new in update(centre, xl, xu, zl, zu, profiles, wanted).items():
                F[f, i, :, :] = new
            return carry

        lax.fori_loop(0, 16, row, 0)

    second((0,))

    for xg in range(4):
        V[16 * xg : 16 * xg + 16, :] = (H[0, 4 * xg + 1, 8:24, :] + H[0, 4 * xg + 2, 8:24, :]) + (
            H[0, 4 * xg + 3, 8:24, :] + H[0, 4 * xg + 4, 8:24, :]
        )
        V[64 + 16 * xg : 80 + 16 * xg, :] = (F[0, 4 * xg] + F[0, 4 * xg + 1]) + (
            F[0, 4 * xg + 2] + F[0, 4 * xg + 3]
        )
    to = lax.broadcasted_iota(jnp.int32, (128, 128), 0)
    of = lax.broadcasted_iota(jnp.int32, (128, 128), 1)
    wanted = ((lax.rem(of, 16) // 4) * 4 + lax.rem(of, 64) // 16) * 8 + 6 + of // 64
    place_to = (to == wanted).astype(BF16)
    sums = halves(V[...])
    gathered = dot(
        jnp.concatenate([place_to, place_to], axis=1), jnp.concatenate(sums, axis=0)
    )
    block = (
        lax.broadcasted_iota(jnp.int32, (64, 256), 0)
        == lax.broadcasted_iota(jnp.int32, (64, 256), 1) // 4
    ).astype(BF16) * BF16(1.0 / 64.0)
    coarse = dot(
        jnp.concatenate([block, block], axis=1), jnp.concatenate(halves(gathered), axis=1), NT
    )
    for i in range(32):
        late_send[i] = coarse[2 * i : 2 * i + 2]
    spread_z(2, lambda peer: late_send.at[peer], late_slots)
    late_slots[gz] = late_send[gz]

    wait_all(group_recv, 8, e_slots)
    e_mid[...] = sum_slots_of(e_slots)
    spread_line(9, lambda peer: e_mid, e_mid_slots)
    e_mid_slots[along] = e_mid[...]

    wait_all(group_recv, 3, g_mid_slots)
    g_part[...] = sum_slots_of(g_mid_slots)
    spread_line(5, lambda peer: g_part, g_parts)
    g_parts[along] = g_part[...]

    first_edges((2, 4))
    second((1, 2, 3, 4))
    store = pltpu.make_async_copy(F, out_fields, out_sem)
    store.start()

    wait_all(group_recv, 5, g_parts)
    for r in range(8):
        g_whole[r : r + 1, :] = g_parts[r]
    spread_yz(7, lambda peer: g_whole, g_all)
    g_all[yz] = g_whole[...]

    wait_all(group_recv, 9, e_mid_slots)
    e_part[...] = sum_slots_of(e_mid_slots)
    spread_yz(10, lambda peer: e_part, e_all)
    e_all[yz] = e_part[...]

    wait_all(group_recv, 2, late_slots)
    got = jnp.concatenate([late_slots[:, 0, :], late_slots[:, 1, :]], axis=0).T
    for zx in range(16):
        S[8:16, zx * 64 : zx * 64 + 64] = S[8:16, zx * 64 : zx * 64 + 64] + got[zx * 8 : zx * 8 + 8]
    low = S[8:16, :]
    low = jnp.where(lax.broadcasted_iota(jnp.int32, low.shape, 0) >= 6, low, 0.0)
    late = halves(jnp.concatenate([jnp.zeros_like(low), low], axis=0))
    both = dot(jnp.concatenate(late, axis=0), basis_h[...])
    c_late = (both[:16] + both[16:] + dot(late[0], basis_l[...]))[14:16]
    k_late = dot_three(late, halves(S[...]), NT)[14:16]
    late = jnp.concatenate([c_late, k_late, jnp.zeros((2, 112), F32)], axis=1)
    c_send[...] = late
    send_core(4, c_send, c_other)
    wait_one(group_recv, 4, c_other)
    both = late + c_other[...]
    c_mid[...] = both
    spread_chips(6, c_mid, c_slots)
    c_slots[chip] = both

    wait_all(group_recv, 7, g_all)
    every = g_all[...].reshape(128, 384)
    cross = every[:, 128:256]
    metric = jnp.concatenate(
        [every[:, :256], jnp.concatenate([cross.T, every[:, 256:]], axis=1)], axis=0
    ) * (1.0 / rows_total)
    unit = eye(256)
    removed = 4.0 * unit - 6.0 * metric + dot_high(dot_high(metric, metric), 4.0 * unit - metric)
    wait_all(group_recv, 10, e_all)
    early = e_all[...].reshape(16, 384)
    wait_all(group_recv, 6, c_slots)
    total = jnp.concatenate([early[:14], sum_slots_of(c_slots)], axis=0) * (1.0 / rows_total)
    c_one = total[:, :256]
    gram = total[:, 256:272]
    low_row = lax.broadcasted_iota(jnp.int32, (16, 16), 0) >= 14
    low_col = lax.broadcasted_iota(jnp.int32, (16, 16), 1) >= 14
    below = jnp.where(low_row, gram, 0.0)
    size = jnp.where(low_col & ~low_row, below.T, gram)
    gram = size - dot_high(dot_high(c_one, removed), c_one, NT)
    coeffs = 2.0 * c_one - dot_high(c_one, metric)
    out_coeffs[...] = coeffs
    factor_t, inverse, pivots = cholesky(gram + gram_eps * eye(16))
    out_factor[...] = factor_t
    out_inverse[...] = inverse
    diagonal = eye(16) > 0.0
    scale = jnp.sum(jnp.where(diagonal, size, 0.0), axis=0, keepdims=True)
    sound = jnp.where(pivots > least_pivot * scale, 1, 0)
    out_sound[0, 0] = jnp.min(sound)
    out_resid[...] = S[...] - dot_three(halves(coeffs), pair(), NT)

    for copy in halos:
        copy.wait_send()
    for place, slots in (
        (0, early_slots), (1, g_slots), (2, late_slots), (3, g_mid_slots), (5, g_parts),
        (6, c_slots), (7, g_all), (8, e_slots), (9, e_mid_slots), (10, e_all),
    ):
        wait_all(group_send, place, slots)
    wait_one(group_send, 4, c_other)
    store.wait()


def front(sizes, fields, profiles, earlier, basis_view):
    nx, nz = sizes
    vmem = pl.BlockSpec(memory_space=pltpu.VMEM)
    hbm = pl.BlockSpec(memory_space=pltpu.HBM)
    smem = pl.BlockSpec(memory_space=pltpu.SMEM)
    v = pltpu.VMEM
    return pl.pallas_call(
        functools.partial(front_kernel, sizes),
        out_shape=(
            jax.ShapeDtypeStruct(fields.shape, F32),
            jax.ShapeDtypeStruct((16, 256), F32),
            jax.ShapeDtypeStruct((16, 16), F32),
            jax.ShapeDtypeStruct((16, 16), F32),
            jax.ShapeDtypeStruct((1, 1), jnp.int32),
            jax.ShapeDtypeStruct((16, 1024), F32),
        ),
        in_specs=[hbm] * 6,
        out_specs=(hbm, vmem, vmem, vmem, smem, vmem),
        scratch_shapes=[
            v((5, 20, 32, 256), F32),
            v((5, 18, 32, 256), F32),
            v((5, 16, 16, 256), F32),
            v((2, 2, 5, 32, 256), F32),
            v((2, 2, 5, 32, 256), F32),
            v((4, 8, 256), F32),
            v((4, 8, 256), F32),
            v((128, 256), F32),
            v((2048, 128), F32),
            v((1024, 256), F32),
            v((1024, 256), BF16),
            v((1024, 256), BF16),
            v((64, 256), F32),
            v((32, 2, 256), F32),
            v((32, 2, 256), F32),
            v((32, 2, 128), F32),
            v((32, 2, 128), F32),
            v((16, 1024), F32),
            v((16, 8, 384), F32),
            v((16, 8, 384), F32),
            v((8, 1, 384), F32),
            v((8, 1, 384), F32),
            v((1, 384), F32),
            v((8, 1, 384), F32),
            v((8, 384), F32),
            v((16, 8, 384), F32),
            v((16, 1, 384), F32),
            v((16, 1, 384), F32),
            v((1, 384), F32),
            v((8, 1, 384), F32),
            v((1, 384), F32),
            v((16, 1, 384), F32),
            v((2, 384), F32),
            v((2, 384), F32),
            v((2, 384), F32),
            v((64, 2, 384), F32),
            v((14, 4, 256), F32),
            v((3, 1, 256), F32),
            pltpu.SemaphoreType.DMA((4,)),
            pltpu.SemaphoreType.DMA,
            pltpu.SemaphoreType.DMA,
            pltpu.SemaphoreType.DMA,
            pltpu.SemaphoreType.DMA((8,)),
            pltpu.SemaphoreType.DMA((8,)),
            pltpu.SemaphoreType.DMA((11,)),
            pltpu.SemaphoreType.DMA((11,)),
        ],
        compiler_params=pltpu.CompilerParams(
            collective_id=0, has_side_effects=True, vmem_limit_bytes=62 * 1024 * 1024
        ),
    )(fields, *profiles, earlier, basis_view)


def direct_factor(resid):
    rows_total = 1024.0 * lax.axis_size("gx") * lax.axis_size("gz")
    gram = lax.psum(jnp.dot(resid, resid.T, precision=HIGH), ("gx", "gz")) / rows_total
    identity = jnp.eye(16, dtype=F32)
    factor = jnp.linalg.cholesky(gram + gram_eps * identity)
    return factor.T, jax.scipy.linalg.solve_triangular(factor, identity, lower=True)


def on_device(fields, courant, shear_rate, gradient, earlier, basis_modes, core_matrix):
    sizes = (lax.axis_size("gx"), lax.axis_size("gz"))
    view = view_of(basis_modes)
    profiles = [p.reshape(1, -1) for p in (courant, shear_rate, gradient)]
    finished, coeffs, factor_t, inverse, sound, resid = front(
        sizes, fields, profiles, earlier, view
    )
    factor_t, inverse = lax.cond(
        sound[0, 0] > 0,
        lambda resid, factor_t, inverse: (factor_t, inverse),
        lambda resid, factor_t, inverse: direct_factor(resid),
        resid, factor_t, inverse,
    )
    finished, new_view, new_core = tail(
        core_matrix, coeffs, factor_t, inverse, resid, view, finished
    )
    return (finished, basis_of(new_view), new_core)


def solution(mesh):
    return jax.shard_map(
        on_device,
        mesh=mesh,
        in_specs=(
            P(None, "gx", "gz", None),
            P(),
            P(),
            P(),
            P(None, "gx", "gz"),
            P("gx", None, "gz", None),
            P(),
        ),
        out_specs=(P(None, "gx", "gz", None), P("gx", None, "gz", None), P()),
        check_vma=False,
    )
```

```python
import functools

import jax
import jax.numpy as jnp
from jax import lax
from jax.experimental import pallas as pl
from jax.experimental.pallas import tpu as pltpu
from jax.sharding import PartitionSpec as P

F32, BF16 = jnp.float32, jnp.bfloat16
HIGH = lax.Precision.HIGHEST
SIGN_STEPS = 10
POLAR_STEPS = 3
gram_eps = 1e-06


def halves(values):
    head = values.astype(BF16)
    return head, (values - head.astype(F32)).astype(BF16)


def dot(left, right, over=((1,), (0,))):
    return lax.dot_general(left, right, (over, ((), ())), preferred_element_type=F32)


def dot_three(left, right, over=((1,), (0,))):
    (lh, ll), (rh, rl) = left, right
    return dot(lh, rh, over) + (dot(lh, rl, over) + dot(ll, rh, over))


def dot_high(left, right, over=((1,), (0,))):
    return lax.dot_general(
        left, right, (over, ((), ())), precision=HIGH, preferred_element_type=F32
    )


TN = ((0,), (0,))
NT = ((1,), (1,))


def tripled_left(pair):
    return jnp.concatenate([pair[0], pair[0], pair[1]], axis=0)


def tripled_right(pair):
    return jnp.concatenate([pair[0], pair[1], pair[0]], axis=0)


def eye(count):
    return (
        lax.broadcasted_iota(jnp.int32, (count, count), 0)
        == lax.broadcasted_iota(jnp.int32, (count, count), 1)
    ).astype(F32)


def row_places(z_lanes):
    places = []
    for zc in range(4):
        for x in range(4):
            for y in range(2):
                places.append((zc, x, y))
    return places


def take_basis(view_ref, rows_ref):
    for place, (zc, x, y) in enumerate(row_places(0)):
        for half in range(2):
            rows_ref[pl.ds(place * 32, 32), pl.ds(half * 128, 128)] = view_ref[
                pl.ds(512 * x + 4 * zc + 2 * half + y, 32, stride=16), :
            ]


def give_basis(rows, view_ref, first):
    for step in range(8):
        zc, x, y = row_places(0)[first + step]
        for half in range(2):
            view_ref[pl.ds(512 * x + 4 * zc + 2 * half + y, 32, stride=16), :] = rows[
                step * 32 : step * 32 + 32, half * 128 : half * 128 + 128
            ]


def eliminate(left, right, pivots, columns):
    row_index = lax.broadcasted_iota(jnp.int32, left.shape, 0)
    col_index = lax.broadcasted_iota(jnp.int32, pivots.shape, 1)
    for j in columns:
        pivot = left[j : j + 1, j : j + 1]
        pivots = jnp.where(col_index == j, pivot, pivots)
        scale = lax.rsqrt(pivot)
        scale = scale * (1.5 - 0.5 * pivot * scale * scale)
        column = left[:, j : j + 1] * scale
        row_l = left[j : j + 1, :] * scale
        row_r = right[j : j + 1, :] * scale
        below = row_index > j
        here = row_index == j
        left = jnp.where(below, left - column * row_l, jnp.where(here, row_l, left))
        right = jnp.where(below, right - column * row_r, jnp.where(here, row_r, right))
    return left, right, pivots


def wide_left(v, d):
    modes = v.shape[1]
    vh, vl = halves(v)
    dh, dl = halves(d)
    bh, bl = vh[modes:].astype(F32), vl[modes:].astype(F32)
    turned = jnp.concatenate([bh, bh, bl], axis=0).T.astype(BF16)
    edge = jnp.concatenate([turned, jnp.concatenate([dh, dh, dl], axis=1)], axis=0)
    return vh, vl, edge, jnp.concatenate([vh[modes:], vh[modes:], vl[modes:], edge[modes:]], axis=1)


def product(left, right_v, right_d):
    modes = right_v.shape[1]
    rh, rl = halves(right_v)
    dh, dl = halves(right_d)
    ah, bh = rh[:modes], rh[modes:]
    al, bl = rl[:modes], rl[modes:]
    stacked = jnp.concatenate([ah, al, ah, bh, bl, bh], axis=0)
    low = jnp.concatenate([bh, bl, bh, dh, dl, dh], axis=1)
    vh, vl, edge, wide = left
    thin = jnp.concatenate([bh, bl, bh], axis=0)
    top = (dot(vh[:modes], ah) + dot(vh[:modes], al)) + (dot(vl[:modes], ah) + dot(edge[:modes], thin))
    bottom = dot(wide, jnp.concatenate([ah, al, ah, thin], axis=0))
    return jnp.concatenate([top, bottom], axis=0), dot(wide, low, NT)


def tail_kernel(core_ref, coeffs_ref, factor_ref, inverse_ref, snaps_ref, basis_hbm, fields_hbm,
                out_fields, out_basis, out_core, v_ref, d_ref, basis_view, basis_rows, held, sem, field_sem):
    modes = core_ref.shape[0]
    fetch = pltpu.make_async_copy(basis_hbm, basis_view, sem)
    fetch.start()
    taking = pltpu.make_async_copy(fields_hbm, held, field_sem)
    taking.start()
    factor_t = factor_ref[...]
    inverse = inverse_ref[...]
    coeffs = coeffs_ref[...]
    unit = eye(modes)
    unit_d = eye(16)
    parts = halves(coeffs)
    corr_a = core_ref[...] + dot(tripled_left(parts), tripled_right(parts), TN)
    corr_b = dot_high(factor_t, coeffs)
    corr_d = dot_high(factor_t, factor_t, NT)
    shift_a = corr_a - unit
    shift_d = corr_d - unit_d
    total = (
        jnp.sum(shift_a * shift_a, keepdims=True)
        + 2.0 * jnp.sum(corr_b * corr_b, keepdims=True)
        + jnp.sum(shift_d * shift_d, keepdims=True)
    )
    scale = 1.0 / jnp.sqrt(total)
    v_ref[:modes] = shift_a * scale
    v_ref[modes:] = corr_b * scale
    d_ref[...] = shift_d * scale
    unit_v = jnp.concatenate([unit, jnp.zeros((16, modes), F32)], axis=0)

    def sign_step(step, carry):
        v = v_ref[...]
        d = d_ref[...]
        left = wide_left(v, d)
        square_v, square_d = product(left, v, d)
        next_v, next_d = product(
            left, 1.5 * unit_v - 0.5 * square_v, 1.5 * unit_d - 0.5 * square_d
        )
        v_ref[...] = next_v
        d_ref[...] = next_d
        return carry

    lax.fori_loop(0, SIGN_STEPS, sign_step, 0)

    fetch.wait()
    taking.wait()
    passing = pltpu.make_async_copy(held, out_fields, field_sem)
    passing.start()
    take_basis(basis_view, basis_rows)

    rot = 0.5 * (unit_v + v_ref[...])
    pair = halves(rot)
    top = (pair[0][:modes], pair[1][:modes])
    low = (pair[0][modes:], pair[1][modes:])
    inner = dot_three(top, top) + dot(tripled_left(low), tripled_right(low), TN)
    for step in range(POLAR_STEPS):
        factor = 1.5 * unit - 0.5 * inner
        fp = halves(factor)
        rot = dot_three(halves(rot), fp)
        if step < POLAR_STEPS - 1:
            inner = dot_three(halves(dot_three(halves(inner), fp)), fp)
    rp = halves(rot)
    corr_v = jnp.concatenate([corr_a, corr_b], axis=0)
    moved = dot_three(halves(corr_v), (rp[0][:modes], rp[1][:modes]))
    rb48 = tripled_right((rp[0][modes:], rp[1][modes:]))
    moved = moved + jnp.concatenate(
        [
            dot(tripled_left(halves(corr_b)), rb48, TN),
            dot(tripled_left(halves(corr_d)), rb48, TN),
        ],
        axis=0,
    )
    out_core[...] = dot_three(rp, halves(moved), TN)

    mix = dot_high(inverse, rot[modes:], TN)
    mix48 = tripled_right(halves(mix))
    ra = halves(rot[:modes] - dot(tripled_left(parts), mix48, TN))
    for part in range(4):
        rows = basis_rows[pl.ds(part * 256, 256), :]
        left = tripled_left(halves(snaps_ref[:, part * 256 : part * 256 + 256]))
        give_basis(dot_three(halves(rows), ra) + dot(left, mix48, TN), out_basis, part * 8)
    passing.wait()


def tail(core, coeffs, factor_t, inverse, snaps, basis_view, fields):
    vmem = pl.BlockSpec(memory_space=pltpu.VMEM)
    hbm = pl.BlockSpec(memory_space=pltpu.HBM)
    return pl.pallas_call(
        tail_kernel,
        out_shape=(
            jax.ShapeDtypeStruct(fields.shape, F32),
            jax.ShapeDtypeStruct((2048, 128), F32),
            jax.ShapeDtypeStruct((256, 256), F32),
        ),
        in_specs=[vmem, vmem, vmem, vmem, vmem, hbm, hbm],
        out_specs=(hbm, vmem, vmem),
        scratch_shapes=[
            pltpu.VMEM((272, 256), F32),
            pltpu.VMEM((16, 16), F32),
            pltpu.VMEM((2048, 128), F32),
            pltpu.VMEM((1024, 256), F32),
            pltpu.VMEM(fields.shape, F32),
            pltpu.SemaphoreType.DMA,
            pltpu.SemaphoreType.DMA,
        ],
        compiler_params=pltpu.CompilerParams(vmem_limit_bytes=60 * 1024 * 1024),
    )(core, coeffs, factor_t, inverse, snaps, basis_view, fields)


def view_of(basis):
    return basis.reshape(4, 128, 2, 2, 128).transpose(0, 1, 3, 2, 4).reshape(2048, 128)


def basis_of(view):
    return view.reshape(4, 128, 2, 2, 128).transpose(0, 1, 3, 2, 4).reshape(4, 128, 2, 256)


MESH = pl.DeviceIdType.MESH
press_coef = 0.25
compress_coef = 0.25
visc_coef = 0.05
heat_coef = 0.03
FIELDS = 5
least_pivot = 2.0**-7


def shifted(values):
    width = values.shape[-1]
    lane = lax.broadcasted_iota(jnp.int32, values.shape, 1)
    lower = jnp.where(lane == 0, 0.0, pltpu.roll(values, 1, 1))
    upper = jnp.where(lane == width - 1, 0.0, pltpu.roll(values, width - 1, 1))
    return lower, upper


def update(centre, xl, xu, zl, zu, profiles, wanted=range(FIELDS)):
    courant, shear_rate, gradient = profiles
    beside = [shifted(c) for c in centre]
    keep = [1.0 - 6.0 * visc_coef - courant] * 3 + [1.0 - 6.0 * visc_coef]
    keep = keep + [1.0 - 6.0 * heat_coef - courant]
    bring = [visc_coef + courant] * 3 + [visc_coef, heat_coef + courant]
    spread = [visc_coef] * 4 + [heat_coef]
    half_press = 0.5 * press_coef
    divergence = (xu[0] - xl[0]) + (beside[1][1] - beside[1][0]) + (zu[2] - zl[2])
    sources = [
        shear_rate * centre[1] + half_press * (xu[3] - xl[3]),
        half_press * (beside[3][1] - beside[3][0]),
        half_press * (zu[3] - zl[3]),
        0.5 * compress_coef * divergence,
        gradient * centre[1],
    ]
    new = {}
    for f in wanted:
        around = (xu[f] + zl[f]) + (zu[f] + beside[f][0]) + beside[f][1]
        new[f] = keep[f] * centre[f] + bring[f] * xl[f] + spread[f] * around - sources[f]
    return new


def front_kernel(sizes, fields_hbm, courant_hbm, shear_hbm, gradient_hbm, earlier_hbm, basis_hbm,
                 out_fields, out_coeffs, out_factor, out_inverse, out_sound, out_snaps,
                 P, H, F, Zs, Zr, Cs, Cr, V, basis_view, basis_rows, basis_h, basis_l,
                 E2, early_send, early_slots, late_send, late_slots, S,
                 g_send, g_slots, g_mid, g_mid_slots, g_part, g_parts, g_whole, g_all,
                 e_send, e_slots, e_mid, e_mid_slots, e_part, e_all,
                 c_send, c_other, c_mid, c_slots,
                 earlier_ref, profile_rows, small_sem, load_sem, basis_sem, out_sem, halo_send, halo_recv,
                 group_send, group_recv):
    nx, nz = sizes
    gx = lax.axis_index("gx")
    gz = lax.axis_index("gz")
    rows_total = 1024.0 * nx * nz

    barrier = pltpu.get_barrier_semaphore()
    x_beside = (lax.rem(gx + nx - 1, nx), lax.rem(gx + 1, nx))
    z_beside = (lax.rem(gz + nz - 1, nz), lax.rem(gz + 1, nz))

    def greet(where):
        pl.semaphore_signal(barrier, inc=1, device_id=where, device_id_type=MESH)

    def greet_z(d, carry):
        greet((gx, lax.rem(gz + d, nz)))
        return carry

    load = pltpu.make_async_copy(fields_hbm, P.at[:, 2:18, 8:24, :], load_sem)
    load.start()
    fetch = pltpu.make_async_copy(basis_hbm, basis_view, basis_sem)
    fetch.start()
    small = [
        pltpu.make_async_copy(earlier_hbm, earlier_ref, small_sem.at[0]),
        pltpu.make_async_copy(courant_hbm, profile_rows.at[0], small_sem.at[1]),
        pltpu.make_async_copy(shear_hbm, profile_rows.at[1], small_sem.at[2]),
        pltpu.make_async_copy(gradient_hbm, profile_rows.at[2], small_sem.at[3]),
    ]
    for copy in small:
        copy.start()
    for d in range(1, nx):
        greet((lax.rem(gx + d, nx), gz))
    for xs in range(2):
        for zs in range(2):
            greet((x_beside[xs], z_beside[zs]))
    for d in range(1, nx):
        greet((lax.rem(gx + d, nx), gz + 1 - 2 * lax.rem(gz, 2)))
    lax.fori_loop(1, nz, greet_z, 0)

    for copy in small:
        copy.wait()
    E2[...] = jnp.zeros_like(E2)
    for m in range(14):
        for x in range(4):
            E2[x * 16 + m : x * 16 + m + 1, :] = earlier_ref[m, x : x + 1, :]
    turned = E2[...].T
    turned = jnp.concatenate([turned[64 * z : 64 * z + 64] for z in range(4)], axis=1)
    for i in range(32):
        early_send[i] = turned[2 * i : 2 * i + 2]
    pl.semaphore_wait(barrier, nz - 1 + 2 * (nx - 1) + 4)

    def spread_z(place, source, slots):
        def body(d, carry):
            peer = lax.rem(gz + d, nz)
            pltpu.make_async_remote_copy(
                src_ref=source(peer), dst_ref=slots.at[gz], send_sem=group_send.at[place],
                recv_sem=group_recv.at[place], device_id=(gx, peer), device_id_type=MESH,
            ).start()
            return carry

        lax.fori_loop(1, nz, body, 0)

    spread_z(0, lambda peer: early_send.at[peer], early_slots)
    early_slots[gz] = early_send[gz]

    load.wait()

    halos = []

    def send_halo(source, target, where):
        place = len(halos)
        copy = pltpu.make_async_remote_copy(
            src_ref=source, dst_ref=target, send_sem=halo_send.at[place],
            recv_sem=halo_recv.at[place], device_id=where, device_id_type=MESH,
        )
        copy.start()
        halos.append(copy)

    for side in range(2):
        send_halo(
            P.at[:, 2 + 14 * side : 4 + 14 * side, 8:24, :],
            P.at[:, 18 - 18 * side : 20 - 18 * side, 8:24, :],
            (x_beside[side], gz),
        )

    for side in range(2):
        for layer in range(2):
            z = 8 + 14 * side + layer
            for f in range(FIELDS):
                for half in range(2):
                    lanes = pl.ds(128 * half, 128)
                    Zs[side, layer, f, 8:24, lanes] = P[f, 2:18, z, lanes]
    for xs in range(2):
        for zs in range(2):
            for f in range(FIELDS):
                Cs[2 * xs + zs, f : f + 1, :] = P[f, 2 + 15 * xs, 8 + 15 * zs : 9 + 15 * zs, :]

    for side in range(2):
        send_halo(Zs.at[side, :, :, 8:24, :], Zr.at[1 - side, :, :, 8:24, :], (gx, z_beside[side]))
    for xs in range(2):
        for zs in range(2):
            send_halo(
                Cs.at[2 * xs + zs], Cr.at[2 * (1 - xs) + 1 - zs], (x_beside[xs], z_beside[zs])
            )

    yz = gz // 2
    places = nz // 2
    along = (lax.rem(gz, 2) * (nx // 2) + gx // 2) * 2 + lax.rem(gx, 2)
    line = 2 * nx

    def spread_yz(place, source, slots):
        def body(d, carry):
            peer = lax.rem(yz + d, places)
            pltpu.make_async_remote_copy(
                src_ref=source(peer), dst_ref=slots.at[yz], send_sem=group_send.at[place],
                recv_sem=group_recv.at[place], device_id=(gx, 2 * peer + lax.rem(gz, 2)),
                device_id_type=MESH,
            ).start()
            return carry

        lax.fori_loop(1, places, body, 0)

    def spread_line(place, source, slots):
        def body(d, carry):
            peer = lax.rem(along + d, line)
            where = (lax.rem(peer, nx), 2 * yz + peer // nx)
            pltpu.make_async_remote_copy(
                src_ref=source(peer), dst_ref=slots.at[along], send_sem=group_send.at[place],
                recv_sem=group_recv.at[place], device_id=where, device_id_type=MESH,
            ).start()
            return carry

        lax.fori_loop(1, line, body, 0)

    core = lax.rem(gx, 2)
    chip = (gx // 2) * nz + gz
    chips = (nx // 2) * nz

    def send_core(place, source, target):
        pltpu.make_async_remote_copy(
            src_ref=source, dst_ref=target, send_sem=group_send.at[place],
            recv_sem=group_recv.at[place], device_id=(gx + 1 - 2 * core, gz), device_id_type=MESH,
        ).start()

    def spread_chips(place, source, slots):
        def body(d, carry):
            peer = lax.rem(chip + d, chips)
            where = (2 * (peer // nz) + core, lax.rem(peer, nz))
            pltpu.make_async_remote_copy(
                src_ref=source, dst_ref=slots.at[chip], send_sem=group_send.at[place],
                recv_sem=group_recv.at[place], device_id=where, device_id_type=MESH,
            ).start()
            return carry

        lax.fori_loop(1, chips, body, 0)

    def wait_one(sems, place, part):
        pltpu.make_async_copy(part, part, sems.at[place]).wait()

    def sum_slots_of(slots):
        terms = [slots[j] for j in range(slots.shape[0])]
        while len(terms) > 1:
            terms = [a + b for a, b in zip(terms[::2], terms[1::2])] + terms[len(terms) & ~1 :]
        return terms[0]

    def wait_all(sems, place, slots):
        some = slots.at[pl.ds(0, slots.shape[0] - 1)]
        pltpu.make_async_copy(some, some, sems.at[place]).wait()

    fetch.wait()
    take_basis(basis_view, basis_rows)
    rows = basis_rows[...]
    head = rows.astype(BF16)
    basis_h[...] = head
    basis_l[...] = (rows - head.astype(F32)).astype(BF16)

    def pair():
        return basis_h[...], basis_l[...]

    inner = dot_three(pair(), pair(), TN)
    for i in range(16):
        g_send[i, :, :256] = inner[8 * i : 8 * i + 8]
        g_send[i, :, 256:] = inner[128 + 8 * i : 136 + 8 * i, 128:]
    spread_yz(1, lambda peer: g_send.at[peer], g_slots)
    g_slots[yz] = g_send[yz]

    profiles = [profile_rows[k] for k in range(3)]

    def first(i, wanted=range(FIELDS)):
        centre = [P[f, i + 1, 8:24, :] for f in range(FIELDS)]
        xl = [P[f, i, 8:24, :] for f in range(FIELDS)]
        xu = [P[f, i + 2, 8:24, :] for f in range(FIELDS)]
        zl = [P[f, i + 1, 7:23, :] for f in range(FIELDS)]
        zu = [P[f, i + 1, 9:25, :] for f in range(FIELDS)]
        for f, new in update(centre, xl, xu, zl, zu, profiles, wanted).items():
            H[f, i, 8:24, :] = new

    def first_inside(i, carry):
        first(i)
        return carry

    lax.fori_loop(2, 16, first_inside, 0)

    wait_all(group_recv, 0, early_slots)
    got = jnp.concatenate([early_slots[:, 0, :], early_slots[:, 1, :]], axis=0).T
    for zx in range(16):
        S[:, zx * 64 : zx * 64 + 64] = got[zx * 16 : zx * 16 + 16]
    snaps = halves(S[...])
    c_early = dot_three(snaps, pair())
    k_early = dot_three(snaps, snaps, NT)
    early = jnp.concatenate([c_early, k_early, jnp.zeros((16, 112), F32)], axis=1)
    for m in range(16):
        e_send[m] = early[m : m + 1]
    spread_yz(8, lambda peer: e_send.at[peer], e_slots)
    e_slots[yz] = e_send[yz]

    for copy in halos:
        copy.wait_recv()
    for f in range(FIELDS):
        for xs in range(2):
            row = 7 + 17 * xs
            x = 1 + 17 * xs
            for zs in range(2):
                corner = Cr[2 * xs + zs, f : f + 1, :]
                Zr[zs, 1 - zs, f, row : row + 1, :] = corner
                P[f, x, 7 + 17 * zs : 8 + 17 * zs, :] = corner
                Zs[zs, zs, f, row : row + 1, :] = P[f, x, 8 + 15 * zs : 9 + 15 * zs, :]

    def first_edges(wanted):
        def rows(k, carry):
            first(k + 14 * (k // 2), wanted)
            return carry

        lax.fori_loop(0, 4, rows, 0)
        for side in range(2):
            layers = [
                Zr.at[side, side], Zr.at[side, 1 - side], Zs.at[side, side], Zs.at[side, 1 - side]
            ]
            for edge in range(2):
                outer, mid, inside = layers[edge : edge + 3]
                centre = [mid[f, 8:24, :] for f in range(FIELDS)]
                xl = [mid[f, 7:23, :] for f in range(FIELDS)]
                xu = [mid[f, 9:25, :] for f in range(FIELDS)]
                out = [outer[f, 8:24, :] for f in range(FIELDS)]
                within = [inside[f, 8:24, :] for f in range(FIELDS)]
                zl, zu = (out, within) if side == 0 else (within, out)
                z = 7 + edge if side == 0 else 24 - edge
                for f, new in update(centre, xl, xu, zl, zu, profiles, wanted).items():
                    H[f, 1:17, z, :] = new

    first_edges((0, 1, 3))

    wait_all(group_recv, 1, g_slots)
    total = sum_slots_of(g_slots)
    for r in range(8):
        g_mid[r] = total[r : r + 1]
    spread_line(3, lambda peer: g_mid.at[peer], g_mid_slots)
    g_mid_slots[along] = g_mid[along]

    def second(wanted):
        def row(i, carry):
            centre = [H[f, i + 1, 8:24, :] for f in range(FIELDS)]
            xl = [H[f, i, 8:24, :] for f in range(FIELDS)]
            xu = [H[f, i + 2, 8:24, :] for f in range(FIELDS)]
            zl = [H[f, i + 1, 7:23, :] for f in range(FIELDS)]
            zu = [H[f, i + 1, 9:25, :] for f in range(FIELDS)]
            for f, new in update(centre, xl, xu, zl, zu, profiles, wanted).items():
                F[f, i, :, :] = new
            return carry

        lax.fori_loop(0, 16, row, 0)

    second((0,))

    for xg in range(4):
        V[16 * xg : 16 * xg + 16, :] = (H[0, 4 * xg + 1, 8:24, :] + H[0, 4 * xg + 2, 8:24, :]) + (
            H[0, 4 * xg + 3, 8:24, :] + H[0, 4 * xg + 4, 8:24, :]
        )
        V[64 + 16 * xg : 80 + 16 * xg, :] = (F[0, 4 * xg] + F[0, 4 * xg + 1]) + (
            F[0, 4 * xg + 2] + F[0, 4 * xg + 3]
        )
    to = lax.broadcasted_iota(jnp.int32, (128, 128), 0)
    of = lax.broadcasted_iota(jnp.int32, (128, 128), 1)
    wanted = ((lax.rem(of, 16) // 4) * 4 + lax.rem(of, 64) // 16) * 8 + 6 + of // 64
    place_to = (to == wanted).astype(BF16)
    sums = halves(V[...])
    gathered = dot(
        jnp.concatenate([place_to, place_to], axis=1), jnp.concatenate(sums, axis=0)
    )
    block = (
        lax.broadcasted_iota(jnp.int32, (64, 256), 0)
        == lax.broadcasted_iota(jnp.int32, (64, 256), 1) // 4
    ).astype(BF16) * BF16(1.0 / 64.0)
    coarse = dot(
        jnp.concatenate([block, block], axis=1), jnp.concatenate(halves(gathered), axis=1), NT
    )
    for i in range(32):
        late_send[i] = coarse[2 * i : 2 * i + 2]
    spread_z(2, lambda peer: late_send.at[peer], late_slots)
    late_slots[gz] = late_send[gz]

    wait_all(group_recv, 8, e_slots)
    e_mid[...] = sum_slots_of(e_slots)
    spread_line(9, lambda peer: e_mid, e_mid_slots)
    e_mid_slots[along] = e_mid[...]

    wait_all(group_recv, 3, g_mid_slots)
    g_part[...] = sum_slots_of(g_mid_slots)
    spread_line(5, lambda peer: g_part, g_parts)
    g_parts[along] = g_part[...]

    first_edges((2, 4))
    second((1, 2, 3, 4))
    store = pltpu.make_async_copy(F, out_fields, out_sem)
    store.start()

    wait_all(group_recv, 5, g_parts)
    for r in range(8):
        g_whole[r : r + 1, :] = g_parts[r]
    spread_yz(7, lambda peer: g_whole, g_all)
    g_all[yz] = g_whole[...]

    wait_all(group_recv, 9, e_mid_slots)
    e_part[...] = sum_slots_of(e_mid_slots)
    spread_yz(10, lambda peer: e_part, e_all)
    e_all[yz] = e_part[...]

    wait_all(group_recv, 2, late_slots)
    got = jnp.concatenate([late_slots[:, 0, :], late_slots[:, 1, :]], axis=0).T
    for zx in range(16):
        S[8:16, zx * 64 : zx * 64 + 64] = S[8:16, zx * 64 : zx * 64 + 64] + got[zx * 8 : zx * 8 + 8]
    out_snaps[...] = S[...]
    low = S[8:16, :]
    low = jnp.where(lax.broadcasted_iota(jnp.int32, low.shape, 0) >= 6, low, 0.0)
    late = halves(jnp.concatenate([jnp.zeros_like(low), low], axis=0))
    both = dot(jnp.concatenate(late, axis=0), basis_h[...])
    c_late = (both[:16] + both[16:] + dot(late[0], basis_l[...]))[14:16]
    k_late = dot_three(late, halves(S[...]), NT)[14:16]
    late = jnp.concatenate([c_late, k_late, jnp.zeros((2, 112), F32)], axis=1)
    c_send[...] = late
    send_core(4, c_send, c_other)
    wait_one(group_recv, 4, c_other)
    both = late + c_other[...]
    c_mid[...] = both
    spread_chips(6, c_mid, c_slots)
    c_slots[chip] = both

    wait_all(group_recv, 7, g_all)
    every = g_all[...].reshape(128, 384)
    cross = every[:, 128:256]
    metric = jnp.concatenate(
        [every[:, :256], jnp.concatenate([cross.T, every[:, 256:]], axis=1)], axis=0
    ) * (1.0 / rows_total)
    unit = eye(256)
    removed = 4.0 * unit - 6.0 * metric + dot_high(dot_high(metric, metric), 4.0 * unit - metric)
    wait_all(group_recv, 10, e_all)
    early = e_all[...].reshape(16, 384) * (1.0 / rows_total)
    c_early = early[:, :256]
    identity = eye(16)
    gram = early[:, 256:272] - dot_high(dot_high(c_early, removed), c_early, NT)
    left, right, pivots = eliminate(
        gram + gram_eps * identity, identity, jnp.zeros((1, 16), F32), range(14)
    )
    low_row = lax.broadcasted_iota(jnp.int32, (16, 16), 0) >= 14
    low_col = lax.broadcasted_iota(jnp.int32, (16, 16), 1) >= 14

    wait_all(group_recv, 6, c_slots)
    total = jnp.concatenate([early[:14], sum_slots_of(c_slots) * (1.0 / rows_total)], axis=0)
    c_one = total[:, :256]
    size = total[:, 256:272]
    out_coeffs[...] = 2.0 * c_one - dot_high(c_one, metric)
    gram = size - dot_high(dot_high(c_one, removed), c_one, NT) + gram_eps * identity
    across = dot_high(jnp.where(low_row & ~low_col, gram, 0.0), right, NT)
    corner = jnp.where(low_row & low_col, gram, 0.0) - dot_high(across, across, NT)
    left, right, pivots = eliminate(
        jnp.where(low_row, corner, left + across.T), right - dot_high(across, right), pivots,
        range(14, 16),
    )
    upper = lax.broadcasted_iota(jnp.int32, (16, 16), 0) <= lax.broadcasted_iota(
        jnp.int32, (16, 16), 1
    )
    out_factor[...] = jnp.where(upper, left, 0.0)
    out_inverse[...] = right
    scale = jnp.sum(jnp.where(identity > 0.0, size, 0.0), axis=0, keepdims=True)
    sound = jnp.where(pivots > least_pivot * scale, 1, 0)
    out_sound[0, 0] = jnp.min(sound)

    for copy in halos:
        copy.wait_send()
    for place, slots in (
        (0, early_slots), (1, g_slots), (2, late_slots), (3, g_mid_slots), (5, g_parts),
        (6, c_slots), (7, g_all), (8, e_slots), (9, e_mid_slots), (10, e_all),
    ):
        wait_all(group_send, place, slots)
    wait_one(group_send, 4, c_other)
    store.wait()


def front(sizes, fields, profiles, earlier, basis_view):
    nx, nz = sizes
    vmem = pl.BlockSpec(memory_space=pltpu.VMEM)
    hbm = pl.BlockSpec(memory_space=pltpu.HBM)
    smem = pl.BlockSpec(memory_space=pltpu.SMEM)
    v = pltpu.VMEM
    return pl.pallas_call(
        functools.partial(front_kernel, sizes),
        out_shape=(
            jax.ShapeDtypeStruct(fields.shape, F32),
            jax.ShapeDtypeStruct((16, 256), F32),
            jax.ShapeDtypeStruct((16, 16), F32),
            jax.ShapeDtypeStruct((16, 16), F32),
            jax.ShapeDtypeStruct((1, 1), jnp.int32),
            jax.ShapeDtypeStruct((16, 1024), F32),
        ),
        in_specs=[hbm] * 6,
        out_specs=(hbm, vmem, vmem, vmem, smem, vmem),
        scratch_shapes=[
            v((5, 20, 32, 256), F32),
            v((5, 18, 32, 256), F32),
            v((5, 16, 16, 256), F32),
            v((2, 2, 5, 32, 256), F32),
            v((2, 2, 5, 32, 256), F32),
            v((4, 8, 256), F32),
            v((4, 8, 256), F32),
            v((128, 256), F32),
            v((2048, 128), F32),
            v((1024, 256), F32),
            v((1024, 256), BF16),
            v((1024, 256), BF16),
            v((64, 256), F32),
            v((32, 2, 256), F32),
            v((32, 2, 256), F32),
            v((32, 2, 128), F32),
            v((32, 2, 128), F32),
            v((16, 1024), F32),
            v((16, 8, 384), F32),
            v((16, 8, 384), F32),
            v((8, 1, 384), F32),
            v((8, 1, 384), F32),
            v((1, 384), F32),
            v((8, 1, 384), F32),
            v((8, 384), F32),
            v((16, 8, 384), F32),
            v((16, 1, 384), F32),
            v((16, 1, 384), F32),
            v((1, 384), F32),
            v((8, 1, 384), F32),
            v((1, 384), F32),
            v((16, 1, 384), F32),
            v((2, 384), F32),
            v((2, 384), F32),
            v((2, 384), F32),
            v((64, 2, 384), F32),
            v((14, 4, 256), F32),
            v((3, 1, 256), F32),
            pltpu.SemaphoreType.DMA((4,)),
            pltpu.SemaphoreType.DMA,
            pltpu.SemaphoreType.DMA,
            pltpu.SemaphoreType.DMA,
            pltpu.SemaphoreType.DMA((8,)),
            pltpu.SemaphoreType.DMA((8,)),
            pltpu.SemaphoreType.DMA((11,)),
            pltpu.SemaphoreType.DMA((11,)),
        ],
        compiler_params=pltpu.CompilerParams(
            collective_id=0, has_side_effects=True, vmem_limit_bytes=62 * 1024 * 1024
        ),
    )(fields, *profiles, earlier, basis_view)


def direct_factor(snaps, coeffs, basis_modes):
    rows_total = 1024.0 * lax.axis_size("gx") * lax.axis_size("gz")
    rows = basis_modes.reshape(4, 32, 4, 2, 256).transpose(2, 0, 3, 1, 4).reshape(1024, 256)
    resid = snaps - jnp.dot(coeffs, rows.T, precision=HIGH)
    gram = lax.psum(jnp.dot(resid, resid.T, precision=HIGH), ("gx", "gz")) / rows_total
    identity = jnp.eye(16, dtype=F32)
    factor = jnp.linalg.cholesky(gram + gram_eps * identity)
    return factor.T, jax.scipy.linalg.solve_triangular(factor, identity, lower=True)


def on_device(fields, courant, shear_rate, gradient, earlier, basis_modes, core_matrix):
    sizes = (lax.axis_size("gx"), lax.axis_size("gz"))
    view = view_of(basis_modes)
    profiles = [p.reshape(1, -1) for p in (courant, shear_rate, gradient)]
    finished, coeffs, factor_t, inverse, sound, snaps = front(
        sizes, fields, profiles, earlier, view
    )
    factor_t, inverse = lax.cond(
        sound[0, 0] > 0,
        lambda snaps, coeffs, basis_modes, factor_t, inverse: (factor_t, inverse),
        lambda snaps, coeffs, basis_modes, factor_t, inverse: direct_factor(
            snaps, coeffs, basis_modes
        ),
        snaps, coeffs, basis_modes, factor_t, inverse,
    )
    finished, new_view, new_core = tail(
        core_matrix, coeffs, factor_t, inverse, snaps, view, finished
    )
    return (finished, basis_of(new_view), new_core)


def solution(mesh):
    return jax.shard_map(
        on_device,
        mesh=mesh,
        in_specs=(
            P(None, "gx", "gz", None),
            P(),
            P(),
            P(),
            P(None, "gx", "gz"),
            P("gx", None, "gz", None),
            P(),
        ),
        out_specs=(P(None, "gx", "gz", None), P("gx", None, "gz", None), P()),
        check_vma=False,
    )
```

```python
import functools

import jax
import jax.numpy as jnp
from jax import lax
from jax.experimental import pallas as pl
from jax.experimental.pallas import tpu as pltpu
from jax.sharding import PartitionSpec as P

F32, BF16 = jnp.float32, jnp.bfloat16
HIGH = lax.Precision.HIGHEST
SIGN_STEPS = 10
POLAR_STEPS = 3
gram_eps = 1e-06


def halves(values):
    head = values.astype(BF16)
    return head, (values - head.astype(F32)).astype(BF16)


def dot(left, right, over=((1,), (0,))):
    return lax.dot_general(left, right, (over, ((), ())), preferred_element_type=F32)


def dot_three(left, right, over=((1,), (0,))):
    (lh, ll), (rh, rl) = left, right
    return dot(lh, rh, over) + (dot(lh, rl, over) + dot(ll, rh, over))


def dot_high(left, right, over=((1,), (0,))):
    return lax.dot_general(
        left, right, (over, ((), ())), precision=HIGH, preferred_element_type=F32
    )


TN = ((0,), (0,))
NT = ((1,), (1,))


def tripled_left(pair):
    return jnp.concatenate([pair[0], pair[0], pair[1]], axis=0)


def tripled_right(pair):
    return jnp.concatenate([pair[0], pair[1], pair[0]], axis=0)


def eye(count):
    return (
        lax.broadcasted_iota(jnp.int32, (count, count), 0)
        == lax.broadcasted_iota(jnp.int32, (count, count), 1)
    ).astype(F32)


def row_places(z_lanes):
    places = []
    for zc in range(4):
        for x in range(4):
            for y in range(2):
                places.append((zc, x, y))
    return places


def take_basis(view_ref, rows_ref):
    for place, (zc, x, y) in enumerate(row_places(0)):
        for half in range(2):
            rows_ref[pl.ds(place * 32, 32), pl.ds(half * 128, 128)] = view_ref[
                pl.ds(512 * x + 4 * zc + 2 * half + y, 32, stride=16), :
            ]


def give_basis(rows, view_ref, first):
    for step in range(8):
        zc, x, y = row_places(0)[first + step]
        for half in range(2):
            view_ref[pl.ds(512 * x + 4 * zc + 2 * half + y, 32, stride=16), :] = rows[
                step * 32 : step * 32 + 32, half * 128 : half * 128 + 128
            ]


def eliminate(left, right, pivots, columns):
    row_index = lax.broadcasted_iota(jnp.int32, left.shape, 0)
    col_index = lax.broadcasted_iota(jnp.int32, pivots.shape, 1)
    for j in columns:
        pivot = left[j : j + 1, j : j + 1]
        pivots = jnp.where(col_index == j, pivot, pivots)
        scale = lax.rsqrt(pivot)
        scale = scale * (1.5 - 0.5 * pivot * scale * scale)
        column = left[:, j : j + 1] * scale
        row_l = left[j : j + 1, :] * scale
        row_r = right[j : j + 1, :] * scale
        below = row_index > j
        here = row_index == j
        left = jnp.where(below, left - column * row_l, jnp.where(here, row_l, left))
        right = jnp.where(below, right - column * row_r, jnp.where(here, row_r, right))
    return left, right, pivots


def wide_left(v, d):
    modes = v.shape[1]
    vh, vl = halves(v)
    dh, dl = halves(d)
    bh, bl = vh[modes:].astype(F32), vl[modes:].astype(F32)
    turned = jnp.concatenate([bh, bh, bl], axis=0).T.astype(BF16)
    edge = jnp.concatenate([turned, jnp.concatenate([dh, dh, dl], axis=1)], axis=0)
    return vh, vl, edge, jnp.concatenate([vh[modes:], vh[modes:], vl[modes:], edge[modes:]], axis=1)


def product(left, right_v, right_d):
    modes = right_v.shape[1]
    rh, rl = halves(right_v)
    dh, dl = halves(right_d)
    ah, bh = rh[:modes], rh[modes:]
    al, bl = rl[:modes], rl[modes:]
    stacked = jnp.concatenate([ah, al, ah, bh, bl, bh], axis=0)
    low = jnp.concatenate([bh, bl, bh, dh, dl, dh], axis=1)
    vh, vl, edge, wide = left
    thin = jnp.concatenate([bh, bl, bh], axis=0)
    top = (dot(vh[:modes], ah) + dot(vh[:modes], al)) + (dot(vl[:modes], ah) + dot(edge[:modes], thin))
    bottom = dot(wide, jnp.concatenate([ah, al, ah, thin], axis=0))
    return jnp.concatenate([top, bottom], axis=0), dot(wide, low, NT)


def tail_kernel(core_ref, coeffs_ref, factor_ref, inverse_ref, snaps_ref, basis_hbm, fields_hbm,
                out_fields, out_basis, out_core, v_ref, d_ref, basis_view, basis_rows, held, sem, field_sem):
    modes = core_ref.shape[0]
    fetch = pltpu.make_async_copy(basis_hbm, basis_view, sem)
    fetch.start()
    taking = pltpu.make_async_copy(fields_hbm, held, field_sem)
    taking.start()
    factor_t = factor_ref[...]
    inverse = inverse_ref[...]
    coeffs = coeffs_ref[...]
    unit = eye(modes)
    unit_d = eye(16)
    parts = halves(coeffs)
    corr_a = core_ref[...] + dot(tripled_left(parts), tripled_right(parts), TN)
    corr_b = dot_high(factor_t, coeffs)
    corr_d = dot_high(factor_t, factor_t, NT)
    shift_a = corr_a - unit
    shift_d = corr_d - unit_d
    total = (
        jnp.sum(shift_a * shift_a, keepdims=True)
        + 2.0 * jnp.sum(corr_b * corr_b, keepdims=True)
        + jnp.sum(shift_d * shift_d, keepdims=True)
    )
    scale = 1.0 / jnp.sqrt(total)
    v_ref[:modes] = shift_a * scale
    v_ref[modes:] = corr_b * scale
    d_ref[...] = shift_d * scale
    unit_v = jnp.concatenate([unit, jnp.zeros((16, modes), F32)], axis=0)

    def sign_step(step, carry):
        v = v_ref[...]
        d = d_ref[...]
        left = wide_left(v, d)
        square_v, square_d = product(left, v, d)
        next_v, next_d = product(
            left, 1.5 * unit_v - 0.5 * square_v, 1.5 * unit_d - 0.5 * square_d
        )
        v_ref[...] = next_v
        d_ref[...] = next_d
        return carry

    lax.fori_loop(0, SIGN_STEPS, sign_step, 0)

    fetch.wait()
    taking.wait()
    passing = pltpu.make_async_copy(held, out_fields, field_sem)
    passing.start()
    take_basis(basis_view, basis_rows)

    rot = 0.5 * (unit_v + v_ref[...])
    pair = halves(rot)
    top = (pair[0][:modes], pair[1][:modes])
    low = (pair[0][modes:], pair[1][modes:])
    inner = dot_three(top, top) + dot(tripled_left(low), tripled_right(low), TN)
    for step in range(POLAR_STEPS):
        factor = 1.5 * unit - 0.5 * inner
        fp = halves(factor)
        rot = dot_three(halves(rot), fp)
        if step < POLAR_STEPS - 1:
            inner = dot_three(halves(dot_three(halves(inner), fp)), fp)
    rp = halves(rot)
    corr_v = jnp.concatenate([corr_a, corr_b], axis=0)
    moved = dot_three(halves(corr_v), (rp[0][:modes], rp[1][:modes]))
    rb48 = tripled_right((rp[0][modes:], rp[1][modes:]))
    moved = moved + jnp.concatenate(
        [
            dot(tripled_left(halves(corr_b)), rb48, TN),
            dot(tripled_left(halves(corr_d)), rb48, TN),
        ],
        axis=0,
    )
    out_core[...] = dot_three(rp, halves(moved), TN)

    mix = dot_high(inverse, rot[modes:], TN)
    mix48 = tripled_right(halves(mix))
    ra = halves(rot[:modes] - dot(tripled_left(parts), mix48, TN))
    for part in range(4):
        rows = basis_rows[pl.ds(part * 256, 256), :]
        left = tripled_left(halves(snaps_ref[:, part * 256 : part * 256 + 256]))
        give_basis(dot_three(halves(rows), ra) + dot(left, mix48, TN), out_basis, part * 8)
    passing.wait()


def tail(core, coeffs, factor_t, inverse, snaps, basis_view, fields):
    vmem = pl.BlockSpec(memory_space=pltpu.VMEM)
    hbm = pl.BlockSpec(memory_space=pltpu.HBM)
    return pl.pallas_call(
        tail_kernel,
        out_shape=(
            jax.ShapeDtypeStruct(fields.shape, F32),
            jax.ShapeDtypeStruct((2048, 128), F32),
            jax.ShapeDtypeStruct((256, 256), F32),
        ),
        in_specs=[vmem, vmem, vmem, vmem, vmem, hbm, hbm],
        out_specs=(hbm, vmem, vmem),
        scratch_shapes=[
            pltpu.VMEM((272, 256), F32),
            pltpu.VMEM((16, 16), F32),
            pltpu.VMEM((2048, 128), F32),
            pltpu.VMEM((1024, 256), F32),
            pltpu.VMEM(fields.shape, F32),
            pltpu.SemaphoreType.DMA,
            pltpu.SemaphoreType.DMA,
        ],
        compiler_params=pltpu.CompilerParams(vmem_limit_bytes=60 * 1024 * 1024),
    )(core, coeffs, factor_t, inverse, snaps, basis_view, fields)


def view_of(basis):
    return basis.reshape(4, 128, 2, 2, 128).transpose(0, 1, 3, 2, 4).reshape(2048, 128)


def basis_of(view):
    return view.reshape(4, 128, 2, 2, 128).transpose(0, 1, 3, 2, 4).reshape(4, 128, 2, 256)


MESH = pl.DeviceIdType.MESH
press_coef = 0.25
compress_coef = 0.25
visc_coef = 0.05
heat_coef = 0.03
FIELDS = 5
least_pivot = 2.0**-7


def shifted(values):
    width = values.shape[-1]
    lane = lax.broadcasted_iota(jnp.int32, values.shape, 1)
    lower = jnp.where(lane == 0, 0.0, pltpu.roll(values, 1, 1))
    upper = jnp.where(lane == width - 1, 0.0, pltpu.roll(values, width - 1, 1))
    return lower, upper


class Fields:
    def __init__(self, read):
        self.read = read
        self.known = {}

    def __getitem__(self, f):
        if f not in self.known:
            self.known[f] = self.read(f)
        return self.known[f]


def update(centre, xl, xu, zl, zu, profiles, wanted=range(FIELDS)):
    courant, shear_rate, gradient = profiles
    beside = Fields(lambda f: shifted(centre[f]))
    keep = [1.0 - 6.0 * visc_coef - courant] * 3 + [1.0 - 6.0 * visc_coef]
    keep = keep + [1.0 - 6.0 * heat_coef - courant]
    bring = [visc_coef + courant] * 3 + [visc_coef, heat_coef + courant]
    spread = [visc_coef] * 4 + [heat_coef]
    half_press = 0.5 * press_coef
    sources = Fields(lambda f: (
        lambda: shear_rate * centre[1] + half_press * (xu[3] - xl[3]),
        lambda: half_press * (beside[3][1] - beside[3][0]),
        lambda: half_press * (zu[3] - zl[3]),
        lambda: 0.5 * compress_coef * (
            (xu[0] - xl[0]) + (beside[1][1] - beside[1][0]) + (zu[2] - zl[2])
        ),
        lambda: gradient * centre[1],
    )[f]())
    new = {}
    for f in wanted:
        around = (xu[f] + zl[f]) + (zu[f] + beside[f][0]) + beside[f][1]
        new[f] = keep[f] * centre[f] + bring[f] * xl[f] + spread[f] * around - sources[f]
    return new


def front_kernel(sizes, fields_hbm, courant_hbm, shear_hbm, gradient_hbm, earlier_hbm, basis_hbm,
                 out_fields, out_coeffs, out_factor, out_inverse, out_sound, out_snaps,
                 P, H, F, Zs, Zr, Cs, Cr, V, basis_view, basis_rows, basis_h, basis_l,
                 E2, early_send, early_slots, late_send, late_slots, S,
                 g_send, g_slots, g_mid, g_mid_slots, g_part, g_parts, g_whole, g_all,
                 e_send, e_slots, e_mid, e_mid_slots, e_part, e_all,
                 c_send, c_other, c_mid, c_slots,
                 earlier_ref, profile_rows, small_sem, load_sem, basis_sem, out_sem, halo_send, halo_recv,
                 group_send, group_recv):
    nx, nz = sizes
    gx = lax.axis_index("gx")
    gz = lax.axis_index("gz")
    rows_total = 1024.0 * nx * nz

    barrier = pltpu.get_barrier_semaphore()
    x_beside = (lax.rem(gx + nx - 1, nx), lax.rem(gx + 1, nx))
    z_beside = (lax.rem(gz + nz - 1, nz), lax.rem(gz + 1, nz))

    def greet(where):
        pl.semaphore_signal(barrier, inc=1, device_id=where, device_id_type=MESH)

    def greet_z(d, carry):
        greet((gx, lax.rem(gz + d, nz)))
        return carry

    load = pltpu.make_async_copy(fields_hbm, P.at[:, 2:18, 8:24, :], load_sem)
    load.start()
    fetch = pltpu.make_async_copy(basis_hbm, basis_view, basis_sem)
    fetch.start()
    small = [
        pltpu.make_async_copy(earlier_hbm, earlier_ref, small_sem.at[0]),
        pltpu.make_async_copy(courant_hbm, profile_rows.at[0], small_sem.at[1]),
        pltpu.make_async_copy(shear_hbm, profile_rows.at[1], small_sem.at[2]),
        pltpu.make_async_copy(gradient_hbm, profile_rows.at[2], small_sem.at[3]),
    ]
    for copy in small:
        copy.start()
    for d in range(1, nx):
        greet((lax.rem(gx + d, nx), gz))
    for xs in range(2):
        for zs in range(2):
            greet((x_beside[xs], z_beside[zs]))
    for d in range(1, nx):
        greet((lax.rem(gx + d, nx), gz + 1 - 2 * lax.rem(gz, 2)))
    lax.fori_loop(1, nz, greet_z, 0)

    for copy in small:
        copy.wait()
    E2[...] = jnp.zeros_like(E2)
    for m in range(14):
        for x in range(4):
            E2[x * 16 + m : x * 16 + m + 1, :] = earlier_ref[m, x : x + 1, :]
    turned = E2[...].T
    turned = jnp.concatenate([turned[64 * z : 64 * z + 64] for z in range(4)], axis=1)
    for i in range(32):
        early_send[i] = turned[2 * i : 2 * i + 2]
    pl.semaphore_wait(barrier, nz - 1 + 2 * (nx - 1) + 4)

    def spread_z(place, source, slots):
        def body(d, carry):
            peer = lax.rem(gz + d, nz)
            pltpu.make_async_remote_copy(
                src_ref=source(peer), dst_ref=slots.at[gz], send_sem=group_send.at[place],
                recv_sem=group_recv.at[place], device_id=(gx, peer), device_id_type=MESH,
            ).start()
            return carry

        lax.fori_loop(1, nz, body, 0)

    spread_z(0, lambda peer: early_send.at[peer], early_slots)
    early_slots[gz] = early_send[gz]

    load.wait()

    halos = []

    def send_halo(source, target, where):
        place = len(halos)
        copy = pltpu.make_async_remote_copy(
            src_ref=source, dst_ref=target, send_sem=halo_send.at[place],
            recv_sem=halo_recv.at[place], device_id=where, device_id_type=MESH,
        )
        copy.start()
        halos.append(copy)

    def send_x(side, fields, layers):
        first_own = 2 + 14 * side + layers[0]
        first_there = 18 - 18 * side + layers[0]
        send_halo(
            P.at[fields, first_own : first_own + len(layers), 8:24, :],
            P.at[fields, first_there : first_there + len(layers), 8:24, :],
            (x_beside[side], gz),
        )

    def send_z(side, layer, fields):
        send_halo(
            Zs.at[side, layer, fields, 8:24, :],
            Zr.at[1 - side, layer, fields, 8:24, :],
            (gx, z_beside[side]),
        )

    for side in range(2):
        send_x(side, pl.ds(0, 1), (0, 1))
        send_x(side, pl.ds(3, 1), (0, 1))
        send_x(side, pl.ds(1, 2), (side,))

    for side in range(2):
        for layer in range(2):
            z = 8 + 14 * side + layer
            for f in range(FIELDS):
                for half in range(2):
                    lanes = pl.ds(128 * half, 128)
                    Zs[side, layer, f, 8:24, lanes] = P[f, 2:18, z, lanes]
    for xs in range(2):
        for zs in range(2):
            for f in range(FIELDS):
                Cs[2 * xs + zs, f : f + 1, :] = P[f, 2 + 15 * xs, 8 + 15 * zs : 9 + 15 * zs, :]

    for side in range(2):
        send_z(side, side, pl.ds(0, 4))
        send_z(side, 1 - side, pl.ds(0, 1))
    for xs in range(2):
        for zs in range(2):
            send_halo(
                Cs.at[2 * xs + zs], Cr.at[2 * (1 - xs) + 1 - zs], (x_beside[xs], z_beside[zs])
            )
    urgent = len(halos)

    yz = gz // 2
    places = nz // 2
    along = (lax.rem(gz, 2) * (nx // 2) + gx // 2) * 2 + lax.rem(gx, 2)
    line = 2 * nx

    def spread_yz(place, source, slots):
        def body(d, carry):
            peer = lax.rem(yz + d, places)
            pltpu.make_async_remote_copy(
                src_ref=source(peer), dst_ref=slots.at[yz], send_sem=group_send.at[place],
                recv_sem=group_recv.at[place], device_id=(gx, 2 * peer + lax.rem(gz, 2)),
                device_id_type=MESH,
            ).start()
            return carry

        lax.fori_loop(1, places, body, 0)

    def spread_line(place, source, slots):
        def body(d, carry):
            peer = lax.rem(along + d, line)
            where = (lax.rem(peer, nx), 2 * yz + peer // nx)
            pltpu.make_async_remote_copy(
                src_ref=source(peer), dst_ref=slots.at[along], send_sem=group_send.at[place],
                recv_sem=group_recv.at[place], device_id=where, device_id_type=MESH,
            ).start()
            return carry

        lax.fori_loop(1, line, body, 0)

    core = lax.rem(gx, 2)
    chip = (gx // 2) * nz + gz
    chips = (nx // 2) * nz

    def send_core(place, source, target):
        pltpu.make_async_remote_copy(
            src_ref=source, dst_ref=target, send_sem=group_send.at[place],
            recv_sem=group_recv.at[place], device_id=(gx + 1 - 2 * core, gz), device_id_type=MESH,
        ).start()

    def spread_chips(place, source, slots):
        def body(d, carry):
            peer = lax.rem(chip + d, chips)
            where = (2 * (peer // nz) + core, lax.rem(peer, nz))
            pltpu.make_async_remote_copy(
                src_ref=source, dst_ref=slots.at[chip], send_sem=group_send.at[place],
                recv_sem=group_recv.at[place], device_id=where, device_id_type=MESH,
            ).start()
            return carry

        lax.fori_loop(1, chips, body, 0)

    def wait_one(sems, place, part):
        pltpu.make_async_copy(part, part, sems.at[place]).wait()

    def sum_slots_of(slots):
        terms = [slots[j] for j in range(slots.shape[0])]
        while len(terms) > 1:
            terms = [a + b for a, b in zip(terms[::2], terms[1::2])] + terms[len(terms) & ~1 :]
        return terms[0]

    def wait_all(sems, place, slots):
        some = slots.at[pl.ds(0, slots.shape[0] - 1)]
        pltpu.make_async_copy(some, some, sems.at[place]).wait()

    fetch.wait()
    take_basis(basis_view, basis_rows)
    rows = basis_rows[...]
    head = rows.astype(BF16)
    basis_h[...] = head
    basis_l[...] = (rows - head.astype(F32)).astype(BF16)

    def pair():
        return basis_h[...], basis_l[...]

    inner = dot_three(pair(), pair(), TN)
    for i in range(16):
        g_send[i, :, :256] = inner[8 * i : 8 * i + 8]
        g_send[i, :, 256:] = inner[128 + 8 * i : 136 + 8 * i, 128:]
    spread_yz(1, lambda peer: g_send.at[peer], g_slots)
    g_slots[yz] = g_send[yz]
    for side in range(2):
        send_x(side, pl.ds(1, 2), (1 - side,))
        send_x(side, pl.ds(4, 1), (0, 1))
        send_z(side, side, pl.ds(4, 1))
        send_z(side, 1 - side, pl.ds(1, 4))

    profiles = [profile_rows[k] for k in range(3)]

    def first(i, wanted=range(FIELDS)):
        centre = Fields(lambda f: P[f, i + 1, 8:24, :])
        xl = Fields(lambda f: P[f, i, 8:24, :])
        xu = Fields(lambda f: P[f, i + 2, 8:24, :])
        zl = Fields(lambda f: P[f, i + 1, 7:23, :])
        zu = Fields(lambda f: P[f, i + 1, 9:25, :])
        for f, new in update(centre, xl, xu, zl, zu, profiles, wanted).items():
            H[f, i, 8:24, :] = new

    def first_inside(i, carry):
        first(i)
        return carry

    lax.fori_loop(2, 16, first_inside, 0)

    wait_all(group_recv, 0, early_slots)
    got = jnp.concatenate([early_slots[:, 0, :], early_slots[:, 1, :]], axis=0).T
    for zx in range(16):
        S[:, zx * 64 : zx * 64 + 64] = got[zx * 16 : zx * 16 + 16]
    snaps = halves(S[...])
    c_early = dot_three(snaps, pair())
    k_early = dot_three(snaps, snaps, NT)
    early = jnp.concatenate([c_early, k_early, jnp.zeros((16, 112), F32)], axis=1)
    for m in range(16):
        e_send[m] = early[m : m + 1]
    spread_yz(8, lambda peer: e_send.at[peer], e_slots)
    e_slots[yz] = e_send[yz]

    for copy in halos[:urgent]:
        copy.wait_recv()

    def fill_corners(fields):
        for f in fields:
            for xs in range(2):
                row = 7 + 17 * xs
                x = 1 + 17 * xs
                for zs in range(2):
                    corner = Cr[2 * xs + zs, f : f + 1, :]
                    Zr[zs, 1 - zs, f, row : row + 1, :] = corner
                    P[f, x, 7 + 17 * zs : 8 + 17 * zs, :] = corner
                    Zs[zs, zs, f, row : row + 1, :] = P[f, x, 8 + 15 * zs : 9 + 15 * zs, :]

    def first_edges(outside_x, outside_z, inside):
        def outside_rows(k, carry):
            first(17 * k, outside_x)
            return carry

        def inside_rows(k, carry):
            first(1 + 15 * k, inside)
            return carry

        lax.fori_loop(0, 2, outside_rows, 0)
        lax.fori_loop(0, 2, inside_rows, 0)
        for side in range(2):
            layers = [
                Zr.at[side, side], Zr.at[side, 1 - side], Zs.at[side, side], Zs.at[side, 1 - side]
            ]
            for edge in range(2):
                edge_layer(side, edge, layers[edge : edge + 3], (outside_z, inside)[edge])

    def edge_layer(side, edge, layers, wanted):
        outer, mid, inside = layers
        centre = Fields(lambda f: mid[f, 8:24, :])
        xl = Fields(lambda f: mid[f, 7:23, :])
        xu = Fields(lambda f: mid[f, 9:25, :])
        out = Fields(lambda f: outer[f, 8:24, :])
        within = Fields(lambda f: inside[f, 8:24, :])
        zl, zu = (out, within) if side == 0 else (within, out)
        z = 7 + edge if side == 0 else 24 - edge
        for f, new in update(centre, xl, xu, zl, zu, profiles, wanted).items():
            H[f, 1:17, z, :] = new

    fill_corners(range(4))
    first_edges((0, 3), (0,), (0, 1, 3))

    def second(wanted):
        def row(i, carry):
            centre = Fields(lambda f: H[f, i + 1, 8:24, :])
            xl = Fields(lambda f: H[f, i, 8:24, :])
            xu = Fields(lambda f: H[f, i + 2, 8:24, :])
            zl = Fields(lambda f: H[f, i + 1, 7:23, :])
            zu = Fields(lambda f: H[f, i + 1, 9:25, :])
            for f, new in update(centre, xl, xu, zl, zu, profiles, wanted).items():
                F[f, i, :, :] = new
            return carry

        lax.fori_loop(0, 16, row, 0)

    second((0,))

    for xg in range(4):
        V[16 * xg : 16 * xg + 16, :] = (H[0, 4 * xg + 1, 8:24, :] + H[0, 4 * xg + 2, 8:24, :]) + (
            H[0, 4 * xg + 3, 8:24, :] + H[0, 4 * xg + 4, 8:24, :]
        )
        V[64 + 16 * xg : 80 + 16 * xg, :] = (F[0, 4 * xg] + F[0, 4 * xg + 1]) + (
            F[0, 4 * xg + 2] + F[0, 4 * xg + 3]
        )
    to = lax.broadcasted_iota(jnp.int32, (128, 128), 0)
    of = lax.broadcasted_iota(jnp.int32, (128, 128), 1)
    wanted = ((lax.rem(of, 16) // 4) * 4 + lax.rem(of, 64) // 16) * 8 + 6 + of // 64
    place_to = (to == wanted).astype(BF16)
    sums = halves(V[...])
    gathered = dot(
        jnp.concatenate([place_to, place_to], axis=1), jnp.concatenate(sums, axis=0)
    )
    block = (
        lax.broadcasted_iota(jnp.int32, (64, 256), 0)
        == lax.broadcasted_iota(jnp.int32, (64, 256), 1) // 4
    ).astype(BF16) * BF16(1.0 / 64.0)
    coarse = dot(
        jnp.concatenate([block, block], axis=1), jnp.concatenate(halves(gathered), axis=1), NT
    )
    for i in range(32):
        late_send[i] = coarse[2 * i : 2 * i + 2]
    spread_z(2, lambda peer: late_send.at[peer], late_slots)
    late_slots[gz] = late_send[gz]

    wait_all(group_recv, 1, g_slots)
    total = sum_slots_of(g_slots)
    for r in range(8):
        g_mid[r] = total[r : r + 1]
    spread_line(3, lambda peer: g_mid.at[peer], g_mid_slots)
    g_mid_slots[along] = g_mid[along]

    wait_all(group_recv, 8, e_slots)
    e_mid[...] = sum_slots_of(e_slots)
    spread_line(9, lambda peer: e_mid, e_mid_slots)
    e_mid_slots[along] = e_mid[...]

    wait_all(group_recv, 3, g_mid_slots)
    g_part[...] = sum_slots_of(g_mid_slots)
    spread_line(5, lambda peer: g_part, g_parts)
    g_parts[along] = g_part[...]

    for copy in halos[urgent:]:
        copy.wait_recv()
    fill_corners((4,))
    first_edges((1, 2, 4), (1, 2, 3, 4), (2, 4))
    second((1, 2, 3, 4))
    store = pltpu.make_async_copy(F, out_fields, out_sem)
    store.start()

    wait_all(group_recv, 5, g_parts)
    for r in range(8):
        g_whole[r : r + 1, :] = g_parts[r]
    spread_yz(7, lambda peer: g_whole, g_all)
    g_all[yz] = g_whole[...]

    wait_all(group_recv, 9, e_mid_slots)
    e_part[...] = sum_slots_of(e_mid_slots)
    spread_yz(10, lambda peer: e_part, e_all)
    e_all[yz] = e_part[...]

    wait_all(group_recv, 2, late_slots)
    got = jnp.concatenate([late_slots[:, 0, :], late_slots[:, 1, :]], axis=0).T
    for zx in range(16):
        S[8:16, zx * 64 : zx * 64 + 64] = S[8:16, zx * 64 : zx * 64 + 64] + got[zx * 8 : zx * 8 + 8]
    out_snaps[...] = S[...]
    low = S[8:16, :]
    low = jnp.where(lax.broadcasted_iota(jnp.int32, low.shape, 0) >= 6, low, 0.0)
    late = halves(jnp.concatenate([jnp.zeros_like(low), low], axis=0))
    both = dot(jnp.concatenate(late, axis=0), basis_h[...])
    c_late = (both[:16] + both[16:] + dot(late[0], basis_l[...]))[14:16]
    k_late = dot_three(late, halves(S[...]), NT)[14:16]
    late = jnp.concatenate([c_late, k_late, jnp.zeros((2, 112), F32)], axis=1)
    c_send[...] = late
    send_core(4, c_send, c_other)
    wait_one(group_recv, 4, c_other)
    both = late + c_other[...]
    c_mid[...] = both
    spread_chips(6, c_mid, c_slots)
    c_slots[chip] = both

    wait_all(group_recv, 7, g_all)
    every = g_all[...].reshape(128, 384)
    cross = every[:, 128:256]
    metric = jnp.concatenate(
        [every[:, :256], jnp.concatenate([cross.T, every[:, 256:]], axis=1)], axis=0
    ) * (1.0 / rows_total)
    unit = eye(256)
    removed = 4.0 * unit - 6.0 * metric + dot_high(dot_high(metric, metric), 4.0 * unit - metric)
    wait_all(group_recv, 10, e_all)
    early = e_all[...].reshape(16, 384) * (1.0 / rows_total)
    c_early = early[:, :256]
    identity = eye(16)
    gram = early[:, 256:272] - dot_high(dot_high(c_early, removed), c_early, NT)
    left, right, pivots = eliminate(
        gram + gram_eps * identity, identity, jnp.zeros((1, 16), F32), range(14)
    )
    low_row = lax.broadcasted_iota(jnp.int32, (16, 16), 0) >= 14
    low_col = lax.broadcasted_iota(jnp.int32, (16, 16), 1) >= 14

    wait_all(group_recv, 6, c_slots)
    total = jnp.concatenate([early[:14], sum_slots_of(c_slots) * (1.0 / rows_total)], axis=0)
    c_one = total[:, :256]
    size = total[:, 256:272]
    out_coeffs[...] = 2.0 * c_one - dot_high(c_one, metric)
    gram = size - dot_high(dot_high(c_one, removed), c_one, NT) + gram_eps * identity
    across = dot_high(jnp.where(low_row & ~low_col, gram, 0.0), right, NT)
    corner = jnp.where(low_row & low_col, gram, 0.0) - dot_high(across, across, NT)
    left, right, pivots = eliminate(
        jnp.where(low_row, corner, left + across.T), right - dot_high(across, right), pivots,
        range(14, 16),
    )
    upper = lax.broadcasted_iota(jnp.int32, (16, 16), 0) <= lax.broadcasted_iota(
        jnp.int32, (16, 16), 1
    )
    out_factor[...] = jnp.where(upper, left, 0.0)
    out_inverse[...] = right
    scale = jnp.sum(jnp.where(identity > 0.0, size, 0.0), axis=0, keepdims=True)
    sound = jnp.where(pivots > least_pivot * scale, 1, 0)
    out_sound[0, 0] = jnp.min(sound)

    for copy in halos:
        copy.wait_send()
    for place, slots in (
        (0, early_slots), (1, g_slots), (2, late_slots), (3, g_mid_slots), (5, g_parts),
        (6, c_slots), (7, g_all), (8, e_slots), (9, e_mid_slots), (10, e_all),
    ):
        wait_all(group_send, place, slots)
    wait_one(group_send, 4, c_other)
    store.wait()


def front(sizes, fields, profiles, earlier, basis_view):
    nx, nz = sizes
    vmem = pl.BlockSpec(memory_space=pltpu.VMEM)
    hbm = pl.BlockSpec(memory_space=pltpu.HBM)
    smem = pl.BlockSpec(memory_space=pltpu.SMEM)
    v = pltpu.VMEM
    return pl.pallas_call(
        functools.partial(front_kernel, sizes),
        out_shape=(
            jax.ShapeDtypeStruct(fields.shape, F32),
            jax.ShapeDtypeStruct((16, 256), F32),
            jax.ShapeDtypeStruct((16, 16), F32),
            jax.ShapeDtypeStruct((16, 16), F32),
            jax.ShapeDtypeStruct((1, 1), jnp.int32),
            jax.ShapeDtypeStruct((16, 1024), F32),
        ),
        in_specs=[hbm] * 6,
        out_specs=(hbm, vmem, vmem, vmem, smem, vmem),
        scratch_shapes=[
            v((5, 20, 32, 256), F32),
            v((5, 18, 32, 256), F32),
            v((5, 16, 16, 256), F32),
            v((2, 2, 5, 32, 256), F32),
            v((2, 2, 5, 32, 256), F32),
            v((4, 8, 256), F32),
            v((4, 8, 256), F32),
            v((128, 256), F32),
            v((2048, 128), F32),
            v((1024, 256), F32),
            v((1024, 256), BF16),
            v((1024, 256), BF16),
            v((64, 256), F32),
            v((32, 2, 256), F32),
            v((32, 2, 256), F32),
            v((32, 2, 128), F32),
            v((32, 2, 128), F32),
            v((16, 1024), F32),
            v((16, 8, 384), F32),
            v((16, 8, 384), F32),
            v((8, 1, 384), F32),
            v((8, 1, 384), F32),
            v((1, 384), F32),
            v((8, 1, 384), F32),
            v((8, 384), F32),
            v((16, 8, 384), F32),
            v((16, 1, 384), F32),
            v((16, 1, 384), F32),
            v((1, 384), F32),
            v((8, 1, 384), F32),
            v((1, 384), F32),
            v((16, 1, 384), F32),
            v((2, 384), F32),
            v((2, 384), F32),
            v((2, 384), F32),
            v((64, 2, 384), F32),
            v((14, 4, 256), F32),
            v((3, 1, 256), F32),
            pltpu.SemaphoreType.DMA((4,)),
            pltpu.SemaphoreType.DMA,
            pltpu.SemaphoreType.DMA,
            pltpu.SemaphoreType.DMA,
            pltpu.SemaphoreType.DMA((22,)),
            pltpu.SemaphoreType.DMA((22,)),
            pltpu.SemaphoreType.DMA((11,)),
            pltpu.SemaphoreType.DMA((11,)),
        ],
        compiler_params=pltpu.CompilerParams(
            collective_id=0, has_side_effects=True, vmem_limit_bytes=62 * 1024 * 1024
        ),
    )(fields, *profiles, earlier, basis_view)


def direct_factor(snaps, coeffs, basis_modes):
    rows_total = 1024.0 * lax.axis_size("gx") * lax.axis_size("gz")
    rows = basis_modes.reshape(4, 32, 4, 2, 256).transpose(2, 0, 3, 1, 4).reshape(1024, 256)
    resid = snaps - jnp.dot(coeffs, rows.T, precision=HIGH)
    gram = lax.psum(jnp.dot(resid, resid.T, precision=HIGH), ("gx", "gz")) / rows_total
    identity = jnp.eye(16, dtype=F32)
    factor = jnp.linalg.cholesky(gram + gram_eps * identity)
    return factor.T, jax.scipy.linalg.solve_triangular(factor, identity, lower=True)


def on_device(fields, courant, shear_rate, gradient, earlier, basis_modes, core_matrix):
    sizes = (lax.axis_size("gx"), lax.axis_size("gz"))
    view = view_of(basis_modes)
    profiles = [p.reshape(1, -1) for p in (courant, shear_rate, gradient)]
    finished, coeffs, factor_t, inverse, sound, snaps = front(
        sizes, fields, profiles, earlier, view
    )
    factor_t, inverse = lax.cond(
        sound[0, 0] > 0,
        lambda snaps, coeffs, basis_modes, factor_t, inverse: (factor_t, inverse),
        lambda snaps, coeffs, basis_modes, factor_t, inverse: direct_factor(
            snaps, coeffs, basis_modes
        ),
        snaps, coeffs, basis_modes, factor_t, inverse,
    )
    finished, new_view, new_core = tail(
        core_matrix, coeffs, factor_t, inverse, snaps, view, finished
    )
    return (finished, basis_of(new_view), new_core)


def solution(mesh):
    return jax.shard_map(
        on_device,
        mesh=mesh,
        in_specs=(
            P(None, "gx", "gz", None),
            P(),
            P(),
            P(),
            P(None, "gx", "gz"),
            P("gx", None, "gz", None),
            P(),
        ),
        out_specs=(P(None, "gx", "gz", None), P("gx", None, "gz", None), P()),
        check_vma=False,
    )
```

```python
import functools

import jax
import jax.numpy as jnp
from jax import lax
from jax.experimental import pallas as pl
from jax.experimental.pallas import tpu as pltpu
from jax.sharding import PartitionSpec as P

F32, BF16 = jnp.float32, jnp.bfloat16
HIGH = lax.Precision.HIGHEST
SIGN_STEPS = 10
POLAR_STEPS = 3
gram_eps = 1e-06


def halves(values):
    head = values.astype(BF16)
    return head, (values - head.astype(F32)).astype(BF16)


def dot(left, right, over=((1,), (0,))):
    return lax.dot_general(left, right, (over, ((), ())), preferred_element_type=F32)


def dot_three(left, right, over=((1,), (0,))):
    (lh, ll), (rh, rl) = left, right
    return dot(lh, rh, over) + (dot(lh, rl, over) + dot(ll, rh, over))


def dot_high(left, right, over=((1,), (0,))):
    return lax.dot_general(
        left, right, (over, ((), ())), precision=HIGH, preferred_element_type=F32
    )


TN = ((0,), (0,))
NT = ((1,), (1,))


def tripled_left(pair):
    return jnp.concatenate([pair[0], pair[0], pair[1]], axis=0)


def tripled_right(pair):
    return jnp.concatenate([pair[0], pair[1], pair[0]], axis=0)


def eye(count):
    return (
        lax.broadcasted_iota(jnp.int32, (count, count), 0)
        == lax.broadcasted_iota(jnp.int32, (count, count), 1)
    ).astype(F32)


def row_places(z_lanes):
    places = []
    for zc in range(4):
        for x in range(4):
            for y in range(2):
                places.append((zc, x, y))
    return places


def take_basis(view_ref, rows_ref):
    for place, (zc, x, y) in enumerate(row_places(0)):
        for half in range(2):
            rows_ref[pl.ds(place * 32, 32), pl.ds(half * 128, 128)] = view_ref[
                pl.ds(512 * x + 4 * zc + 2 * half + y, 32, stride=16), :
            ]


def give_basis(rows, view_ref, first):
    for step in range(8):
        zc, x, y = row_places(0)[first + step]
        for half in range(2):
            view_ref[pl.ds(512 * x + 4 * zc + 2 * half + y, 32, stride=16), :] = rows[
                step * 32 : step * 32 + 32, half * 128 : half * 128 + 128
            ]


def eliminate(left, right, pivots, columns):
    row_index = lax.broadcasted_iota(jnp.int32, left.shape, 0)
    col_index = lax.broadcasted_iota(jnp.int32, pivots.shape, 1)
    for j in columns:
        pivot = left[j : j + 1, j : j + 1]
        pivots = jnp.where(col_index == j, pivot, pivots)
        scale = lax.rsqrt(pivot)
        scale = scale * (1.5 - 0.5 * pivot * scale * scale)
        column = left[:, j : j + 1] * scale
        row_l = left[j : j + 1, :] * scale
        row_r = right[j : j + 1, :] * scale
        below = row_index > j
        here = row_index == j
        left = jnp.where(below, left - column * row_l, jnp.where(here, row_l, left))
        right = jnp.where(below, right - column * row_r, jnp.where(here, row_r, right))
    return left, right, pivots


def wide_left(v, d):
    modes = v.shape[1]
    vh, vl = halves(v)
    dh, dl = halves(d)
    bh, bl = vh[modes:].astype(F32), vl[modes:].astype(F32)
    turned = jnp.concatenate([bh, bh, bl], axis=0).T.astype(BF16)
    edge = jnp.concatenate([turned, jnp.concatenate([dh, dh, dl], axis=1)], axis=0)
    return vh, vl, edge, jnp.concatenate([vh[modes:], vh[modes:], vl[modes:], edge[modes:]], axis=1)


def product(left, right_v, right_d):
    modes = right_v.shape[1]
    rh, rl = halves(right_v)
    dh, dl = halves(right_d)
    ah, bh = rh[:modes], rh[modes:]
    al, bl = rl[:modes], rl[modes:]
    stacked = jnp.concatenate([ah, al, ah, bh, bl, bh], axis=0)
    low = jnp.concatenate([bh, bl, bh, dh, dl, dh], axis=1)
    vh, vl, edge, wide = left
    thin = jnp.concatenate([bh, bl, bh], axis=0)
    top = (dot(vh[:modes], ah) + dot(vh[:modes], al)) + (dot(vl[:modes], ah) + dot(edge[:modes], thin))
    bottom = dot(wide, jnp.concatenate([ah, al, ah, thin], axis=0))
    return jnp.concatenate([top, bottom], axis=0), dot(wide, low, NT)


def tail_kernel(core_ref, coeffs_ref, factor_ref, inverse_ref, snaps_ref, basis_hbm, fields_hbm,
                out_fields, out_basis, out_core, v_ref, d_ref, basis_view, basis_rows, held, sem, field_sem):
    modes = core_ref.shape[0]
    fetch = pltpu.make_async_copy(basis_hbm, basis_view, sem)
    fetch.start()
    taking = pltpu.make_async_copy(fields_hbm, held, field_sem)
    taking.start()
    factor_t = factor_ref[...]
    inverse = inverse_ref[...]
    coeffs = coeffs_ref[...]
    unit = eye(modes)
    unit_d = eye(16)
    parts = halves(coeffs)
    corr_a = core_ref[...] + dot(tripled_left(parts), tripled_right(parts), TN)
    corr_b = dot_high(factor_t, coeffs)
    corr_d = dot_high(factor_t, factor_t, NT)
    shift_a = corr_a - unit
    shift_d = corr_d - unit_d
    total = (
        jnp.sum(shift_a * shift_a, keepdims=True)
        + 2.0 * jnp.sum(corr_b * corr_b, keepdims=True)
        + jnp.sum(shift_d * shift_d, keepdims=True)
    )
    scale = 1.0 / jnp.sqrt(total)
    v_ref[:modes] = shift_a * scale
    v_ref[modes:] = corr_b * scale
    d_ref[...] = shift_d * scale
    unit_v = jnp.concatenate([unit, jnp.zeros((16, modes), F32)], axis=0)

    def sign_step(step, carry):
        v = v_ref[...]
        d = d_ref[...]
        left = wide_left(v, d)
        square_v, square_d = product(left, v, d)
        next_v, next_d = product(
            left, 1.5 * unit_v - 0.5 * square_v, 1.5 * unit_d - 0.5 * square_d
        )
        v_ref[...] = next_v
        d_ref[...] = next_d
        return carry

    lax.fori_loop(0, SIGN_STEPS, sign_step, 0)

    fetch.wait()
    taking.wait()
    passing = pltpu.make_async_copy(held, out_fields, field_sem)
    passing.start()
    take_basis(basis_view, basis_rows)

    rot = 0.5 * (unit_v + v_ref[...])
    pair = halves(rot)
    top = (pair[0][:modes], pair[1][:modes])
    low = (pair[0][modes:], pair[1][modes:])
    inner = dot_three(top, top) + dot(tripled_left(low), tripled_right(low), TN)
    for step in range(POLAR_STEPS):
        factor = 1.5 * unit - 0.5 * inner
        fp = halves(factor)
        rot = dot_three(halves(rot), fp)
        if step < POLAR_STEPS - 1:
            inner = dot_three(halves(dot_three(halves(inner), fp)), fp)
    rp = halves(rot)
    corr_v = jnp.concatenate([corr_a, corr_b], axis=0)
    moved = dot_three(halves(corr_v), (rp[0][:modes], rp[1][:modes]))
    rb48 = tripled_right((rp[0][modes:], rp[1][modes:]))
    moved = moved + jnp.concatenate(
        [
            dot(tripled_left(halves(corr_b)), rb48, TN),
            dot(tripled_left(halves(corr_d)), rb48, TN),
        ],
        axis=0,
    )
    out_core[...] = dot_three(rp, halves(moved), TN)

    mix = dot_high(inverse, rot[modes:], TN)
    mix48 = tripled_right(halves(mix))
    ra = halves(rot[:modes] - dot(tripled_left(parts), mix48, TN))
    for part in range(4):
        rows = basis_rows[pl.ds(part * 256, 256), :]
        left = tripled_left(halves(snaps_ref[:, part * 256 : part * 256 + 256]))
        give_basis(dot_three(halves(rows), ra) + dot(left, mix48, TN), out_basis, part * 8)
    passing.wait()


def tail(core, coeffs, factor_t, inverse, snaps, basis_view, fields):
    vmem = pl.BlockSpec(memory_space=pltpu.VMEM)
    hbm = pl.BlockSpec(memory_space=pltpu.HBM)
    return pl.pallas_call(
        tail_kernel,
        out_shape=(
            jax.ShapeDtypeStruct(fields.shape, F32),
            jax.ShapeDtypeStruct((2048, 128), F32),
            jax.ShapeDtypeStruct((256, 256), F32),
        ),
        in_specs=[vmem, vmem, vmem, vmem, vmem, hbm, hbm],
        out_specs=(hbm, vmem, vmem),
        scratch_shapes=[
            pltpu.VMEM((272, 256), F32),
            pltpu.VMEM((16, 16), F32),
            pltpu.VMEM((2048, 128), F32),
            pltpu.VMEM((1024, 256), F32),
            pltpu.VMEM(fields.shape, F32),
            pltpu.SemaphoreType.DMA,
            pltpu.SemaphoreType.DMA,
        ],
        compiler_params=pltpu.CompilerParams(vmem_limit_bytes=60 * 1024 * 1024),
    )(core, coeffs, factor_t, inverse, snaps, basis_view, fields)


def view_of(basis):
    return basis.reshape(4, 128, 2, 2, 128).transpose(0, 1, 3, 2, 4).reshape(2048, 128)


def basis_of(view):
    return view.reshape(4, 128, 2, 2, 128).transpose(0, 1, 3, 2, 4).reshape(4, 128, 2, 256)


MESH = pl.DeviceIdType.MESH
press_coef = 0.25
compress_coef = 0.25
visc_coef = 0.05
heat_coef = 0.03
FIELDS = 5
least_pivot = 2.0**-7


def shifted(values):
    width = values.shape[-1]
    lane = lax.broadcasted_iota(jnp.int32, values.shape, 1)
    lower = jnp.where(lane == 0, 0.0, pltpu.roll(values, 1, 1))
    upper = jnp.where(lane == width - 1, 0.0, pltpu.roll(values, width - 1, 1))
    return lower, upper


class Fields:
    def __init__(self, read):
        self.read = read
        self.known = {}

    def __getitem__(self, f):
        if f not in self.known:
            self.known[f] = self.read(f)
        return self.known[f]


def update(centre, xl, xu, zl, zu, profiles, wanted=range(FIELDS)):
    courant, shear_rate, gradient = profiles
    beside = Fields(lambda f: shifted(centre[f]))
    keep = [1.0 - 6.0 * visc_coef - courant] * 3 + [1.0 - 6.0 * visc_coef]
    keep = keep + [1.0 - 6.0 * heat_coef - courant]
    bring = [visc_coef + courant] * 3 + [visc_coef, heat_coef + courant]
    spread = [visc_coef] * 4 + [heat_coef]
    half_press = 0.5 * press_coef
    sources = Fields(lambda f: (
        lambda: shear_rate * centre[1] + half_press * (xu[3] - xl[3]),
        lambda: half_press * (beside[3][1] - beside[3][0]),
        lambda: half_press * (zu[3] - zl[3]),
        lambda: 0.5 * compress_coef * (
            (xu[0] - xl[0]) + (beside[1][1] - beside[1][0]) + (zu[2] - zl[2])
        ),
        lambda: gradient * centre[1],
    )[f]())
    new = {}
    for f in wanted:
        around = (xu[f] + zl[f]) + (zu[f] + beside[f][0]) + beside[f][1]
        new[f] = keep[f] * centre[f] + bring[f] * xl[f] + spread[f] * around - sources[f]
    return new


def front_kernel(sizes, fields_hbm, courant_hbm, shear_hbm, gradient_hbm, earlier_hbm, basis_hbm,
                 out_fields, out_coeffs, out_factor, out_inverse, out_sound, out_snaps,
                 P, H, F, Zs, Zr, Cs, Cr, V, basis_view, basis_rows, basis_h, basis_l,
                 E2, early_send, early_slots, late_send, late_slots, S,
                 g_send, g_slots, g_mid, g_mid_slots, g_part, g_parts, g_whole, g_all,
                 e_send, e_slots, e_mid, e_mid_slots, e_part, e_all,
                 c_send, c_other, c_mid, c_slots,
                 earlier_ref, profile_rows, small_sem, load_sem, basis_sem, out_sem, halo_send, halo_recv,
                 group_send, group_recv):
    nx, nz = sizes
    gx = lax.axis_index("gx")
    gz = lax.axis_index("gz")
    rows_total = 1024.0 * nx * nz

    barrier = pltpu.get_barrier_semaphore()
    x_beside = (lax.rem(gx + nx - 1, nx), lax.rem(gx + 1, nx))
    z_beside = (lax.rem(gz + nz - 1, nz), lax.rem(gz + 1, nz))

    def greet(where):
        pl.semaphore_signal(barrier, inc=1, device_id=where, device_id_type=MESH)

    def greet_z(d, carry):
        greet((gx, lax.rem(gz + d, nz)))
        return carry

    load = pltpu.make_async_copy(fields_hbm, P.at[:, 2:18, 8:24, :], load_sem)
    load.start()
    fetch = pltpu.make_async_copy(basis_hbm, basis_view, basis_sem)
    fetch.start()
    small = [
        pltpu.make_async_copy(earlier_hbm, earlier_ref, small_sem.at[0]),
        pltpu.make_async_copy(courant_hbm, profile_rows.at[0], small_sem.at[1]),
        pltpu.make_async_copy(shear_hbm, profile_rows.at[1], small_sem.at[2]),
        pltpu.make_async_copy(gradient_hbm, profile_rows.at[2], small_sem.at[3]),
    ]
    for copy in small:
        copy.start()
    for d in range(1, nx):
        greet((lax.rem(gx + d, nx), gz))
    for xs in range(2):
        for zs in range(2):
            greet((x_beside[xs], z_beside[zs]))
    for d in range(1, nx):
        greet((lax.rem(gx + d, nx), gz + 1 - 2 * lax.rem(gz, 2)))
    lax.fori_loop(1, nz, greet_z, 0)

    for copy in small:
        copy.wait()
    E2[...] = jnp.zeros_like(E2)
    for m in range(14):
        for x in range(4):
            E2[x * 16 + m : x * 16 + m + 1, :] = earlier_ref[m, x : x + 1, :]
    turned = E2[...].T
    turned = jnp.concatenate([turned[64 * z : 64 * z + 64] for z in range(4)], axis=1)
    for i in range(32):
        early_send[i] = turned[2 * i : 2 * i + 2]
    pl.semaphore_wait(barrier, nz - 1 + 2 * (nx - 1) + 4)

    def spread_z(place, source, slots):
        def body(d, carry):
            peer = lax.rem(gz + d, nz)
            pltpu.make_async_remote_copy(
                src_ref=source(peer), dst_ref=slots.at[gz], send_sem=group_send.at[place],
                recv_sem=group_recv.at[place], device_id=(gx, peer), device_id_type=MESH,
            ).start()
            return carry

        lax.fori_loop(1, nz, body, 0)

    spread_z(0, lambda peer: early_send.at[peer], early_slots)
    early_slots[gz] = early_send[gz]

    load.wait()

    halos = []

    def send_halo(source, target, where):
        place = len(halos)
        copy = pltpu.make_async_remote_copy(
            src_ref=source, dst_ref=target, send_sem=halo_send.at[place],
            recv_sem=halo_recv.at[place], device_id=where, device_id_type=MESH,
        )
        copy.start()
        halos.append(copy)

    def send_x(side, fields, layers):
        first_own = 2 + 14 * side + layers[0]
        first_there = 18 - 18 * side + layers[0]
        send_halo(
            P.at[fields, first_own : first_own + len(layers), 8:24, :],
            P.at[fields, first_there : first_there + len(layers), 8:24, :],
            (x_beside[side], gz),
        )

    def send_z(side, layer, fields):
        send_halo(
            Zs.at[side, layer, fields, 8:24, :],
            Zr.at[1 - side, layer, fields, 8:24, :],
            (gx, z_beside[side]),
        )

    for side in range(2):
        send_x(side, pl.ds(0, 1), (0, 1))
        send_x(side, pl.ds(3, 1), (0, 1))
        send_x(side, pl.ds(1, 2), (side,))

    for side in range(2):
        for layer in range(2):
            z = 8 + 14 * side + layer
            for f in range(FIELDS):
                for half in range(2):
                    lanes = pl.ds(128 * half, 128)
                    Zs[side, layer, f, 8:24, lanes] = P[f, 2:18, z, lanes]
    for xs in range(2):
        for zs in range(2):
            for f in range(FIELDS):
                Cs[2 * xs + zs, f : f + 1, :] = P[f, 2 + 15 * xs, 8 + 15 * zs : 9 + 15 * zs, :]

    for side in range(2):
        send_z(side, side, pl.ds(0, 4))
        send_z(side, 1 - side, pl.ds(0, 1))
    for xs in range(2):
        for zs in range(2):
            send_halo(
                Cs.at[2 * xs + zs], Cr.at[2 * (1 - xs) + 1 - zs], (x_beside[xs], z_beside[zs])
            )
    urgent = len(halos)

    yz = gz // 2
    places = nz // 2
    along = (lax.rem(gz, 2) * (nx // 2) + gx // 2) * 2 + lax.rem(gx, 2)
    line = 2 * nx

    def spread_yz(place, source, slots):
        def body(d, carry):
            peer = lax.rem(yz + d, places)
            pltpu.make_async_remote_copy(
                src_ref=source(peer), dst_ref=slots.at[yz], send_sem=group_send.at[place],
                recv_sem=group_recv.at[place], device_id=(gx, 2 * peer + lax.rem(gz, 2)),
                device_id_type=MESH,
            ).start()
            return carry

        lax.fori_loop(1, places, body, 0)

    def spread_line(place, source, slots):
        def body(d, carry):
            peer = lax.rem(along + d, line)
            where = (lax.rem(peer, nx), 2 * yz + peer // nx)
            pltpu.make_async_remote_copy(
                src_ref=source(peer), dst_ref=slots.at[along], send_sem=group_send.at[place],
                recv_sem=group_recv.at[place], device_id=where, device_id_type=MESH,
            ).start()
            return carry

        lax.fori_loop(1, line, body, 0)

    core = lax.rem(gx, 2)
    chip = (gx // 2) * nz + gz
    chips = (nx // 2) * nz

    def send_core(place, source, target):
        pltpu.make_async_remote_copy(
            src_ref=source, dst_ref=target, send_sem=group_send.at[place],
            recv_sem=group_recv.at[place], device_id=(gx + 1 - 2 * core, gz), device_id_type=MESH,
        ).start()

    def spread_chips(place, source, slots):
        def body(d, carry):
            peer = lax.rem(chip + d, chips)
            where = (2 * (peer // nz) + core, lax.rem(peer, nz))
            pltpu.make_async_remote_copy(
                src_ref=source, dst_ref=slots.at[chip], send_sem=group_send.at[place],
                recv_sem=group_recv.at[place], device_id=where, device_id_type=MESH,
            ).start()
            return carry

        lax.fori_loop(1, chips, body, 0)

    def wait_one(sems, place, part):
        pltpu.make_async_copy(part, part, sems.at[place]).wait()

    def sum_slots_of(slots):
        terms = [slots[j] for j in range(slots.shape[0])]
        while len(terms) > 1:
            terms = [a + b for a, b in zip(terms[::2], terms[1::2])] + terms[len(terms) & ~1 :]
        return terms[0]

    def wait_all(sems, place, slots):
        some = slots.at[pl.ds(0, slots.shape[0] - 1)]
        pltpu.make_async_copy(some, some, sems.at[place]).wait()

    fetch.wait()
    take_basis(basis_view, basis_rows)
    rows = basis_rows[...]
    head = rows.astype(BF16)
    basis_h[...] = head
    basis_l[...] = (rows - head.astype(F32)).astype(BF16)

    def pair():
        return basis_h[...], basis_l[...]

    inner = dot_three(pair(), pair(), TN)
    for i in range(16):
        g_send[i, :, :256] = inner[8 * i : 8 * i + 8]
        g_send[i, :, 256:] = inner[128 + 8 * i : 136 + 8 * i, 128:]
    spread_yz(1, lambda peer: g_send.at[peer], g_slots)
    g_slots[yz] = g_send[yz]
    for side in range(2):
        send_x(side, pl.ds(1, 2), (1 - side,))
        send_x(side, pl.ds(4, 1), (0, 1))
        send_z(side, side, pl.ds(4, 1))
        send_z(side, 1 - side, pl.ds(1, 4))

    profiles = [profile_rows[k] for k in range(3)]

    def first(i, wanted=range(FIELDS)):
        centre = Fields(lambda f: P[f, i + 1, 8:24, :])
        xl = Fields(lambda f: P[f, i, 8:24, :])
        xu = Fields(lambda f: P[f, i + 2, 8:24, :])
        zl = Fields(lambda f: P[f, i + 1, 7:23, :])
        zu = Fields(lambda f: P[f, i + 1, 9:25, :])
        for f, new in update(centre, xl, xu, zl, zu, profiles, wanted).items():
            H[f, i, 8:24, :] = new

    def first_inside(i, carry):
        first(i)
        return carry

    lax.fori_loop(2, 16, first_inside, 0)

    wait_all(group_recv, 0, early_slots)
    got = jnp.concatenate([early_slots[:, 0, :], early_slots[:, 1, :]], axis=0).T
    for zx in range(16):
        S[:, zx * 64 : zx * 64 + 64] = got[zx * 16 : zx * 16 + 16]
    snaps = halves(S[...])
    c_early = dot_three(snaps, pair())
    k_early = dot_three(snaps, snaps, NT)
    early = jnp.concatenate([c_early, k_early, jnp.zeros((16, 112), F32)], axis=1)
    for m in range(16):
        e_send[m] = early[m : m + 1]
    spread_yz(8, lambda peer: e_send.at[peer], e_slots)
    e_slots[yz] = e_send[yz]

    for copy in halos[:urgent]:
        copy.wait_recv()

    def fill_corners(fields):
        for f in fields:
            for xs in range(2):
                row = 7 + 17 * xs
                x = 1 + 17 * xs
                for zs in range(2):
                    corner = Cr[2 * xs + zs, f : f + 1, :]
                    Zr[zs, 1 - zs, f, row : row + 1, :] = corner
                    P[f, x, 7 + 17 * zs : 8 + 17 * zs, :] = corner
                    Zs[zs, zs, f, row : row + 1, :] = P[f, x, 8 + 15 * zs : 9 + 15 * zs, :]

    def first_edges(outside_x, outside_z, inside):
        def outside_rows(k, carry):
            first(17 * k, outside_x)
            return carry

        def inside_rows(k, carry):
            first(1 + 15 * k, inside)
            return carry

        lax.fori_loop(0, 2, outside_rows, 0)
        lax.fori_loop(0, 2, inside_rows, 0)
        for side in range(2):
            layers = [
                Zr.at[side, side], Zr.at[side, 1 - side], Zs.at[side, side], Zs.at[side, 1 - side]
            ]
            for edge in range(2):
                edge_layer(side, edge, layers[edge : edge + 3], (outside_z, inside)[edge])

    def edge_layer(side, edge, layers, wanted):
        outer, mid, inside = layers
        centre = Fields(lambda f: mid[f, 8:24, :])
        xl = Fields(lambda f: mid[f, 7:23, :])
        xu = Fields(lambda f: mid[f, 9:25, :])
        out = Fields(lambda f: outer[f, 8:24, :])
        within = Fields(lambda f: inside[f, 8:24, :])
        zl, zu = (out, within) if side == 0 else (within, out)
        z = 7 + edge if side == 0 else 24 - edge
        for f, new in update(centre, xl, xu, zl, zu, profiles, wanted).items():
            H[f, 1:17, z, :] = new

    wait_all(group_recv, 1, g_slots)
    total = sum_slots_of(g_slots)
    for r in range(8):
        g_mid[r] = total[r : r + 1]
    spread_line(3, lambda peer: g_mid.at[peer], g_mid_slots)
    g_mid_slots[along] = g_mid[along]

    fill_corners(range(4))
    first_edges((0, 3), (0,), (0, 1, 3))

    def second(wanted):
        def row(i, carry):
            centre = Fields(lambda f: H[f, i + 1, 8:24, :])
            xl = Fields(lambda f: H[f, i, 8:24, :])
            xu = Fields(lambda f: H[f, i + 2, 8:24, :])
            zl = Fields(lambda f: H[f, i + 1, 7:23, :])
            zu = Fields(lambda f: H[f, i + 1, 9:25, :])
            for f, new in update(centre, xl, xu, zl, zu, profiles, wanted).items():
                F[f, i, :, :] = new
            return carry

        lax.fori_loop(0, 16, row, 0)

    second((0,))

    for xg in range(4):
        V[16 * xg : 16 * xg + 16, :] = (H[0, 4 * xg + 1, 8:24, :] + H[0, 4 * xg + 2, 8:24, :]) + (
            H[0, 4 * xg + 3, 8:24, :] + H[0, 4 * xg + 4, 8:24, :]
        )
        V[64 + 16 * xg : 80 + 16 * xg, :] = (F[0, 4 * xg] + F[0, 4 * xg + 1]) + (
            F[0, 4 * xg + 2] + F[0, 4 * xg + 3]
        )
    to = lax.broadcasted_iota(jnp.int32, (128, 128), 0)
    of = lax.broadcasted_iota(jnp.int32, (128, 128), 1)
    wanted = ((lax.rem(of, 16) // 4) * 4 + lax.rem(of, 64) // 16) * 8 + 6 + of // 64
    place_to = (to == wanted).astype(BF16)
    sums = halves(V[...])
    gathered = dot(
        jnp.concatenate([place_to, place_to], axis=1), jnp.concatenate(sums, axis=0)
    )
    block = (
        lax.broadcasted_iota(jnp.int32, (64, 256), 0)
        == lax.broadcasted_iota(jnp.int32, (64, 256), 1) // 4
    ).astype(BF16) * BF16(1.0 / 64.0)
    coarse = dot(
        jnp.concatenate([block, block], axis=1), jnp.concatenate(halves(gathered), axis=1), NT
    )
    for i in range(32):
        late_send[i] = coarse[2 * i : 2 * i + 2]
    spread_z(2, lambda peer: late_send.at[peer], late_slots)
    late_slots[gz] = late_send[gz]

    wait_all(group_recv, 8, e_slots)
    e_mid[...] = sum_slots_of(e_slots)
    spread_line(9, lambda peer: e_mid, e_mid_slots)
    e_mid_slots[along] = e_mid[...]

    wait_all(group_recv, 3, g_mid_slots)
    g_part[...] = sum_slots_of(g_mid_slots)
    spread_line(5, lambda peer: g_part, g_parts)
    g_parts[along] = g_part[...]

    for copy in halos[urgent:]:
        copy.wait_recv()
    fill_corners((4,))
    first_edges((1, 2, 4), (1, 2, 3, 4), (2, 4))
    second((1, 2, 3, 4))
    store = pltpu.make_async_copy(F, out_fields, out_sem)
    store.start()

    wait_all(group_recv, 5, g_parts)
    for r in range(8):
        g_whole[r : r + 1, :] = g_parts[r]
    spread_yz(7, lambda peer: g_whole, g_all)
    g_all[yz] = g_whole[...]

    wait_all(group_recv, 9, e_mid_slots)
    e_part[...] = sum_slots_of(e_mid_slots)
    spread_yz(10, lambda peer: e_part, e_all)
    e_all[yz] = e_part[...]

    wait_all(group_recv, 2, late_slots)
    got = jnp.concatenate([late_slots[:, 0, :], late_slots[:, 1, :]], axis=0).T
    for zx in range(16):
        S[8:16, zx * 64 : zx * 64 + 64] = S[8:16, zx * 64 : zx * 64 + 64] + got[zx * 8 : zx * 8 + 8]
    out_snaps[...] = S[...]
    low = S[8:16, :]
    low = jnp.where(lax.broadcasted_iota(jnp.int32, low.shape, 0) >= 6, low, 0.0)
    late = halves(jnp.concatenate([jnp.zeros_like(low), low], axis=0))
    both = dot(jnp.concatenate(late, axis=0), basis_h[...])
    c_late = (both[:16] + both[16:] + dot(late[0], basis_l[...]))[14:16]
    k_late = dot_three(late, halves(S[...]), NT)[14:16]
    late = jnp.concatenate([c_late, k_late, jnp.zeros((2, 112), F32)], axis=1)
    c_send[...] = late
    send_core(4, c_send, c_other)
    wait_one(group_recv, 4, c_other)
    both = late + c_other[...]
    c_mid[...] = both
    spread_chips(6, c_mid, c_slots)
    c_slots[chip] = both

    wait_all(group_recv, 7, g_all)
    every = g_all[...].reshape(128, 384)
    cross = every[:, 128:256]
    metric = jnp.concatenate(
        [every[:, :256], jnp.concatenate([cross.T, every[:, 256:]], axis=1)], axis=0
    ) * (1.0 / rows_total)
    unit = eye(256)
    removed = 4.0 * unit - 6.0 * metric + dot_high(dot_high(metric, metric), 4.0 * unit - metric)
    wait_all(group_recv, 10, e_all)
    early = e_all[...].reshape(16, 384) * (1.0 / rows_total)
    c_early = early[:, :256]
    identity = eye(16)
    gram = early[:, 256:272] - dot_high(dot_high(c_early, removed), c_early, NT)
    left, right, pivots = eliminate(
        gram + gram_eps * identity, identity, jnp.zeros((1, 16), F32), range(14)
    )
    low_row = lax.broadcasted_iota(jnp.int32, (16, 16), 0) >= 14
    low_col = lax.broadcasted_iota(jnp.int32, (16, 16), 1) >= 14

    wait_all(group_recv, 6, c_slots)
    total = jnp.concatenate([early[:14], sum_slots_of(c_slots) * (1.0 / rows_total)], axis=0)
    c_one = total[:, :256]
    size = total[:, 256:272]
    out_coeffs[...] = 2.0 * c_one - dot_high(c_one, metric)
    gram = size - dot_high(dot_high(c_one, removed), c_one, NT) + gram_eps * identity
    across = dot_high(jnp.where(low_row & ~low_col, gram, 0.0), right, NT)
    corner = jnp.where(low_row & low_col, gram, 0.0) - dot_high(across, across, NT)
    left, right, pivots = eliminate(
        jnp.where(low_row, corner, left + across.T), right - dot_high(across, right), pivots,
        range(14, 16),
    )
    upper = lax.broadcasted_iota(jnp.int32, (16, 16), 0) <= lax.broadcasted_iota(
        jnp.int32, (16, 16), 1
    )
    out_factor[...] = jnp.where(upper, left, 0.0)
    out_inverse[...] = right
    scale = jnp.sum(jnp.where(identity > 0.0, size, 0.0), axis=0, keepdims=True)
    sound = jnp.where(pivots > least_pivot * scale, 1, 0)
    out_sound[0, 0] = jnp.min(sound)

    for copy in halos:
        copy.wait_send()
    for place, slots in (
        (0, early_slots), (1, g_slots), (2, late_slots), (3, g_mid_slots), (5, g_parts),
        (6, c_slots), (7, g_all), (8, e_slots), (9, e_mid_slots), (10, e_all),
    ):
        wait_all(group_send, place, slots)
    wait_one(group_send, 4, c_other)
    store.wait()


def front(sizes, fields, profiles, earlier, basis_view):
    nx, nz = sizes
    vmem = pl.BlockSpec(memory_space=pltpu.VMEM)
    hbm = pl.BlockSpec(memory_space=pltpu.HBM)
    smem = pl.BlockSpec(memory_space=pltpu.SMEM)
    v = pltpu.VMEM
    return pl.pallas_call(
        functools.partial(front_kernel, sizes),
        out_shape=(
            jax.ShapeDtypeStruct(fields.shape, F32),
            jax.ShapeDtypeStruct((16, 256), F32),
            jax.ShapeDtypeStruct((16, 16), F32),
            jax.ShapeDtypeStruct((16, 16), F32),
            jax.ShapeDtypeStruct((1, 1), jnp.int32),
            jax.ShapeDtypeStruct((16, 1024), F32),
        ),
        in_specs=[hbm] * 6,
        out_specs=(hbm, vmem, vmem, vmem, smem, vmem),
        scratch_shapes=[
            v((5, 20, 32, 256), F32),
            v((5, 18, 32, 256), F32),
            v((5, 16, 16, 256), F32),
            v((2, 2, 5, 32, 256), F32),
            v((2, 2, 5, 32, 256), F32),
            v((4, 8, 256), F32),
            v((4, 8, 256), F32),
            v((128, 256), F32),
            v((2048, 128), F32),
            v((1024, 256), F32),
            v((1024, 256), BF16),
            v((1024, 256), BF16),
            v((64, 256), F32),
            v((32, 2, 256), F32),
            v((32, 2, 256), F32),
            v((32, 2, 128), F32),
            v((32, 2, 128), F32),
            v((16, 1024), F32),
            v((16, 8, 384), F32),
            v((16, 8, 384), F32),
            v((8, 1, 384), F32),
            v((8, 1, 384), F32),
            v((1, 384), F32),
            v((8, 1, 384), F32),
            v((8, 384), F32),
            v((16, 8, 384), F32),
            v((16, 1, 384), F32),
            v((16, 1, 384), F32),
            v((1, 384), F32),
            v((8, 1, 384), F32),
            v((1, 384), F32),
            v((16, 1, 384), F32),
            v((2, 384), F32),
            v((2, 384), F32),
            v((2, 384), F32),
            v((64, 2, 384), F32),
            v((14, 4, 256), F32),
            v((3, 1, 256), F32),
            pltpu.SemaphoreType.DMA((4,)),
            pltpu.SemaphoreType.DMA,
            pltpu.SemaphoreType.DMA,
            pltpu.SemaphoreType.DMA,
            pltpu.SemaphoreType.DMA((22,)),
            pltpu.SemaphoreType.DMA((22,)),
            pltpu.SemaphoreType.DMA((11,)),
            pltpu.SemaphoreType.DMA((11,)),
        ],
        compiler_params=pltpu.CompilerParams(
            collective_id=0, has_side_effects=True, vmem_limit_bytes=62 * 1024 * 1024
        ),
    )(fields, *profiles, earlier, basis_view)


def direct_factor(snaps, coeffs, basis_modes):
    rows_total = 1024.0 * lax.axis_size("gx") * lax.axis_size("gz")
    rows = basis_modes.reshape(4, 32, 4, 2, 256).transpose(2, 0, 3, 1, 4).reshape(1024, 256)
    resid = snaps - jnp.dot(coeffs, rows.T, precision=HIGH)
    gram = lax.psum(jnp.dot(resid, resid.T, precision=HIGH), ("gx", "gz")) / rows_total
    identity = jnp.eye(16, dtype=F32)
    factor = jnp.linalg.cholesky(gram + gram_eps * identity)
    return factor.T, jax.scipy.linalg.solve_triangular(factor, identity, lower=True)


def on_device(fields, courant, shear_rate, gradient, earlier, basis_modes, core_matrix):
    sizes = (lax.axis_size("gx"), lax.axis_size("gz"))
    view = view_of(basis_modes)
    profiles = [p.reshape(1, -1) for p in (courant, shear_rate, gradient)]
    finished, coeffs, factor_t, inverse, sound, snaps = front(
        sizes, fields, profiles, earlier, view
    )
    factor_t, inverse = lax.cond(
        sound[0, 0] > 0,
        lambda snaps, coeffs, basis_modes, factor_t, inverse: (factor_t, inverse),
        lambda snaps, coeffs, basis_modes, factor_t, inverse: direct_factor(
            snaps, coeffs, basis_modes
        ),
        snaps, coeffs, basis_modes, factor_t, inverse,
    )
    finished, new_view, new_core = tail(
        core_matrix, coeffs, factor_t, inverse, snaps, view, finished
    )
    return (finished, basis_of(new_view), new_core)


def solution(mesh):
    return jax.shard_map(
        on_device,
        mesh=mesh,
        in_specs=(
            P(None, "gx", "gz", None),
            P(),
            P(),
            P(),
            P(None, "gx", "gz"),
            P("gx", None, "gz", None),
            P(),
        ),
        out_specs=(P(None, "gx", "gz", None), P("gx", None, "gz", None), P()),
        check_vma=False,
    )
```

```python
import functools

import jax
import jax.numpy as jnp
from jax import lax
from jax.experimental import pallas as pl
from jax.experimental.pallas import tpu as pltpu
from jax.sharding import PartitionSpec as P

F32, BF16 = jnp.float32, jnp.bfloat16
HIGH = lax.Precision.HIGHEST
SIGN_STEPS = 10
POLAR_STEPS = 3
gram_eps = 1e-06


def halves(values):
    head = values.astype(BF16)
    return head, (values - head.astype(F32)).astype(BF16)


def dot(left, right, over=((1,), (0,))):
    return lax.dot_general(left, right, (over, ((), ())), preferred_element_type=F32)


def dot_three(left, right, over=((1,), (0,))):
    (lh, ll), (rh, rl) = left, right
    return dot(lh, rh, over) + (dot(lh, rl, over) + dot(ll, rh, over))


def dot_high(left, right, over=((1,), (0,))):
    return lax.dot_general(
        left, right, (over, ((), ())), precision=HIGH, preferred_element_type=F32
    )


TN = ((0,), (0,))
NT = ((1,), (1,))


def tripled_left(pair):
    return jnp.concatenate([pair[0], pair[0], pair[1]], axis=0)


def tripled_right(pair):
    return jnp.concatenate([pair[0], pair[1], pair[0]], axis=0)


def eye(count):
    return (
        lax.broadcasted_iota(jnp.int32, (count, count), 0)
        == lax.broadcasted_iota(jnp.int32, (count, count), 1)
    ).astype(F32)


def row_places(z_lanes):
    places = []
    for zc in range(4):
        for x in range(4):
            for y in range(2):
                places.append((zc, x, y))
    return places


def take_basis(view_ref, rows_ref):
    for place, (zc, x, y) in enumerate(row_places(0)):
        for half in range(2):
            rows_ref[pl.ds(place * 32, 32), pl.ds(half * 128, 128)] = view_ref[
                pl.ds(512 * x + 4 * zc + 2 * half + y, 32, stride=16), :
            ]


def give_basis(rows, view_ref, first):
    for step in range(8):
        zc, x, y = row_places(0)[first + step]
        for half in range(2):
            view_ref[pl.ds(512 * x + 4 * zc + 2 * half + y, 32, stride=16), :] = rows[
                step * 32 : step * 32 + 32, half * 128 : half * 128 + 128
            ]


def eliminate(left, right, pivots, columns):
    row_index = lax.broadcasted_iota(jnp.int32, left.shape, 0)
    col_index = lax.broadcasted_iota(jnp.int32, pivots.shape, 1)
    for j in columns:
        pivot = left[j : j + 1, j : j + 1]
        pivots = jnp.where(col_index == j, pivot, pivots)
        scale = lax.rsqrt(pivot)
        scale = scale * (1.5 - 0.5 * pivot * scale * scale)
        column = left[:, j : j + 1] * scale
        row_l = left[j : j + 1, :] * scale
        row_r = right[j : j + 1, :] * scale
        below = row_index > j
        here = row_index == j
        left = jnp.where(below, left - column * row_l, jnp.where(here, row_l, left))
        right = jnp.where(below, right - column * row_r, jnp.where(here, row_r, right))
    return left, right, pivots


def wide_left(v, d):
    modes = v.shape[1]
    vh, vl = halves(v)
    dh, dl = halves(d)
    bh, bl = vh[modes:].astype(F32), vl[modes:].astype(F32)
    turned = jnp.concatenate([bh, bh, bl], axis=0).T.astype(BF16)
    edge = jnp.concatenate([turned, jnp.concatenate([dh, dh, dl], axis=1)], axis=0)
    return vh, vl, edge, jnp.concatenate([vh[modes:], vh[modes:], vl[modes:], edge[modes:]], axis=1)


def product(left, right_v, right_d):
    modes = right_v.shape[1]
    rh, rl = halves(right_v)
    dh, dl = halves(right_d)
    ah, bh = rh[:modes], rh[modes:]
    al, bl = rl[:modes], rl[modes:]
    stacked = jnp.concatenate([ah, al, ah, bh, bl, bh], axis=0)
    low = jnp.concatenate([bh, bl, bh, dh, dl, dh], axis=1)
    vh, vl, edge, wide = left
    thin = jnp.concatenate([bh, bl, bh], axis=0)
    top = (dot(vh[:modes], ah) + dot(vh[:modes], al)) + (dot(vl[:modes], ah) + dot(edge[:modes], thin))
    bottom = dot(wide, jnp.concatenate([ah, al, ah, thin], axis=0))
    return jnp.concatenate([top, bottom], axis=0), dot(wide, low, NT)


def tail_kernel(core_ref, coeffs_ref, factor_ref, inverse_ref, snaps_ref, basis_hbm, fields_hbm,
                out_fields, out_basis, out_core, v_ref, d_ref, basis_view, basis_rows, held, sem, field_sem):
    modes = core_ref.shape[0]
    fetch = pltpu.make_async_copy(basis_hbm, basis_view, sem)
    fetch.start()
    taking = pltpu.make_async_copy(fields_hbm, held, field_sem)
    taking.start()
    factor_t = factor_ref[...]
    inverse = inverse_ref[...]
    coeffs = coeffs_ref[...]
    unit = eye(modes)
    unit_d = eye(16)
    parts = halves(coeffs)
    corr_a = core_ref[...] + dot(tripled_left(parts), tripled_right(parts), TN)
    corr_b = dot_high(factor_t, coeffs)
    corr_d = dot_high(factor_t, factor_t, NT)
    shift_a = corr_a - unit
    shift_d = corr_d - unit_d
    total = (
        jnp.sum(shift_a * shift_a, keepdims=True)
        + 2.0 * jnp.sum(corr_b * corr_b, keepdims=True)
        + jnp.sum(shift_d * shift_d, keepdims=True)
    )
    scale = 1.0 / jnp.sqrt(total)
    v_ref[:modes] = shift_a * scale
    v_ref[modes:] = corr_b * scale
    d_ref[...] = shift_d * scale
    unit_v = jnp.concatenate([unit, jnp.zeros((16, modes), F32)], axis=0)

    def sign_step(step, carry):
        v = v_ref[...]
        d = d_ref[...]
        left = wide_left(v, d)
        square_v, square_d = product(left, v, d)
        next_v, next_d = product(
            left, 1.5 * unit_v - 0.5 * square_v, 1.5 * unit_d - 0.5 * square_d
        )
        v_ref[...] = next_v
        d_ref[...] = next_d
        return carry

    lax.fori_loop(0, SIGN_STEPS, sign_step, 0)

    fetch.wait()
    taking.wait()
    passing = pltpu.make_async_copy(held, out_fields, field_sem)
    passing.start()
    take_basis(basis_view, basis_rows)

    rot = 0.5 * (unit_v + v_ref[...])
    pair = halves(rot)
    top = (pair[0][:modes], pair[1][:modes])
    low = (pair[0][modes:], pair[1][modes:])
    inner = dot_three(top, top) + dot(tripled_left(low), tripled_right(low), TN)
    for step in range(POLAR_STEPS):
        factor = 1.5 * unit - 0.5 * inner
        fp = halves(factor)
        rot = dot_three(halves(rot), fp)
        if step < POLAR_STEPS - 1:
            inner = dot_three(halves(dot_three(halves(inner), fp)), fp)
    rp = halves(rot)
    corr_v = jnp.concatenate([corr_a, corr_b], axis=0)
    moved = dot_three(halves(corr_v), (rp[0][:modes], rp[1][:modes]))
    rb48 = tripled_right((rp[0][modes:], rp[1][modes:]))
    moved = moved + jnp.concatenate(
        [
            dot(tripled_left(halves(corr_b)), rb48, TN),
            dot(tripled_left(halves(corr_d)), rb48, TN),
        ],
        axis=0,
    )
    out_core[...] = dot_three(rp, halves(moved), TN)

    mix = dot_high(inverse, rot[modes:], TN)
    mix48 = tripled_right(halves(mix))
    ra = halves(rot[:modes] - dot(tripled_left(parts), mix48, TN))
    for part in range(4):
        rows = basis_rows[pl.ds(part * 256, 256), :]
        left = tripled_left(halves(snaps_ref[:, part * 256 : part * 256 + 256]))
        give_basis(dot_three(halves(rows), ra) + dot(left, mix48, TN), out_basis, part * 8)
    passing.wait()


def tail(core, coeffs, factor_t, inverse, snaps, basis_view, fields):
    vmem = pl.BlockSpec(memory_space=pltpu.VMEM)
    hbm = pl.BlockSpec(memory_space=pltpu.HBM)
    return pl.pallas_call(
        tail_kernel,
        out_shape=(
            jax.ShapeDtypeStruct(fields.shape, F32),
            jax.ShapeDtypeStruct((2048, 128), F32),
            jax.ShapeDtypeStruct((256, 256), F32),
        ),
        in_specs=[vmem, vmem, vmem, vmem, vmem, hbm, hbm],
        out_specs=(hbm, vmem, vmem),
        scratch_shapes=[
            pltpu.VMEM((272, 256), F32),
            pltpu.VMEM((16, 16), F32),
            pltpu.VMEM((2048, 128), F32),
            pltpu.VMEM((1024, 256), F32),
            pltpu.VMEM(fields.shape, F32),
            pltpu.SemaphoreType.DMA,
            pltpu.SemaphoreType.DMA,
        ],
        compiler_params=pltpu.CompilerParams(vmem_limit_bytes=60 * 1024 * 1024),
    )(core, coeffs, factor_t, inverse, snaps, basis_view, fields)


def view_of(basis):
    return basis.reshape(4, 128, 2, 2, 128).transpose(0, 1, 3, 2, 4).reshape(2048, 128)


def basis_of(view):
    return view.reshape(4, 128, 2, 2, 128).transpose(0, 1, 3, 2, 4).reshape(4, 128, 2, 256)


MESH = pl.DeviceIdType.MESH
press_coef = 0.25
compress_coef = 0.25
visc_coef = 0.05
heat_coef = 0.03
FIELDS = 5
least_pivot = 2.0**-7


def shifted(values):
    width = values.shape[-1]
    lane = lax.broadcasted_iota(jnp.int32, values.shape, 1)
    lower = jnp.where(lane == 0, 0.0, pltpu.roll(values, 1, 1))
    upper = jnp.where(lane == width - 1, 0.0, pltpu.roll(values, width - 1, 1))
    return lower, upper


class Fields:
    def __init__(self, read):
        self.read = read
        self.known = {}

    def __getitem__(self, f):
        if f not in self.known:
            self.known[f] = self.read(f)
        return self.known[f]


def update(centre, xl, xu, zl, zu, profiles, wanted=range(FIELDS)):
    courant, shear_rate, gradient = profiles
    beside = Fields(lambda f: shifted(centre[f]))
    keep = [1.0 - 6.0 * visc_coef - courant] * 3 + [1.0 - 6.0 * visc_coef]
    keep = keep + [1.0 - 6.0 * heat_coef - courant]
    bring = [visc_coef + courant] * 3 + [visc_coef, heat_coef + courant]
    spread = [visc_coef] * 4 + [heat_coef]
    half_press = 0.5 * press_coef
    sources = Fields(lambda f: (
        lambda: shear_rate * centre[1] + half_press * (xu[3] - xl[3]),
        lambda: half_press * (beside[3][1] - beside[3][0]),
        lambda: half_press * (zu[3] - zl[3]),
        lambda: 0.5 * compress_coef * (
            (xu[0] - xl[0]) + (beside[1][1] - beside[1][0]) + (zu[2] - zl[2])
        ),
        lambda: gradient * centre[1],
    )[f]())
    new = {}
    for f in wanted:
        around = (xu[f] + zl[f]) + (zu[f] + beside[f][0]) + beside[f][1]
        new[f] = keep[f] * centre[f] + bring[f] * xl[f] + spread[f] * around - sources[f]
    return new


def front_kernel(sizes, fields_hbm, courant_hbm, shear_hbm, gradient_hbm, earlier_hbm, basis_hbm,
                 out_fields, out_coeffs, out_factor, out_inverse, out_sound, out_snaps,
                 P, H, F, Zs, Zr, Cs, Cr, V, basis_view, basis_rows, basis_h, basis_l,
                 E2, early_send, early_slots, late_send, late_slots, S,
                 g_send, g_slots, g_mid, g_mid_slots, g_part, g_parts, g_whole, g_all,
                 e_send, e_slots, e_mid, e_mid_slots, e_part, e_all,
                 c_send, c_other, c_mid, c_slots,
                 earlier_ref, profile_rows, small_sem, load_sem, basis_sem, out_sem, halo_send, halo_recv,
                 group_send, group_recv):
    nx, nz = sizes
    gx = lax.axis_index("gx")
    gz = lax.axis_index("gz")
    rows_total = 1024.0 * nx * nz

    barrier = pltpu.get_barrier_semaphore()
    x_beside = (lax.rem(gx + nx - 1, nx), lax.rem(gx + 1, nx))
    z_beside = (lax.rem(gz + nz - 1, nz), lax.rem(gz + 1, nz))

    def greet(where):
        pl.semaphore_signal(barrier, inc=1, device_id=where, device_id_type=MESH)

    def greet_z(d, carry):
        greet((gx, lax.rem(gz + d, nz)))
        return carry

    load = pltpu.make_async_copy(fields_hbm, P.at[:, 2:18, 8:24, :], load_sem)
    load.start()
    fetch = pltpu.make_async_copy(basis_hbm, basis_view, basis_sem)
    fetch.start()
    small = [
        pltpu.make_async_copy(earlier_hbm, earlier_ref, small_sem.at[0]),
        pltpu.make_async_copy(courant_hbm, profile_rows.at[0], small_sem.at[1]),
        pltpu.make_async_copy(shear_hbm, profile_rows.at[1], small_sem.at[2]),
        pltpu.make_async_copy(gradient_hbm, profile_rows.at[2], small_sem.at[3]),
    ]
    for copy in small:
        copy.start()
    for d in range(1, nx):
        greet((lax.rem(gx + d, nx), gz))
    for xs in range(2):
        for zs in range(2):
            greet((x_beside[xs], z_beside[zs]))
    for d in range(1, nx):
        greet((lax.rem(gx + d, nx), gz + 1 - 2 * lax.rem(gz, 2)))
    lax.fori_loop(1, nz, greet_z, 0)

    for copy in small:
        copy.wait()
    E2[...] = jnp.zeros_like(E2)
    for m in range(14):
        for x in range(4):
            E2[x * 16 + m : x * 16 + m + 1, :] = earlier_ref[m, x : x + 1, :]
    turned = E2[...].T
    turned = jnp.concatenate([turned[64 * z : 64 * z + 64] for z in range(4)], axis=1)
    for i in range(32):
        early_send[i] = turned[2 * i : 2 * i + 2]
    pl.semaphore_wait(barrier, nz - 1 + 2 * (nx - 1) + 4)

    def spread_z(place, source, slots):
        def body(d, carry):
            peer = lax.rem(gz + d, nz)
            pltpu.make_async_remote_copy(
                src_ref=source(peer), dst_ref=slots.at[gz], send_sem=group_send.at[place],
                recv_sem=group_recv.at[place], device_id=(gx, peer), device_id_type=MESH,
            ).start()
            return carry

        lax.fori_loop(1, nz, body, 0)

    spread_z(0, lambda peer: early_send.at[peer], early_slots)
    early_slots[gz] = early_send[gz]

    load.wait()

    halos = []

    def send_halo(source, target, where):
        place = len(halos)
        copy = pltpu.make_async_remote_copy(
            src_ref=source, dst_ref=target, send_sem=halo_send.at[place],
            recv_sem=halo_recv.at[place], device_id=where, device_id_type=MESH,
        )
        copy.start()
        halos.append(copy)

    def send_x(side, fields, layers):
        first_own = 2 + 14 * side + layers[0]
        first_there = 18 - 18 * side + layers[0]
        send_halo(
            P.at[fields, first_own : first_own + len(layers), 8:24, :],
            P.at[fields, first_there : first_there + len(layers), 8:24, :],
            (x_beside[side], gz),
        )

    def send_z(side, layer, fields):
        send_halo(
            Zs.at[side, layer, fields, 8:24, :],
            Zr.at[1 - side, layer, fields, 8:24, :],
            (gx, z_beside[side]),
        )

    for side in range(2):
        send_x(side, pl.ds(0, 1), (0, 1))
        send_x(side, pl.ds(3, 1), (0, 1))
        send_x(side, pl.ds(1, 2), (side,))

    for side in range(2):
        for layer in range(2):
            z = 8 + 14 * side + layer
            for f in range(FIELDS):
                for half in range(2):
                    lanes = pl.ds(128 * half, 128)
                    Zs[side, layer, f, 8:24, lanes] = P[f, 2:18, z, lanes]
    for xs in range(2):
        for zs in range(2):
            for f in range(FIELDS):
                Cs[2 * xs + zs, f : f + 1, :] = P[f, 2 + 15 * xs, 8 + 15 * zs : 9 + 15 * zs, :]

    for side in range(2):
        send_z(side, side, pl.ds(0, 4))
        send_z(side, 1 - side, pl.ds(0, 1))
    for xs in range(2):
        for zs in range(2):
            send_halo(
                Cs.at[2 * xs + zs], Cr.at[2 * (1 - xs) + 1 - zs], (x_beside[xs], z_beside[zs])
            )
    urgent = len(halos)

    yz = gz // 2
    places = nz // 2
    along = (lax.rem(gz, 2) * (nx // 2) + gx // 2) * 2 + lax.rem(gx, 2)
    line = 2 * nx

    def spread_yz(place, source, slots):
        def body(d, carry):
            peer = lax.rem(yz + d, places)
            pltpu.make_async_remote_copy(
                src_ref=source(peer), dst_ref=slots.at[yz], send_sem=group_send.at[place],
                recv_sem=group_recv.at[place], device_id=(gx, 2 * peer + lax.rem(gz, 2)),
                device_id_type=MESH,
            ).start()
            return carry

        lax.fori_loop(1, places, body, 0)

    def spread_line(place, source, slots):
        def body(d, carry):
            peer = lax.rem(along + d, line)
            where = (lax.rem(peer, nx), 2 * yz + peer // nx)
            pltpu.make_async_remote_copy(
                src_ref=source(peer), dst_ref=slots.at[along], send_sem=group_send.at[place],
                recv_sem=group_recv.at[place], device_id=where, device_id_type=MESH,
            ).start()
            return carry

        lax.fori_loop(1, line, body, 0)

    core = lax.rem(gx, 2)
    chip = (gx // 2) * nz + gz
    chips = (nx // 2) * nz

    def send_core(place, source, target):
        pltpu.make_async_remote_copy(
            src_ref=source, dst_ref=target, send_sem=group_send.at[place],
            recv_sem=group_recv.at[place], device_id=(gx + 1 - 2 * core, gz), device_id_type=MESH,
        ).start()

    def spread_chips(place, source, slots):
        def body(d, carry):
            peer = lax.rem(chip + d, chips)
            where = (2 * (peer // nz) + core, lax.rem(peer, nz))
            pltpu.make_async_remote_copy(
                src_ref=source, dst_ref=slots.at[chip], send_sem=group_send.at[place],
                recv_sem=group_recv.at[place], device_id=where, device_id_type=MESH,
            ).start()
            return carry

        lax.fori_loop(1, chips, body, 0)

    def wait_one(sems, place, part):
        pltpu.make_async_copy(part, part, sems.at[place]).wait()

    def sum_slots_of(slots):
        terms = [slots[j] for j in range(slots.shape[0])]
        while len(terms) > 1:
            terms = [a + b for a, b in zip(terms[::2], terms[1::2])] + terms[len(terms) & ~1 :]
        return terms[0]

    def wait_all(sems, place, slots):
        some = slots.at[pl.ds(0, slots.shape[0] - 1)]
        pltpu.make_async_copy(some, some, sems.at[place]).wait()

    fetch.wait()
    take_basis(basis_view, basis_rows)
    rows = basis_rows[...]
    head = rows.astype(BF16)
    basis_h[...] = head
    basis_l[...] = (rows - head.astype(F32)).astype(BF16)

    def pair():
        return basis_h[...], basis_l[...]

    inner = dot_three(pair(), pair(), TN)
    for i in range(16):
        g_send[i, :, :256] = inner[8 * i : 8 * i + 8]
        g_send[i, :, 256:] = inner[128 + 8 * i : 136 + 8 * i, 128:]
    spread_yz(1, lambda peer: g_send.at[peer], g_slots)
    g_slots[yz] = g_send[yz]
    for side in range(2):
        send_x(side, pl.ds(1, 2), (1 - side,))
        send_x(side, pl.ds(4, 1), (0, 1))
        send_z(side, side, pl.ds(4, 1))
        send_z(side, 1 - side, pl.ds(1, 4))

    profiles = [profile_rows[k] for k in range(3)]

    def first(i, wanted=range(FIELDS)):
        centre = Fields(lambda f: P[f, i + 1, 8:24, :])
        xl = Fields(lambda f: P[f, i, 8:24, :])
        xu = Fields(lambda f: P[f, i + 2, 8:24, :])
        zl = Fields(lambda f: P[f, i + 1, 7:23, :])
        zu = Fields(lambda f: P[f, i + 1, 9:25, :])
        for f, new in update(centre, xl, xu, zl, zu, profiles, wanted).items():
            H[f, i, 8:24, :] = new

    def first_inside(i, carry):
        first(i)
        return carry

    lax.fori_loop(2, 16, first_inside, 0)

    wait_all(group_recv, 0, early_slots)
    got = jnp.concatenate([early_slots[:, 0, :], early_slots[:, 1, :]], axis=0).T
    for zx in range(16):
        S[:, zx * 64 : zx * 64 + 64] = got[zx * 16 : zx * 16 + 16]
    snaps = halves(S[...])
    c_early = dot_three(snaps, pair())
    k_early = dot_three(snaps, snaps, NT)
    early = jnp.concatenate([c_early, k_early, jnp.zeros((16, 112), F32)], axis=1)
    for m in range(16):
        e_send[m] = early[m : m + 1]
    spread_yz(8, lambda peer: e_send.at[peer], e_slots)
    e_slots[yz] = e_send[yz]

    for copy in halos[:urgent]:
        copy.wait_recv()

    def fill_corners(fields):
        for f in fields:
            for xs in range(2):
                row = 7 + 17 * xs
                x = 1 + 17 * xs
                for zs in range(2):
                    corner = Cr[2 * xs + zs, f : f + 1, :]
                    Zr[zs, 1 - zs, f, row : row + 1, :] = corner
                    P[f, x, 7 + 17 * zs : 8 + 17 * zs, :] = corner
                    Zs[zs, zs, f, row : row + 1, :] = P[f, x, 8 + 15 * zs : 9 + 15 * zs, :]

    def first_edges(outside_x, outside_z, inside):
        def outside_rows(k, carry):
            first(17 * k, outside_x)
            return carry

        def inside_rows(k, carry):
            first(1 + 15 * k, inside)
            return carry

        lax.fori_loop(0, 2, outside_rows, 0)
        lax.fori_loop(0, 2, inside_rows, 0)
        for side in range(2):
            layers = [
                Zr.at[side, side], Zr.at[side, 1 - side], Zs.at[side, side], Zs.at[side, 1 - side]
            ]
            for edge in range(2):
                edge_layer(side, edge, layers[edge : edge + 3], (outside_z, inside)[edge])

    def edge_layer(side, edge, layers, wanted):
        outer, mid, inside = layers
        centre = Fields(lambda f: mid[f, 8:24, :])
        xl = Fields(lambda f: mid[f, 7:23, :])
        xu = Fields(lambda f: mid[f, 9:25, :])
        out = Fields(lambda f: outer[f, 8:24, :])
        within = Fields(lambda f: inside[f, 8:24, :])
        zl, zu = (out, within) if side == 0 else (within, out)
        z = 7 + edge if side == 0 else 24 - edge
        for f, new in update(centre, xl, xu, zl, zu, profiles, wanted).items():
            H[f, 1:17, z, :] = new

    wait_all(group_recv, 1, g_slots)
    total = sum_slots_of(g_slots)
    for r in range(8):
        g_mid[r] = total[r : r + 1]
    spread_line(3, lambda peer: g_mid.at[peer], g_mid_slots)
    g_mid_slots[along] = g_mid[along]

    fill_corners(range(4))
    first_edges((0, 3), (0,), (0, 1, 3))

    def second(wanted):
        def row(i, carry):
            centre = Fields(lambda f: H[f, i + 1, 8:24, :])
            xl = Fields(lambda f: H[f, i, 8:24, :])
            xu = Fields(lambda f: H[f, i + 2, 8:24, :])
            zl = Fields(lambda f: H[f, i + 1, 7:23, :])
            zu = Fields(lambda f: H[f, i + 1, 9:25, :])
            for f, new in update(centre, xl, xu, zl, zu, profiles, wanted).items():
                F[f, i, :, :] = new
            return carry

        lax.fori_loop(0, 16, row, 0)

    second((0,))

    for xg in range(4):
        V[16 * xg : 16 * xg + 16, :] = (H[0, 4 * xg + 1, 8:24, :] + H[0, 4 * xg + 2, 8:24, :]) + (
            H[0, 4 * xg + 3, 8:24, :] + H[0, 4 * xg + 4, 8:24, :]
        )
        V[64 + 16 * xg : 80 + 16 * xg, :] = (F[0, 4 * xg] + F[0, 4 * xg + 1]) + (
            F[0, 4 * xg + 2] + F[0, 4 * xg + 3]
        )
    to = lax.broadcasted_iota(jnp.int32, (128, 128), 0)
    of = lax.broadcasted_iota(jnp.int32, (128, 128), 1)
    wanted = ((lax.rem(of, 16) // 4) * 4 + lax.rem(of, 64) // 16) * 8 + 6 + of // 64
    place_to = (to == wanted).astype(BF16)
    sums = halves(V[...])
    gathered = dot(
        jnp.concatenate([place_to, place_to], axis=1), jnp.concatenate(sums, axis=0)
    )
    block = (
        lax.broadcasted_iota(jnp.int32, (64, 256), 0)
        == lax.broadcasted_iota(jnp.int32, (64, 256), 1) // 4
    ).astype(BF16) * BF16(1.0 / 64.0)
    coarse = dot(
        jnp.concatenate([block, block], axis=1), jnp.concatenate(halves(gathered), axis=1), NT
    )
    for i in range(32):
        late_send[i] = coarse[2 * i : 2 * i + 2]
    spread_z(2, lambda peer: late_send.at[peer], late_slots)
    late_slots[gz] = late_send[gz]

    wait_all(group_recv, 3, g_mid_slots)
    g_part[...] = sum_slots_of(g_mid_slots)
    spread_line(5, lambda peer: g_part, g_parts)
    g_parts[along] = g_part[...]

    wait_all(group_recv, 8, e_slots)
    e_mid[...] = sum_slots_of(e_slots)
    spread_line(9, lambda peer: e_mid, e_mid_slots)
    e_mid_slots[along] = e_mid[...]

    for copy in halos[urgent:]:
        copy.wait_recv()
    fill_corners((4,))
    first_edges((1, 2, 4), (1, 2, 3, 4), (2, 4))
    second((1, 2, 3, 4))
    store = pltpu.make_async_copy(F, out_fields, out_sem)
    store.start()

    wait_all(group_recv, 5, g_parts)
    for r in range(8):
        g_whole[r : r + 1, :] = g_parts[r]
    spread_yz(7, lambda peer: g_whole, g_all)
    g_all[yz] = g_whole[...]

    wait_all(group_recv, 9, e_mid_slots)
    e_part[...] = sum_slots_of(e_mid_slots)
    spread_yz(10, lambda peer: e_part, e_all)
    e_all[yz] = e_part[...]

    wait_all(group_recv, 2, late_slots)
    got = jnp.concatenate([late_slots[:, 0, :], late_slots[:, 1, :]], axis=0).T
    for zx in range(16):
        S[8:16, zx * 64 : zx * 64 + 64] = S[8:16, zx * 64 : zx * 64 + 64] + got[zx * 8 : zx * 8 + 8]
    out_snaps[...] = S[...]
    low = S[8:16, :]
    low = jnp.where(lax.broadcasted_iota(jnp.int32, low.shape, 0) >= 6, low, 0.0)
    late = halves(jnp.concatenate([jnp.zeros_like(low), low], axis=0))
    both = dot(jnp.concatenate(late, axis=0), basis_h[...])
    c_late = (both[:16] + both[16:] + dot(late[0], basis_l[...]))[14:16]
    k_late = dot_three(late, halves(S[...]), NT)[14:16]
    late = jnp.concatenate([c_late, k_late, jnp.zeros((2, 112), F32)], axis=1)
    c_send[...] = late
    send_core(4, c_send, c_other)
    wait_one(group_recv, 4, c_other)
    both = late + c_other[...]
    c_mid[...] = both
    spread_chips(6, c_mid, c_slots)
    c_slots[chip] = both

    wait_all(group_recv, 7, g_all)
    every = g_all[...].reshape(128, 384)
    cross = every[:, 128:256]
    metric = jnp.concatenate(
        [every[:, :256], jnp.concatenate([cross.T, every[:, 256:]], axis=1)], axis=0
    ) * (1.0 / rows_total)
    unit = eye(256)
    removed = 4.0 * unit - 6.0 * metric + dot_high(dot_high(metric, metric), 4.0 * unit - metric)
    wait_all(group_recv, 10, e_all)
    early = e_all[...].reshape(16, 384) * (1.0 / rows_total)
    c_early = early[:, :256]
    identity = eye(16)
    gram = early[:, 256:272] - dot_high(dot_high(c_early, removed), c_early, NT)
    left, right, pivots = eliminate(
        gram + gram_eps * identity, identity, jnp.zeros((1, 16), F32), range(14)
    )
    low_row = lax.broadcasted_iota(jnp.int32, (16, 16), 0) >= 14
    low_col = lax.broadcasted_iota(jnp.int32, (16, 16), 1) >= 14

    wait_all(group_recv, 6, c_slots)
    total = jnp.concatenate([early[:14], sum_slots_of(c_slots) * (1.0 / rows_total)], axis=0)
    c_one = total[:, :256]
    size = total[:, 256:272]
    out_coeffs[...] = 2.0 * c_one - dot_high(c_one, metric)
    gram = size - dot_high(dot_high(c_one, removed), c_one, NT) + gram_eps * identity
    across = dot_high(jnp.where(low_row & ~low_col, gram, 0.0), right, NT)
    corner = jnp.where(low_row & low_col, gram, 0.0) - dot_high(across, across, NT)
    left, right, pivots = eliminate(
        jnp.where(low_row, corner, left + across.T), right - dot_high(across, right), pivots,
        range(14, 16),
    )
    upper = lax.broadcasted_iota(jnp.int32, (16, 16), 0) <= lax.broadcasted_iota(
        jnp.int32, (16, 16), 1
    )
    out_factor[...] = jnp.where(upper, left, 0.0)
    out_inverse[...] = right
    scale = jnp.sum(jnp.where(identity > 0.0, size, 0.0), axis=0, keepdims=True)
    sound = jnp.where(pivots > least_pivot * scale, 1, 0)
    out_sound[0, 0] = jnp.min(sound)

    for copy in halos:
        copy.wait_send()
    for place, slots in (
        (0, early_slots), (1, g_slots), (2, late_slots), (3, g_mid_slots), (5, g_parts),
        (6, c_slots), (7, g_all), (8, e_slots), (9, e_mid_slots), (10, e_all),
    ):
        wait_all(group_send, place, slots)
    wait_one(group_send, 4, c_other)
    store.wait()


def front(sizes, fields, profiles, earlier, basis_view):
    nx, nz = sizes
    vmem = pl.BlockSpec(memory_space=pltpu.VMEM)
    hbm = pl.BlockSpec(memory_space=pltpu.HBM)
    smem = pl.BlockSpec(memory_space=pltpu.SMEM)
    v = pltpu.VMEM
    return pl.pallas_call(
        functools.partial(front_kernel, sizes),
        out_shape=(
            jax.ShapeDtypeStruct(fields.shape, F32),
            jax.ShapeDtypeStruct((16, 256), F32),
            jax.ShapeDtypeStruct((16, 16), F32),
            jax.ShapeDtypeStruct((16, 16), F32),
            jax.ShapeDtypeStruct((1, 1), jnp.int32),
            jax.ShapeDtypeStruct((16, 1024), F32),
        ),
        in_specs=[hbm] * 6,
        out_specs=(hbm, vmem, vmem, vmem, smem, vmem),
        scratch_shapes=[
            v((5, 20, 32, 256), F32),
            v((5, 18, 32, 256), F32),
            v((5, 16, 16, 256), F32),
            v((2, 2, 5, 32, 256), F32),
            v((2, 2, 5, 32, 256), F32),
            v((4, 8, 256), F32),
            v((4, 8, 256), F32),
            v((128, 256), F32),
            v((2048, 128), F32),
            v((1024, 256), F32),
            v((1024, 256), BF16),
            v((1024, 256), BF16),
            v((64, 256), F32),
            v((32, 2, 256), F32),
            v((32, 2, 256), F32),
            v((32, 2, 128), F32),
            v((32, 2, 128), F32),
            v((16, 1024), F32),
            v((16, 8, 384), F32),
            v((16, 8, 384), F32),
            v((8, 1, 384), F32),
            v((8, 1, 384), F32),
            v((1, 384), F32),
            v((8, 1, 384), F32),
            v((8, 384), F32),
            v((16, 8, 384), F32),
            v((16, 1, 384), F32),
            v((16, 1, 384), F32),
            v((1, 384), F32),
            v((8, 1, 384), F32),
            v((1, 384), F32),
            v((16, 1, 384), F32),
            v((2, 384), F32),
            v((2, 384), F32),
            v((2, 384), F32),
            v((64, 2, 384), F32),
            v((14, 4, 256), F32),
            v((3, 1, 256), F32),
            pltpu.SemaphoreType.DMA((4,)),
            pltpu.SemaphoreType.DMA,
            pltpu.SemaphoreType.DMA,
            pltpu.SemaphoreType.DMA,
            pltpu.SemaphoreType.DMA((22,)),
            pltpu.SemaphoreType.DMA((22,)),
            pltpu.SemaphoreType.DMA((11,)),
            pltpu.SemaphoreType.DMA((11,)),
        ],
        compiler_params=pltpu.CompilerParams(
            collective_id=0, has_side_effects=True, vmem_limit_bytes=62 * 1024 * 1024
        ),
    )(fields, *profiles, earlier, basis_view)


def direct_factor(snaps, coeffs, basis_modes):
    rows_total = 1024.0 * lax.axis_size("gx") * lax.axis_size("gz")
    rows = basis_modes.reshape(4, 32, 4, 2, 256).transpose(2, 0, 3, 1, 4).reshape(1024, 256)
    resid = snaps - jnp.dot(coeffs, rows.T, precision=HIGH)
    gram = lax.psum(jnp.dot(resid, resid.T, precision=HIGH), ("gx", "gz")) / rows_total
    identity = jnp.eye(16, dtype=F32)
    factor = jnp.linalg.cholesky(gram + gram_eps * identity)
    return factor.T, jax.scipy.linalg.solve_triangular(factor, identity, lower=True)


def on_device(fields, courant, shear_rate, gradient, earlier, basis_modes, core_matrix):
    sizes = (lax.axis_size("gx"), lax.axis_size("gz"))
    view = view_of(basis_modes)
    profiles = [p.reshape(1, -1) for p in (courant, shear_rate, gradient)]
    finished, coeffs, factor_t, inverse, sound, snaps = front(
        sizes, fields, profiles, earlier, view
    )
    factor_t, inverse = lax.cond(
        sound[0, 0] > 0,
        lambda snaps, coeffs, basis_modes, factor_t, inverse: (factor_t, inverse),
        lambda snaps, coeffs, basis_modes, factor_t, inverse: direct_factor(
            snaps, coeffs, basis_modes
        ),
        snaps, coeffs, basis_modes, factor_t, inverse,
    )
    finished, new_view, new_core = tail(
        core_matrix, coeffs, factor_t, inverse, snaps, view, finished
    )
    return (finished, basis_of(new_view), new_core)


def solution(mesh):
    return jax.shard_map(
        on_device,
        mesh=mesh,
        in_specs=(
            P(None, "gx", "gz", None),
            P(),
            P(),
            P(),
            P(None, "gx", "gz"),
            P("gx", None, "gz", None),
            P(),
        ),
        out_specs=(P(None, "gx", "gz", None), P("gx", None, "gz", None), P()),
        check_vma=False,
    )
```
